32 devices in a mesh: dp: 8 (over y, x, core), space: 4 (over z).
Axes of the slice: x: 2, y: 2, z: 4, core: 2. Of those that a mesh axis runs over, the one named last changes fastest.
Arguments:
- features: bfloat16 [8, 12288, 128], P('dp', 'space'), may hold values from -6 to 6
- neighbours: int32 [8, 27, 12288], P('dp', None, 'space'), may hold values from -1 to 12287, as said below
- weight: bfloat16 [27, 128, 128], replicated, may hold values from -0.109375 to 0.109375
- grad_out: bfloat16 [8, 12288, 128], P('dp', 'space'), may hold values from -6 to 6
Outputs:
- conv_out: bfloat16 [8, 12288, 128], P('dp', 'space')
- grad_in: bfloat16 [8, 12288, 128], P('dp', 'space')
- grad_w: float32 [27, 128, 128], replicated
The draws below stay inside these ranges and needn't reach their ends.
Inputs may be any that keep to these rules, and one draw needn't show every extreme that they name: Voxels of a scene are ordered by layer, 1024 per layer and layer z holding indices z * 1024 to (z + 1) * 1024 - 1; within a layer they are ordered by cell y * 64 + x, and every grid row y of every layer holds exactly 16 active voxels, so row y of layer z holds indices z * 1024 + y * 16 onward. An entry for offset (dz, dy, dx) of a voxel in layer z, row y points into layer z + dz, row y + dy. The map is symmetric: neighbours[26 - k, neighbours[k, i]] = i wherever neighbours[k, i] >= 0, and neighbours[13, i] = i.
All inputs are finite; a program needn't handle non-finite values.
Results may differ from the reference program's by a relative error of at most 0.0055.
Values may be sent and summed in bfloat16 or wider, within the bound.
No kernel may reach another device: no remote copies, remote signals or barrier semaphores. Data moves between devices by JAX's collectives and lax.ppermute only.
A program may use at most 64 MiB of HBM per device.

```python
import math
import jax
import jax.numpy as jnp
from jax import lax

C = 128
KVOL = 27
PSIDE = 64
NZ = 12
VOX_S = 12288
SCENES = 8
N_DP = 8


def draw_neighbours(key, part):
    plane = PSIDE * PSIDE
    per_row = PSIDE // 4
    layer_size = plane // 4

    def one_scene(scene_key):
        layer_keys = jax.random.split(scene_key, NZ)

        def pick_cells(layer_key):
            row_keys = jax.random.split(layer_key, PSIDE)

            def pick_row(row_key):
                shuffled = jax.random.permutation(row_key, PSIDE)
                return jnp.sort(shuffled[:per_row]).astype(jnp.int32)
            columns = jax.vmap(pick_row)(row_keys)
            row_base = (jnp.arange(PSIDE, dtype=jnp.int32) * PSIDE)[:, None]
            return (columns + row_base).reshape(-1).astype(jnp.int32)
        cells = jax.vmap(pick_cells)(layer_keys)
        layer_ids = jnp.arange(NZ, dtype=jnp.int32)[:, None]
        ranks = jnp.full((NZ, plane), -1, jnp.int32)
        ranks = ranks.at[jnp.broadcast_to(layer_ids, (NZ, layer_size)), cells].set(jnp.broadcast_to(jnp.arange(layer_size, dtype=jnp.int32)[None, :], (NZ, layer_size)))
        pos_z = jnp.broadcast_to(layer_ids, (NZ, layer_size))
        pos_y = cells // PSIDE
        pos_x = cells % PSIDE
        kernel_maps = []
        for step_z in (-1, 0, 1):
            for step_y in (-1, 0, 1):
                for step_x in (-1, 0, 1):
                    near_z = pos_z + step_z
                    near_y = pos_y + step_y
                    near_x = pos_x + step_x
                    inside = (near_z >= 0) & (near_z < NZ) & (near_y >= 0) & (near_y < PSIDE) & (near_x >= 0) & (near_x < PSIDE)
                    clip_z = jnp.clip(near_z, 0, NZ - 1)
                    clip_y = jnp.clip(near_y, 0, PSIDE - 1)
                    clip_x = jnp.clip(near_x, 0, PSIDE - 1)
                    found = ranks[clip_z, clip_y * PSIDE + clip_x]
                    target = jnp.where(inside & (found >= 0), clip_z * layer_size + found, -1)
                    kernel_maps.append(target.reshape(-1))
        return jnp.stack(kernel_maps).astype(jnp.int32)
    scene_keys = jax.random.split(key, SCENES)
    return jax.vmap(one_scene)(scene_keys)


def levels(stream_key, dims, shards, least, high):
    factor_of, own = 1.0, jax.random.fold_in(stream_key, 6)
    for position, parts in shards:
        steps = jnp.exp(jax.random.uniform(jax.random.fold_in(own, position), (parts,), jnp.float32, least / len(shards), high / len(shards)))
        factor_of = factor_of * jnp.repeat(steps, dims[position] // parts).reshape([-1 if axis == position else 1 for axis in range(len(dims))])
    return factor_of


def gaussian(rng, extent, spread, bound, pieces=(), kind=jnp.bfloat16):
    entries = jax.random.normal(rng, extent, jnp.float32) * spread
    if len(pieces) > 0:
        entries = levels(rng, extent, pieces, -0.22, 0.18) * entries
    return jnp.clip(entries, min=-bound, max=bound).astype(kind)


def setup_inputs(seed: int = 0) -> dict:
    seeds = jax.random.split(jax.random.key(seed), 5)
    return {
        "features": gaussian(seeds[0], (SCENES, VOX_S, C), 1.0, 6.0, ((0, 8), (1, 4))),
        "neighbours": draw_neighbours(jax.random.fold_in(seeds[4], 71), 0),
        "weight": gaussian(seeds[2], (KVOL, C, C), (KVOL * C) ** -0.5, 0.109375),
        "grad_out": gaussian(seeds[3], (SCENES, VOX_S, C), 1.0, 6.0, ((0, 8), (1, 4))),
    }


def conv_scene(feats, neigh_map, weight, grads):
    voxels = feats.shape[0]
    channels = feats.shape[1]
    zero_row = jnp.zeros((1, channels), feats.dtype)
    extended = jnp.concatenate([feats, zero_row], 0)
    grad_ext = jnp.concatenate([grads, zero_row], 0)
    row_index = jnp.where(neigh_map >= 0, neigh_map, voxels).astype(jnp.int32)
    zero_acc = jnp.zeros((voxels, channels), jnp.float32)

    def forward_step(total, pair_item):
        index_row, kernel = pair_item
        picked = jnp.take(extended, index_row, axis=0)
        return (total + jnp.dot(picked, kernel, preferred_element_type=jnp.float32), None)
    result, _ = lax.scan(forward_step, zero_acc, (row_index, weight))

    def backward_step(total, pair_item):
        index_row, kernel = pair_item
        picked = jnp.take(grad_ext, index_row, axis=0)
        return (total + lax.dot_general(picked, kernel, (((1,), (1,)), ((), ())), preferred_element_type=jnp.float32), None)
    grad_x, _ = lax.scan(backward_step, zero_acc, (row_index[::-1], weight))

    def weight_term(index_row):
        picked = jnp.take(extended, index_row, axis=0)
        return lax.dot_general(picked, grads, (((0,), (0,)), ((), ())), preferred_element_type=jnp.float32)
    weight_terms = lax.map(weight_term, row_index)
    return (result.astype(jnp.bfloat16), grad_x.astype(jnp.bfloat16), weight_terms)

def reference(features, neighbours, weight, grad_out):

    def per_scene(scene_item):
        return conv_scene(scene_item[0], scene_item[1], weight, scene_item[2])
    conv_out, grad_in, weight_terms = lax.map(per_scene, (features, neighbours, grad_out))
    norm_factor = 1.0 / math.sqrt(N_DP * VOX_S)
    grad_w = lax.optimization_barrier(jnp.sum(weight_terms, axis=0)) * norm_factor
    return (conv_out, grad_in, grad_w)
```

```python
import functools
import math

import jax
import jax.numpy as jnp
from jax import lax
from jax.experimental import pallas as pl
from jax.experimental.pallas import tpu as pltpu
from jax.sharding import PartitionSpec as P

PSIDE = 64
ROW = PSIDE // 4
LAYER = PSIDE * ROW
T = 128
CHUNK_W = 512
CHUNK_C = 256
VMEM_LIMIT = 56 * 1024 * 1024


def offset_of(k):
    return k // 9 - 1, (k // 3) % 3 - 1, k % 3 - 1


def place_in_window(neighbours, k):
    dy = offset_of(k)[1]
    return jnp.where(neighbours >= 0, (neighbours - ROW * dy) & (T - 1), -1)


def grad_w_kernel(voxels, scale, f_ref, g_ref, low_ref, nb_ref, out_ref, xt, fpad, gpad, rel, gf, gg, acc):
    channels = f_ref.shape[1]
    edge = jnp.zeros((ROW, channels), jnp.bfloat16)
    for pad, ref in ((fpad, f_ref), (gpad, g_ref)):
        pad[0:ROW, :] = edge
        pad[ROW + voxels : 2 * ROW + voxels, :] = edge
        pad[ROW : ROW + voxels, :] = ref[...]
    for t in range(LAYER // T):
        both = low_ref[t * T : (t + 1) * T, :]
        xt[:, t * T : (t + 1) * T] = both.T
    for t in range(voxels // T):
        cols = slice(LAYER + t * T, LAYER + (t + 1) * T)
        xt[0:channels, cols] = f_ref[t * T : (t + 1) * T, :].T
        xt[channels : 2 * channels, cols] = g_ref[t * T : (t + 1) * T, :].T
    none = jnp.full((1, ROW), -1, jnp.int32)
    for k in range(13):
        dy = offset_of(k)[1]
        row = nb_ref[k : k + 1, :]
        row = jnp.where(row >= 0, row & (T - 1), -1)
        if dy == -1:
            row = jnp.concatenate([row[:, ROW:], none], axis=1)
        elif dy == 1:
            row = jnp.concatenate([none, row[:, : voxels - ROW]], axis=1)
        rel[k : k + 1, :] = row
    acc[...] = jnp.zeros_like(acc)
    spot = lax.broadcasted_iota(jnp.int32, (T, T), 0)

    def step(o, dz, ks):
        base = pl.multiple_of(o * CHUNK_W, CHUNK_W)
        for h in range(CHUNK_W // T):
            cols = pl.ds(pl.multiple_of(base + h * T, T), T)
            window = xt[:, pl.ds(pl.multiple_of(base + (dz + 1) * LAYER + h * T, T), T)]
            for p in range(0, len(ks), 2):
                pair = ks[p : p + 2]
                hot = jnp.concatenate(
                    [(rel[k : k + 1, cols] == spot).astype(jnp.bfloat16) for k in pair], axis=1
                )
                picked = jnp.dot(window, hot, preferred_element_type=jnp.float32)
                picked = picked.astype(jnp.bfloat16)
                for q, k in enumerate(pair):
                    at = (p + q) * T
                    part = picked[:, q * T : (q + 1) * T]
                    gf[at : at + T, h * T : (h + 1) * T] = part[:channels]
                    gg[at : at + T, h * T : (h + 1) * T] = part[channels:]
        for dy in (-1, 0, 1):
            group = [k for k in ks if offset_of(k)[1] == dy]
            if not group:
                continue
            lo = ks.index(group[0]) * T
            hi = lo + len(group) * T
            rows = pl.ds(pl.multiple_of(base + ROW - ROW * dy, ROW), CHUNK_W)
            acc[pl.ds(group[0] * T, len(group) * T), :] += jnp.dot(
                gf[lo:hi, :], gpad[rows, :], preferred_element_type=jnp.float32
            )
            acc[pl.ds((14 + group[0]) * T, len(group) * T), :] += jnp.dot(
                gg[lo:hi, :], fpad[rows, :], preferred_element_type=jnp.float32
            )
        if dz == 0:
            own = xt[0:channels, pl.ds(pl.multiple_of(base + LAYER, T), CHUNK_W)]
            rows = pl.ds(pl.multiple_of(base + ROW, ROW), CHUNK_W)
            acc[13 * T : 14 * T, :] += jnp.dot(
                own, gpad[rows, :], preferred_element_type=jnp.float32
            )

    @pl.loop(0, voxels // CHUNK_W)
    def _(o):
        step(o, 0, [9, 10, 11, 12])

    @pl.loop(0, voxels // CHUNK_W)
    def _(o):
        step(o, -1, list(range(9)))

    for k in range(14):
        out_ref[k] = (acc[k * T : (k + 1) * T, :] * scale).astype(out_ref.dtype)
    for k in range(13):
        out_ref[26 - k] = (acc[(14 + k) * T : (15 + k) * T, :].T * scale).astype(out_ref.dtype)


def grad_w_partial(feats, grads, low, neigh, scale):
    voxels, channels = feats.shape
    return pl.pallas_call(
        functools.partial(grad_w_kernel, voxels, scale),
        out_shape=jax.ShapeDtypeStruct((27, channels, channels), jnp.bfloat16),
        in_specs=[pl.BlockSpec(memory_space=pltpu.VMEM)] * 4,
        out_specs=pl.BlockSpec(memory_space=pltpu.VMEM),
        scratch_shapes=[
            pltpu.VMEM((2 * channels, LAYER + voxels), jnp.bfloat16),
            pltpu.VMEM((voxels + 2 * ROW, channels), jnp.bfloat16),
            pltpu.VMEM((voxels + 2 * ROW, channels), jnp.bfloat16),
            pltpu.VMEM((16, voxels), jnp.int32),
            pltpu.VMEM((9 * T, CHUNK_W), jnp.bfloat16),
            pltpu.VMEM((9 * T, CHUNK_W), jnp.bfloat16),
            pltpu.VMEM((27 * T, channels), jnp.float32),
        ],
        compiler_params=pltpu.CompilerParams(vmem_limit_bytes=VMEM_LIMIT),
        cost_estimate=pl.CostEstimate(flops=10**10, bytes_accessed=4 * 10**6, transcendentals=0),
        name="weight_gradient",
    )(feats, grads, low, neigh)


def conv_kernel(voxels, f_ref, g_ref, low_ref, high_ref, nb_ref, w_ref, conv_ref, gin_ref, xe, wt, rel, relt, gf, gg):
    channels = f_ref.shape[1]
    edge = jnp.zeros((ROW, 2 * channels), jnp.bfloat16)
    xe[0:ROW, :] = edge
    xe[ROW : ROW + LAYER, :] = low_ref[...]
    xe[ROW + LAYER : ROW + LAYER + voxels, 0:channels] = f_ref[...]
    xe[ROW + LAYER : ROW + LAYER + voxels, channels:] = g_ref[...]
    xe[ROW + LAYER + voxels : ROW + 2 * LAYER + voxels, :] = high_ref[...]
    xe[ROW + 2 * LAYER + voxels :, :] = edge
    for k in range(27):
        wt[k * T : (k + 1) * T, :] = w_ref[(26 - k) * T : (27 - k) * T, :].T
    for k in range(27):
        rel[k : k + 1, :] = place_in_window(nb_ref[k : k + 1, :], k)
    for k in range(27, 32):
        rel[k : k + 1, :] = jnp.full((1, voxels), -1, jnp.int32)
    for t in range(voxels // T):
        relt[t * T : (t + 1) * T, :] = rel[:, t * T : (t + 1) * T].T
    spot = lax.broadcasted_iota(jnp.int32, (T, T), 1)

    @pl.loop(0, voxels // CHUNK_C)
    def _(o):
        base = pl.multiple_of(o * CHUNK_C, CHUNK_C)
        for h in range(CHUNK_C // T):
            rows = slice(h * T, (h + 1) * T)
            mine = relt[pl.ds(pl.multiple_of(base + h * T, T), T), :]
            for dz in (-1, 0, 1):
                for dy in (-1, 0, 1):
                    start = base + (h * T + ROW + ROW * dy + LAYER * (dz + 1))
                    window = xe[pl.ds(pl.multiple_of(start, ROW), T), :]
                    first = 9 * (dz + 1) + 3 * (dy + 1)
                    ks = [k for k in range(first, first + 3) if k != 13]
                    hot = jnp.concatenate(
                        [(mine[:, k : k + 1] == spot).astype(jnp.bfloat16) for k in ks], axis=0
                    )
                    picked = jnp.dot(hot, window, preferred_element_type=jnp.float32)
                    picked = picked.astype(jnp.bfloat16)
                    for q, k in enumerate(ks):
                        part = picked[q * T : (q + 1) * T]
                        gf[rows, k * T : (k + 1) * T] = part[:, :channels]
                        gg[rows, k * T : (k + 1) * T] = part[:, channels:]
                    if first <= 13 < first + 3:
                        gf[rows, 13 * T : 14 * T] = window[:, :channels]
                        gg[rows, 13 * T : 14 * T] = window[:, channels:]
        out_rows = pl.ds(base, CHUNK_C)
        conv_ref[out_rows, :] = jnp.dot(
            gf[...], w_ref[...], preferred_element_type=jnp.float32
        ).astype(jnp.bfloat16)
        gin_ref[out_rows, :] = jnp.dot(
            gg[...], wt[...], preferred_element_type=jnp.float32
        ).astype(jnp.bfloat16)


def conv_both(feats, grads, low, high, neigh, weight):
    voxels, channels = feats.shape
    out = jax.ShapeDtypeStruct((voxels, channels), jnp.bfloat16)
    return pl.pallas_call(
        functools.partial(conv_kernel, voxels),
        out_shape=(out, out),
        in_specs=[pl.BlockSpec(memory_space=pltpu.VMEM)] * 6,
        out_specs=(pl.BlockSpec(memory_space=pltpu.VMEM),) * 2,
        scratch_shapes=[
            pltpu.VMEM((2 * ROW + 2 * LAYER + voxels, 2 * channels), jnp.bfloat16),
            pltpu.VMEM((27 * T, channels), jnp.bfloat16),
            pltpu.VMEM((32, voxels), jnp.int32),
            pltpu.VMEM((voxels, 32), jnp.int32),
            pltpu.VMEM((CHUNK_C, 27 * T), jnp.bfloat16),
            pltpu.VMEM((CHUNK_C, 27 * T), jnp.bfloat16),
        ],
        compiler_params=pltpu.CompilerParams(vmem_limit_bytes=VMEM_LIMIT),
        cost_estimate=pl.CostEstimate(flops=2 * 10**10, bytes_accessed=6 * 10**6, transcendentals=0),
        name="conv_and_input_gradient",
    )(feats, grads, low, high, neigh, weight.reshape(27 * channels, channels))


def local(features, neighbours, weight, grad_out):
    feats, grads, neigh = features[0], grad_out[0], neighbours[0]
    voxels, channels = feats.shape
    space = lax.axis_size("space")
    devices = lax.axis_size("dp") * space
    up = [(i, i + 1) for i in range(space - 1)]
    down = [(i + 1, i) for i in range(space - 1)]
    last = jnp.concatenate([feats[voxels - LAYER :], grads[voxels - LAYER :]], axis=1)
    first = jnp.concatenate([feats[:LAYER], grads[:LAYER]], axis=1)
    low = lax.ppermute(last, "space", up)
    high = lax.ppermute(first, "space", down)

    scale = 1.0 / math.sqrt(devices * voxels)
    partial = grad_w_partial(feats, grads, low, neigh, scale)
    pieces = partial.reshape(devices, -1, channels)
    pieces = lax.all_to_all(pieces, ("dp", "space"), 0, 0, tiled=True)
    shard = jnp.sum(pieces.astype(jnp.float32), axis=0).astype(jnp.bfloat16)
    whole = lax.all_gather(shard, ("dp", "space"), axis=0, tiled=True)
    grad_w = whole.astype(jnp.float32).reshape(27, channels, channels)

    conv_out, grad_in = conv_both(feats, grads, low, high, neigh, weight)
    return conv_out[None], grad_in[None], grad_w


def solution(mesh):
    in_specs = (P("dp", "space", None), P("dp", None, "space"), P(), P("dp", "space", None))
    out_specs = (P("dp", "space", None), P("dp", "space", None), P())
    return jax.shard_map(local, mesh=mesh, in_specs=in_specs, out_specs=out_specs, check_vma=False)
```

```python
import functools
import math

import jax
import jax.numpy as jnp
from jax import lax
from jax.experimental import pallas as pl
from jax.experimental.pallas import tpu as pltpu
from jax.sharding import PartitionSpec as P

PSIDE = 64
ROW = PSIDE // 4
LAYER = PSIDE * ROW
T = 128
CHUNK_W = 512
CHUNK_C = 256
VMEM_LIMIT = 28 * 1024 * 1024
VMEM = pl.BlockSpec(memory_space=pltpu.VMEM)


def offset_of(k):
    return k // 9 - 1, (k // 3) % 3 - 1, k % 3 - 1


def row_in_scene_window(neighbours, shift):
    return jnp.where(neighbours >= 0, (neighbours - shift) & (T - 1), -1)


def one_hot(hit):
    return jnp.where(hit, jnp.ones((), jnp.bfloat16), jnp.zeros((), jnp.bfloat16))


def fill_padded(pad, ref, voxels):
    edge = jnp.zeros((ROW, ref.shape[1]), jnp.bfloat16)
    pad[0:ROW, :] = edge
    pad[ROW + voxels : 2 * ROW + voxels, :] = edge
    pad[ROW : ROW + voxels, :] = ref[0:voxels, :]


def fill_places(rel, nb_ref, ks, voxels):
    none = jnp.full((1, ROW), -1, jnp.int32)
    for k in ks:
        dy = offset_of(k)[1]
        row = row_in_scene_window(nb_ref[k, :, 0:voxels], 0)
        if dy == -1:
            row = jnp.concatenate([row[:, ROW:], none], axis=1)
        elif dy == 1:
            row = jnp.concatenate([none, row[:, : voxels - ROW]], axis=1)
        rel[k : k + 1, :] = row


def add_weight_terms(o, ks, xt, source, rel, fpad, gpad, gf, gg, acc):
    channels = fpad.shape[1]
    base = pl.multiple_of(o * CHUNK_W, CHUNK_W)
    spot = lax.broadcasted_iota(jnp.int32, (T, T), 0)
    for h in range(CHUNK_W // T):
        cols = pl.ds(pl.multiple_of(base + h * T, T), T)
        window = xt[:, pl.ds(pl.multiple_of(base + source + h * T, T), T)]
        for p in range(0, len(ks), 2):
            pair = ks[p : p + 2]
            hot = jnp.concatenate(
                [one_hot(rel[k : k + 1, cols] == spot) for k in pair], axis=1
            )
            picked = jnp.dot(window, hot, preferred_element_type=jnp.float32)
            picked = picked.astype(jnp.bfloat16)
            for q in range(len(pair)):
                at = (p + q) * T
                part = picked[:, q * T : (q + 1) * T]
                gf[at : at + T, h * T : (h + 1) * T] = part[:channels]
                gg[at : at + T, h * T : (h + 1) * T] = part[channels:]
    for dy in (-1, 0, 1):
        group = [k for k in ks if offset_of(k)[1] == dy]
        if not group:
            continue
        lo = ks.index(group[0]) * T
        hi = lo + len(group) * T
        rows = pl.ds(pl.multiple_of(base + ROW - ROW * dy, ROW), CHUNK_W)
        acc[group[0] * T : (group[-1] + 1) * T, :] += jnp.dot(
            gf[lo:hi, :], gpad[rows, :], preferred_element_type=jnp.float32
        )
        acc[(14 + group[0]) * T : (15 + group[-1]) * T, :] += jnp.dot(
            gg[lo:hi, :], fpad[rows, :], preferred_element_type=jnp.float32
        )


def weight_inner_kernel(voxels, f_ref, g_ref, nb_ref, acc, xt, fpad, gpad, rel, gf, gg):
    channels = f_ref.shape[1]
    fill_padded(fpad, f_ref, voxels)
    fill_padded(gpad, g_ref, voxels)
    for t in range(voxels // T):
        cols = slice(t * T, (t + 1) * T)
        xt[0:channels, cols] = f_ref[t * T : (t + 1) * T, :].T
        xt[channels : 2 * channels, cols] = g_ref[t * T : (t + 1) * T, :].T
    fill_places(rel, nb_ref, range(13), voxels)
    acc[...] = jnp.zeros_like(acc)

    @pl.loop(0, voxels // CHUNK_W)
    def _(o):
        add_weight_terms(o, [9, 10, 11, 12], xt, 0, rel, fpad, gpad, gf, gg, acc)
        base = pl.multiple_of(o * CHUNK_W, CHUNK_W)
        own = xt[0:channels, pl.ds(base, CHUNK_W)]
        rows = pl.ds(pl.multiple_of(base + ROW, ROW), CHUNK_W)
        acc[13 * T : 14 * T, :] += jnp.dot(
            own, gpad[rows, :], preferred_element_type=jnp.float32
        )

    @pl.loop(LAYER // CHUNK_W, voxels // CHUNK_W)
    def _(o):
        add_weight_terms(o, list(range(9)), xt, -LAYER, rel, fpad, gpad, gf, gg, acc)


def weight_halo_kernel(scale, f_ref, g_ref, low_ref, nb_ref, in_ref, out_ref, xt, fpad, gpad, rel, gf, gg, acc):
    voxels = LAYER + ROW
    fill_padded(fpad, f_ref, voxels)
    fill_padded(gpad, g_ref, voxels)
    for t in range(LAYER // T):
        xt[:, t * T : (t + 1) * T] = low_ref[t * T : (t + 1) * T, :].T
    fill_places(rel, nb_ref, range(9), LAYER + T)
    acc[...] = in_ref[...]

    @pl.loop(0, LAYER // CHUNK_W)
    def _(o):
        add_weight_terms(o, list(range(9)), xt, 0, rel, fpad, gpad, gf, gg, acc)

    for k in range(14):
        out_ref[k * T : (k + 1) * T, :] = (acc[k * T : (k + 1) * T, :] * scale).astype(out_ref.dtype)
    for k in range(13):
        out_ref[(26 - k) * T : (27 - k) * T, :] = (
            acc[(14 + k) * T : (15 + k) * T, :].T * scale
        ).astype(out_ref.dtype)
    if out_ref.shape[0] > 27 * T:
        out_ref[27 * T :, :] = jnp.zeros((out_ref.shape[0] - 27 * T, out_ref.shape[1]), out_ref.dtype)


def weight_scratch(voxels, columns, channels):
    return [
        pltpu.VMEM((2 * channels, columns), jnp.bfloat16),
        pltpu.VMEM((voxels + 2 * ROW, channels), jnp.bfloat16),
        pltpu.VMEM((voxels + 2 * ROW, channels), jnp.bfloat16),
    ]


def grad_w_inner(feats, grads, neigh):
    voxels, channels = feats.shape
    return pl.pallas_call(
        functools.partial(weight_inner_kernel, voxels),
        out_shape=jax.ShapeDtypeStruct((27 * T, channels), jnp.float32),
        in_specs=[VMEM] * 3,
        out_specs=VMEM,
        scratch_shapes=weight_scratch(voxels, voxels, channels)
        + [
            pltpu.VMEM((16, voxels), jnp.int32),
            pltpu.VMEM((9 * T, CHUNK_W), jnp.bfloat16),
            pltpu.VMEM((9 * T, CHUNK_W), jnp.bfloat16),
        ],
        compiler_params=pltpu.CompilerParams(vmem_limit_bytes=VMEM_LIMIT),
        cost_estimate=pl.CostEstimate(flops=8 * 10**9, bytes_accessed=4 * 10**6, transcendentals=0),
        name="weight_gradient_inner",
    )(feats, grads, neigh)


def grad_w_halo(feats, grads, low, neigh, partial, scale, rows):
    voxels, channels = feats.shape
    return pl.pallas_call(
        functools.partial(weight_halo_kernel, scale),
        out_shape=jax.ShapeDtypeStruct((rows, channels), jnp.bfloat16),
        in_specs=[VMEM] * 5,
        out_specs=VMEM,
        scratch_shapes=weight_scratch(LAYER + ROW, LAYER, channels)
        + [
            pltpu.VMEM((16, LAYER + T), jnp.int32),
            pltpu.VMEM((9 * T, CHUNK_W), jnp.bfloat16),
            pltpu.VMEM((9 * T, CHUNK_W), jnp.bfloat16),
            pltpu.VMEM((27 * T, channels), jnp.float32),
        ],
        compiler_params=pltpu.CompilerParams(vmem_limit_bytes=VMEM_LIMIT),
        cost_estimate=pl.CostEstimate(flops=3 * 10**9, bytes_accessed=4 * 10**6, transcendentals=0),
        name="weight_gradient_halo",
    )(feats, grads, low, neigh, partial)


def conv_kernel(voxels, first_chunk, f_ref, g_ref, low_ref, high_ref, nb_ref, w_ref, *rest):
    conv_ref, gin_ref, xe, wt, rel, relt, gf, gg = rest[-8:]
    channels = f_ref.shape[1]
    step = pl.program_id(0)

    @pl.when(step == 0)
    def _():
        edge = jnp.zeros((ROW, 2 * channels), jnp.bfloat16)
        xe[0:ROW, :] = edge
        xe[ROW : ROW + LAYER, :] = low_ref[...]
        xe[ROW + LAYER : ROW + LAYER + voxels, 0:channels] = f_ref[...]
        xe[ROW + LAYER : ROW + LAYER + voxels, channels:] = g_ref[...]
        xe[ROW + LAYER + voxels : ROW + 2 * LAYER + voxels, :] = high_ref[...]
        xe[ROW + 2 * LAYER + voxels :, :] = edge
        for k in range(27):
            wt[k * T : (k + 1) * T, :] = w_ref[(26 - k) * T : (27 - k) * T, :].T
        for k in range(27):
            rel[k : k + 1, :] = row_in_scene_window(nb_ref[k], ROW * offset_of(k)[1])
        rel[27:, :] = jnp.full((5, voxels), -1, jnp.int32)
        for t in range(voxels // T):
            relt[t * T : (t + 1) * T, :] = rel[:, t * T : (t + 1) * T].T.astype(jnp.bfloat16)

    spot = lax.broadcasted_iota(jnp.int32, (T, T), 1).astype(jnp.bfloat16)
    base = pl.multiple_of((step + first_chunk) * CHUNK_C, CHUNK_C)
    for h in range(CHUNK_C // T):
        rows = slice(h * T, (h + 1) * T)
        mine = relt[pl.ds(pl.multiple_of(base + h * T, T), T), :]
        for dz in (-1, 0, 1):
            for dy in (-1, 0, 1):
                start = base + (h * T + ROW + ROW * dy + LAYER * (dz + 1))
                window = xe[pl.ds(pl.multiple_of(start, ROW), T), :]
                first = 9 * (dz + 1) + 3 * (dy + 1)
                ks = [k for k in range(first, first + 3) if k != 13]
                hot = jnp.concatenate([one_hot(mine[:, k : k + 1] == spot) for k in ks], axis=0)
                picked = jnp.dot(hot, window, preferred_element_type=jnp.float32)
                picked = picked.astype(jnp.bfloat16)
                for q, k in enumerate(ks):
                    part = picked[q * T : (q + 1) * T]
                    gf[rows, k * T : (k + 1) * T] = part[:, :channels]
                    gg[rows, k * T : (k + 1) * T] = part[:, channels:]
                if first <= 13 < first + 3:
                    gf[rows, 13 * T : 14 * T] = window[:, :channels]
                    gg[rows, 13 * T : 14 * T] = window[:, channels:]
    conv_ref[...] = jnp.dot(gf[...], w_ref[...], preferred_element_type=jnp.float32).astype(jnp.bfloat16)
    gin_ref[...] = jnp.dot(gg[...], wt[...], preferred_element_type=jnp.float32).astype(jnp.bfloat16)


def conv_both(feats, grads, low, high, neigh, weight, chunks, earlier, name):
    voxels, channels = feats.shape
    out = jax.ShapeDtypeStruct((voxels, channels), jnp.bfloat16)
    first_chunk, end_chunk = chunks
    block = pl.BlockSpec((CHUNK_C, channels), lambda i: (i + first_chunk, 0))
    return pl.pallas_call(
        functools.partial(conv_kernel, voxels, first_chunk),
        grid=(end_chunk - first_chunk,),
        out_shape=(out, out),
        in_specs=[VMEM] * 6 + [pl.BlockSpec(memory_space=pl.ANY)] * len(earlier),
        out_specs=(block, block),
        input_output_aliases={6 + i: i for i in range(len(earlier))},
        scratch_shapes=[
            pltpu.VMEM((2 * ROW + 2 * LAYER + voxels, 2 * channels), jnp.bfloat16),
            pltpu.VMEM((27 * T, channels), jnp.bfloat16),
            pltpu.VMEM((32, voxels), jnp.int32),
            pltpu.VMEM((voxels, 32), jnp.bfloat16),
            pltpu.VMEM((CHUNK_C, 27 * T), jnp.bfloat16),
            pltpu.VMEM((CHUNK_C, 27 * T), jnp.bfloat16),
        ],
        compiler_params=pltpu.CompilerParams(vmem_limit_bytes=VMEM_LIMIT),
        cost_estimate=pl.CostEstimate(flops=10**10, bytes_accessed=6 * 10**6, transcendentals=0),
        name=name,
    )(feats, grads, low, high, neigh, weight, *earlier)


def local(features, neighbours, weight, grad_out):
    feats, grads = features[0], grad_out[0]
    neigh = jnp.swapaxes(neighbours, 0, 1)
    voxels, channels = feats.shape
    space = lax.axis_size("space")
    devices = lax.axis_size("dp") * space
    everyone = ("dp", "space")
    up = [(i, i + 1) for i in range(space - 1)]
    down = [(i + 1, i) for i in range(space - 1)]
    last = jnp.concatenate([feats[voxels - LAYER :], grads[voxels - LAYER :]], axis=1)
    first = jnp.concatenate([feats[:LAYER], grads[:LAYER]], axis=1)
    low = lax.ppermute(last, "space", up)
    high = lax.ppermute(first, "space", down)

    scale = 1.0 / math.sqrt(devices * voxels)
    share = -(-27 * channels // (16 * devices)) * 16
    inner = grad_w_inner(feats, grads, neigh)
    partial = grad_w_halo(feats, grads, low, neigh, inner, scale, share * devices)
    pieces = lax.all_to_all(partial.reshape(devices, share, channels), everyone, 0, 0, tiled=True)

    flat_weight = weight.reshape(27 * channels, channels)
    chunks = voxels // CHUNK_C
    half = chunks // 2
    begun = conv_both(feats, grads, low, high, neigh, flat_weight, (0, half), (), "conv_first_half")

    pieces, begun = lax.optimization_barrier((pieces, begun))
    shard = jnp.sum(pieces.astype(jnp.float32), axis=0).astype(jnp.bfloat16)
    spread = jnp.broadcast_to(shard[None], (devices, share, channels))
    whole = lax.all_to_all(spread, everyone, 0, 0, tiled=True)
    conv_out, grad_in = conv_both(
        feats, grads, low, high, neigh, flat_weight, (half, chunks), begun, "conv_second_half"
    )
    grad_w = whole.reshape(devices * share, channels)[: 27 * channels].astype(jnp.float32)
    return conv_out[None], grad_in[None], grad_w.reshape(27, channels, channels)


def solution(mesh):
    in_specs = (P("dp", "space", None), P("dp", None, "space"), P(), P("dp", "space", None))
    out_specs = (P("dp", "space", None), P("dp", "space", None), P())
    return jax.shard_map(local, mesh=mesh, in_specs=in_specs, out_specs=out_specs, check_vma=False)
```

```python
import functools
import math

import jax
import jax.numpy as jnp
from jax import lax
from jax.experimental import pallas as pl
from jax.experimental.pallas import tpu as pltpu
from jax.sharding import PartitionSpec as P

PSIDE = 64
ROW = PSIDE // 4
LAYER = PSIDE * ROW
T = 128
CHUNK_W = 512
CHUNK_C = 256
VMEM_LIMIT = 28 * 1024 * 1024
VMEM = pl.BlockSpec(memory_space=pltpu.VMEM)


def offset_of(k):
    return k // 9 - 1, (k // 3) % 3 - 1, k % 3 - 1


def row_in_scene_window(neighbours, shift):
    return jnp.where(neighbours >= 0, (neighbours - shift) & (T - 1), -1)


def one_hot(hit):
    return jnp.where(hit, jnp.ones((), jnp.bfloat16), jnp.zeros((), jnp.bfloat16))


def fill_padded(pad, ref, voxels):
    edge = jnp.zeros((ROW, ref.shape[1]), jnp.bfloat16)
    pad[0:ROW, :] = edge
    pad[ROW + voxels : 2 * ROW + voxels, :] = edge
    pad[ROW : ROW + voxels, :] = ref[0:voxels, :]


def fill_places(rel, nb_ref, ks, voxels):
    none = jnp.full((1, ROW), -1, jnp.int32)
    for k in ks:
        dy = offset_of(k)[1]
        row = row_in_scene_window(nb_ref[k, :, 0:voxels], 0)
        if dy == -1:
            row = jnp.concatenate([row[:, ROW:], none], axis=1)
        elif dy == 1:
            row = jnp.concatenate([none, row[:, : voxels - ROW]], axis=1)
        rel[k : k + 1, :] = row


def add_weight_terms(o, ks, xt, source, rel, fpad, gpad, gf, gg, acc):
    channels = fpad.shape[1]
    base = pl.multiple_of(o * CHUNK_W, CHUNK_W)
    spot = lax.broadcasted_iota(jnp.int32, (T, T), 0)
    for h in range(CHUNK_W // T):
        cols = pl.ds(pl.multiple_of(base + h * T, T), T)
        window = xt[:, pl.ds(pl.multiple_of(base + source + h * T, T), T)]
        for p in range(0, len(ks), 2):
            pair = ks[p : p + 2]
            hot = jnp.concatenate(
                [one_hot(rel[k : k + 1, cols] == spot) for k in pair], axis=1
            )
            picked = jnp.dot(window, hot, preferred_element_type=jnp.float32)
            picked = picked.astype(jnp.bfloat16)
            for q in range(len(pair)):
                at = (p + q) * T
                part = picked[:, q * T : (q + 1) * T]
                gf[at : at + T, h * T : (h + 1) * T] = part[:channels]
                gg[at : at + T, h * T : (h + 1) * T] = part[channels:]
    for dy in (-1, 0, 1):
        group = [k for k in ks if offset_of(k)[1] == dy]
        if not group:
            continue
        lo = ks.index(group[0]) * T
        hi = lo + len(group) * T
        rows = pl.ds(pl.multiple_of(base + ROW - ROW * dy, ROW), CHUNK_W)
        acc[group[0] * T : (group[-1] + 1) * T, :] += jnp.dot(
            gf[lo:hi, :], gpad[rows, :], preferred_element_type=jnp.float32
        )
        acc[(14 + group[0]) * T : (15 + group[-1]) * T, :] += jnp.dot(
            gg[lo:hi, :], fpad[rows, :], preferred_element_type=jnp.float32
        )


def weight_inner_kernel(voxels, f_ref, g_ref, nb_ref, acc, xt, fpad, gpad, rel, gf, gg):
    channels = f_ref.shape[1]
    fill_padded(fpad, f_ref, voxels)
    fill_padded(gpad, g_ref, voxels)
    for t in range(voxels // T):
        cols = slice(t * T, (t + 1) * T)
        xt[0:channels, cols] = f_ref[t * T : (t + 1) * T, :].T
        xt[channels : 2 * channels, cols] = g_ref[t * T : (t + 1) * T, :].T
    fill_places(rel, nb_ref, range(13), voxels)
    acc[...] = jnp.zeros_like(acc)

    @pl.loop(0, voxels // CHUNK_W)
    def _(o):
        add_weight_terms(o, [9, 10, 11, 12], xt, 0, rel, fpad, gpad, gf, gg, acc)
        base = pl.multiple_of(o * CHUNK_W, CHUNK_W)
        own = xt[0:channels, pl.ds(base, CHUNK_W)]
        rows = pl.ds(pl.multiple_of(base + ROW, ROW), CHUNK_W)
        acc[13 * T : 14 * T, :] += jnp.dot(
            own, gpad[rows, :], preferred_element_type=jnp.float32
        )

    @pl.loop(LAYER // CHUNK_W, voxels // CHUNK_W)
    def _(o):
        add_weight_terms(o, list(range(9)), xt, -LAYER, rel, fpad, gpad, gf, gg, acc)


def weight_halo_kernel(scale, f_ref, g_ref, low_ref, nb_ref, in_ref, out_ref, xt, fpad, gpad, rel, gf, gg, acc):
    voxels = LAYER + ROW
    fill_padded(fpad, f_ref, voxels)
    fill_padded(gpad, g_ref, voxels)
    for t in range(LAYER // T):
        xt[:, t * T : (t + 1) * T] = low_ref[t * T : (t + 1) * T, :].T
    fill_places(rel, nb_ref, range(9), LAYER + T)
    acc[...] = in_ref[...]

    @pl.loop(0, LAYER // CHUNK_W)
    def _(o):
        add_weight_terms(o, list(range(9)), xt, 0, rel, fpad, gpad, gf, gg, acc)

    for k in range(14):
        out_ref[k * T : (k + 1) * T, :] = (acc[k * T : (k + 1) * T, :] * scale).astype(out_ref.dtype)
    for k in range(13):
        out_ref[(26 - k) * T : (27 - k) * T, :] = (
            acc[(14 + k) * T : (15 + k) * T, :].T * scale
        ).astype(out_ref.dtype)
    if out_ref.shape[0] > 27 * T:
        out_ref[27 * T :, :] = jnp.zeros((out_ref.shape[0] - 27 * T, out_ref.shape[1]), out_ref.dtype)


def weight_scratch(voxels, columns, channels):
    return [
        pltpu.VMEM((2 * channels, columns), jnp.bfloat16),
        pltpu.VMEM((voxels + 2 * ROW, channels), jnp.bfloat16),
        pltpu.VMEM((voxels + 2 * ROW, channels), jnp.bfloat16),
    ]


def grad_w_inner(feats, grads, neigh):
    voxels, channels = feats.shape
    return pl.pallas_call(
        functools.partial(weight_inner_kernel, voxels),
        out_shape=jax.ShapeDtypeStruct((27 * T, channels), jnp.float32),
        in_specs=[VMEM] * 3,
        out_specs=VMEM,
        scratch_shapes=weight_scratch(voxels, voxels, channels)
        + [
            pltpu.VMEM((16, voxels), jnp.int32),
            pltpu.VMEM((9 * T, CHUNK_W), jnp.bfloat16),
            pltpu.VMEM((9 * T, CHUNK_W), jnp.bfloat16),
        ],
        compiler_params=pltpu.CompilerParams(vmem_limit_bytes=VMEM_LIMIT),
        cost_estimate=pl.CostEstimate(flops=8 * 10**9, bytes_accessed=4 * 10**6, transcendentals=0),
        name="weight_gradient_inner",
    )(feats, grads, neigh)


def grad_w_halo(feats, grads, low, neigh, partial, scale, rows):
    voxels, channels = feats.shape
    return pl.pallas_call(
        functools.partial(weight_halo_kernel, scale),
        out_shape=jax.ShapeDtypeStruct((rows, channels), jnp.bfloat16),
        in_specs=[VMEM] * 5,
        out_specs=VMEM,
        scratch_shapes=weight_scratch(LAYER + ROW, LAYER, channels)
        + [
            pltpu.VMEM((16, LAYER + T), jnp.int32),
            pltpu.VMEM((9 * T, CHUNK_W), jnp.bfloat16),
            pltpu.VMEM((9 * T, CHUNK_W), jnp.bfloat16),
            pltpu.VMEM((27 * T, channels), jnp.float32),
        ],
        compiler_params=pltpu.CompilerParams(vmem_limit_bytes=VMEM_LIMIT),
        cost_estimate=pl.CostEstimate(flops=3 * 10**9, bytes_accessed=4 * 10**6, transcendentals=0),
        name="weight_gradient_halo",
    )(feats, grads, low, neigh, partial)


def conv_kernel(voxels, layer, make_wt, f_ref, g_ref, low_ref, high_ref, nb_ref, w_ref, *rest):
    if make_wt:
        conv_ref, gin_ref, wt, xe, rel, relt, gf, gg = rest[-8:]
    else:
        wt = rest[0]
        conv_ref, gin_ref, xe, rel, relt, gf, gg = rest[-7:]
    channels = f_ref.shape[1]
    step = pl.program_id(0)
    layers = voxels // LAYER

    @pl.when(step == 0)
    def _():
        edge = jnp.zeros((ROW, 2 * channels), jnp.bfloat16)
        xe[0:ROW, :] = edge
        xe[ROW + 3 * LAYER :, :] = edge
        for near in (-1, 0, 1):
            to = slice(ROW + (near + 1) * LAYER, ROW + (near + 2) * LAYER)
            if layer + near < 0:
                xe[to, :] = low_ref[...]
            elif layer + near >= layers:
                xe[to, :] = high_ref[...]
            else:
                rows = slice((layer + near) * LAYER, (layer + near + 1) * LAYER)
                xe[to, 0:channels] = f_ref[rows, :]
                xe[to, channels:] = g_ref[rows, :]
        if make_wt:
            for k in range(27):
                wt[k * T : (k + 1) * T, :] = w_ref[(26 - k) * T : (27 - k) * T, :].T
        for k in range(27):
            row = nb_ref[k, :, layer * LAYER : (layer + 1) * LAYER]
            rel[k : k + 1, :] = row_in_scene_window(row, ROW * offset_of(k)[1])
        rel[27:, :] = jnp.full((5, LAYER), -1, jnp.int32)
        for t in range(LAYER // T):
            relt[t * T : (t + 1) * T, :] = rel[:, t * T : (t + 1) * T].T.astype(jnp.bfloat16)

    spot = lax.broadcasted_iota(jnp.int32, (T, T), 1).astype(jnp.bfloat16)
    base = pl.multiple_of(step * CHUNK_C, CHUNK_C)
    for h in range(CHUNK_C // T):
        rows = slice(h * T, (h + 1) * T)
        mine = relt[pl.ds(pl.multiple_of(base + h * T, T), T), :]
        for dz in (-1, 0, 1):
            for dy in (-1, 0, 1):
                start = base + (h * T + ROW + ROW * dy + LAYER * (dz + 1))
                window = xe[pl.ds(pl.multiple_of(start, ROW), T), :]
                first = 9 * (dz + 1) + 3 * (dy + 1)
                ks = [k for k in range(first, first + 3) if k != 13]
                hot = jnp.concatenate([one_hot(mine[:, k : k + 1] == spot) for k in ks], axis=0)
                picked = jnp.dot(hot, window, preferred_element_type=jnp.float32)
                picked = picked.astype(jnp.bfloat16)
                for q, k in enumerate(ks):
                    part = picked[q * T : (q + 1) * T]
                    gf[rows, k * T : (k + 1) * T] = part[:, :channels]
                    gg[rows, k * T : (k + 1) * T] = part[:, channels:]
                if first <= 13 < first + 3:
                    gf[rows, 13 * T : 14 * T] = window[:, :channels]
                    gg[rows, 13 * T : 14 * T] = window[:, channels:]
    conv_ref[...] = jnp.dot(gf[...], w_ref[...], preferred_element_type=jnp.float32).astype(jnp.bfloat16)
    gin_ref[...] = jnp.dot(gg[...], wt[...], preferred_element_type=jnp.float32).astype(jnp.bfloat16)


def conv_layer(feats, grads, low, high, neigh, weight, layer, earlier):
    voxels, channels = feats.shape
    out = jax.ShapeDtypeStruct((voxels, channels), jnp.bfloat16)
    turned = jax.ShapeDtypeStruct(weight.shape, jnp.bfloat16)
    steps = LAYER // CHUNK_C
    block = pl.BlockSpec((CHUNK_C, channels), lambda i: (i + layer * steps, 0))
    make_wt = earlier is None
    operands = [feats, grads, low, high, neigh, weight]
    if not make_wt:
        conv_out, grad_in, wt = earlier
        operands += [wt, conv_out, grad_in]
    results = pl.pallas_call(
        functools.partial(conv_kernel, voxels, layer, make_wt),
        grid=(steps,),
        out_shape=(out, out) + ((turned,) if make_wt else ()),
        in_specs=[VMEM] * 6 + ([] if make_wt else [VMEM] + [pl.BlockSpec(memory_space=pl.ANY)] * 2),
        out_specs=(block, block) + ((VMEM,) if make_wt else ()),
        input_output_aliases={} if make_wt else {7: 0, 8: 1},
        scratch_shapes=[
            pltpu.VMEM((2 * ROW + 3 * LAYER, 2 * channels), jnp.bfloat16),
            pltpu.VMEM((32, LAYER), jnp.int32),
            pltpu.VMEM((LAYER, 32), jnp.bfloat16),
            pltpu.VMEM((CHUNK_C, 27 * T), jnp.bfloat16),
            pltpu.VMEM((CHUNK_C, 27 * T), jnp.bfloat16),
        ],
        compiler_params=pltpu.CompilerParams(vmem_limit_bytes=VMEM_LIMIT),
        cost_estimate=pl.CostEstimate(flops=10**10, bytes_accessed=6 * 10**6, transcendentals=0),
        name="conv_layer_%d" % layer,
    )(*operands)
    return tuple(results) if make_wt else (results[0], results[1], wt)


def sum_parts(parts):
    return jnp.sum(parts.astype(jnp.float32), axis=0).astype(jnp.bfloat16)


def to_all(part, axis):
    spread = jnp.broadcast_to(part[None], (lax.axis_size(axis),) + part.shape)
    return lax.all_to_all(spread, axis, 0, 0, tiled=True)


def local(features, neighbours, weight, grad_out):
    feats, grads = features[0], grad_out[0]
    neigh = jnp.swapaxes(neighbours, 0, 1)
    voxels, channels = feats.shape
    space, dp = lax.axis_size("space"), lax.axis_size("dp")
    up = [(i, i + 1) for i in range(space - 1)]
    down = [(i + 1, i) for i in range(space - 1)]
    last = jnp.concatenate([feats[voxels - LAYER :], grads[voxels - LAYER :]], axis=1)
    first = jnp.concatenate([feats[:LAYER], grads[:LAYER]], axis=1)
    low = lax.ppermute(last, "space", up)
    high = lax.ppermute(first, "space", down)

    scale = 1.0 / math.sqrt(dp * space * voxels)
    share = -(-27 * channels // (16 * dp)) * 16
    inner = grad_w_inner(feats, grads, neigh)
    low, high, inner = lax.optimization_barrier((low, high, inner))
    partial = grad_w_halo(feats, grads, low, neigh, inner, scale, share * dp)
    flat_weight = weight.reshape(27 * channels, channels)
    layers = voxels // LAYER
    order = list(range(1, layers)) + [0]

    def conv(done, count):
        for _ in range(count):
            done = conv_layer(feats, grads, low, high, neigh, flat_weight, order.pop(0), done)
        return done

    pieces = lax.all_to_all(partial.reshape(dp, share, channels), "dp", 0, 0, tiled=True)
    done = conv(None, 1)
    pieces, done = lax.optimization_barrier((pieces, done))
    pieces = to_all(sum_parts(pieces), "space")
    done = conv(done, 1)
    pieces, done = lax.optimization_barrier((pieces, done))
    whole = to_all(sum_parts(pieces), "dp")
    conv_out, grad_in, _ = conv(done, len(order))
    grad_w = whole.reshape(dp * share, channels)[: 27 * channels].astype(jnp.float32)
    return conv_out[None], grad_in[None], grad_w.reshape(27, channels, channels)


def solution(mesh):
    in_specs = (P("dp", "space", None), P("dp", None, "space"), P(), P("dp", "space", None))
    out_specs = (P("dp", "space", None), P("dp", "space", None), P())
    return jax.shard_map(local, mesh=mesh, in_specs=in_specs, out_specs=out_specs, check_vma=False)
```

```python
import functools
import math

import jax
import jax.numpy as jnp
from jax import lax
from jax.experimental import pallas as pl
from jax.experimental.pallas import tpu as pltpu
from jax.sharding import PartitionSpec as P

PSIDE = 64
ROW = PSIDE // 4
LAYER = PSIDE * ROW
T = 128
CHUNK_W = 512
CHUNK_C = 512
VMEM_LIMIT = 28 * 1024 * 1024
CONV_VMEM_LIMIT = 36 * 1024 * 1024
VMEM = pl.BlockSpec(memory_space=pltpu.VMEM)


def offset_of(k):
    return k // 9 - 1, (k // 3) % 3 - 1, k % 3 - 1


def row_in_scene_window(neighbours, shift):
    return jnp.where(neighbours >= 0, (neighbours - shift) & (T - 1), -1)


def one_hot(hit):
    return jnp.where(hit, jnp.ones((), jnp.bfloat16), jnp.zeros((), jnp.bfloat16))


def fill_padded(pad, ref, voxels):
    edge = jnp.zeros((ROW, ref.shape[1]), jnp.bfloat16)
    pad[0:ROW, :] = edge
    pad[ROW + voxels : 2 * ROW + voxels, :] = edge
    pad[ROW : ROW + voxels, :] = ref[0:voxels, :]


def fill_places(rel, nb_ref, ks, voxels):
    none = jnp.full((1, ROW), -1, jnp.int32)
    for k in ks:
        dy = offset_of(k)[1]
        row = row_in_scene_window(nb_ref[k, :, 0:voxels], 0)
        if dy == -1:
            row = jnp.concatenate([row[:, ROW:], none], axis=1)
        elif dy == 1:
            row = jnp.concatenate([none, row[:, : voxels - ROW]], axis=1)
        rel[k : k + 1, :] = row


def add_weight_terms(o, ks, xt, source, rel, fpad, gpad, gf, gg, acc):
    channels = fpad.shape[1]
    base = pl.multiple_of(o * CHUNK_W, CHUNK_W)
    spot = lax.broadcasted_iota(jnp.int32, (T, T), 0)
    for h in range(CHUNK_W // T):
        cols = pl.ds(pl.multiple_of(base + h * T, T), T)
        window = xt[:, pl.ds(pl.multiple_of(base + source + h * T, T), T)]
        for p in range(0, len(ks), 2):
            pair = ks[p : p + 2]
            hot = jnp.concatenate(
                [one_hot(rel[k : k + 1, cols] == spot) for k in pair], axis=1
            )
            picked = jnp.dot(window, hot, preferred_element_type=jnp.float32)
            picked = picked.astype(jnp.bfloat16)
            for q in range(len(pair)):
                at = (p + q) * T
                part = picked[:, q * T : (q + 1) * T]
                gf[at : at + T, h * T : (h + 1) * T] = part[:channels]
                gg[at : at + T, h * T : (h + 1) * T] = part[channels:]
    for dy in (-1, 0, 1):
        group = [k for k in ks if offset_of(k)[1] == dy]
        if not group:
            continue
        lo = ks.index(group[0]) * T
        hi = lo + len(group) * T
        rows = pl.ds(pl.multiple_of(base + ROW - ROW * dy, ROW), CHUNK_W)
        acc[group[0] * T : (group[-1] + 1) * T, :] += jnp.dot(
            gf[lo:hi, :], gpad[rows, :], preferred_element_type=jnp.float32
        )
        acc[(14 + group[0]) * T : (15 + group[-1]) * T, :] += jnp.dot(
            gg[lo:hi, :], fpad[rows, :], preferred_element_type=jnp.float32
        )


def weight_inner_kernel(voxels, f_ref, g_ref, nb_ref, acc, xt, fpad, gpad, rel, gf, gg):
    channels = f_ref.shape[1]
    fill_padded(fpad, f_ref, voxels)
    fill_padded(gpad, g_ref, voxels)
    for t in range(voxels // T):
        cols = slice(t * T, (t + 1) * T)
        xt[0:channels, cols] = f_ref[t * T : (t + 1) * T, :].T
        xt[channels : 2 * channels, cols] = g_ref[t * T : (t + 1) * T, :].T
    fill_places(rel, nb_ref, range(13), voxels)
    acc[...] = jnp.zeros_like(acc)

    @pl.loop(0, voxels // CHUNK_W)
    def _(o):
        add_weight_terms(o, [9, 10, 11, 12], xt, 0, rel, fpad, gpad, gf, gg, acc)
        base = pl.multiple_of(o * CHUNK_W, CHUNK_W)
        own = xt[0:channels, pl.ds(base, CHUNK_W)]
        rows = pl.ds(pl.multiple_of(base + ROW, ROW), CHUNK_W)
        acc[13 * T : 14 * T, :] += jnp.dot(
            own, gpad[rows, :], preferred_element_type=jnp.float32
        )

    @pl.loop(LAYER // CHUNK_W, voxels // CHUNK_W)
    def _(o):
        add_weight_terms(o, list(range(9)), xt, -LAYER, rel, fpad, gpad, gf, gg, acc)


def weight_halo_kernel(scale, f_ref, g_ref, low_ref, nb_ref, in_ref, out_ref, xt, fpad, gpad, rel, gf, gg, acc):
    voxels = LAYER + ROW
    fill_padded(fpad, f_ref, voxels)
    fill_padded(gpad, g_ref, voxels)
    for t in range(LAYER // T):
        xt[:, t * T : (t + 1) * T] = low_ref[t * T : (t + 1) * T, :].T
    fill_places(rel, nb_ref, range(9), LAYER + T)
    acc[...] = in_ref[...]

    @pl.loop(0, LAYER // CHUNK_W)
    def _(o):
        add_weight_terms(o, list(range(9)), xt, 0, rel, fpad, gpad, gf, gg, acc)

    for k in range(14):
        out_ref[k * T : (k + 1) * T, :] = (acc[k * T : (k + 1) * T, :] * scale).astype(out_ref.dtype)
    for k in range(13):
        out_ref[(26 - k) * T : (27 - k) * T, :] = (
            acc[(14 + k) * T : (15 + k) * T, :].T * scale
        ).astype(out_ref.dtype)
    if out_ref.shape[0] > 27 * T:
        out_ref[27 * T :, :] = jnp.zeros((out_ref.shape[0] - 27 * T, out_ref.shape[1]), out_ref.dtype)


def weight_scratch(voxels, columns, channels):
    return [
        pltpu.VMEM((2 * channels, columns), jnp.bfloat16),
        pltpu.VMEM((voxels + 2 * ROW, channels), jnp.bfloat16),
        pltpu.VMEM((voxels + 2 * ROW, channels), jnp.bfloat16),
    ]


def grad_w_inner(feats, grads, neigh):
    voxels, channels = feats.shape
    return pl.pallas_call(
        functools.partial(weight_inner_kernel, voxels),
        out_shape=jax.ShapeDtypeStruct((27 * T, channels), jnp.float32),
        in_specs=[VMEM] * 3,
        out_specs=VMEM,
        scratch_shapes=weight_scratch(voxels, voxels, channels)
        + [
            pltpu.VMEM((16, voxels), jnp.int32),
            pltpu.VMEM((9 * T, CHUNK_W), jnp.bfloat16),
            pltpu.VMEM((9 * T, CHUNK_W), jnp.bfloat16),
        ],
        compiler_params=pltpu.CompilerParams(vmem_limit_bytes=VMEM_LIMIT),
        cost_estimate=pl.CostEstimate(flops=8 * 10**9, bytes_accessed=4 * 10**6, transcendentals=0),
        name="weight_gradient_inner",
    )(feats, grads, neigh)


def grad_w_halo(feats, grads, low, neigh, partial, scale, rows):
    voxels, channels = feats.shape
    return pl.pallas_call(
        functools.partial(weight_halo_kernel, scale),
        out_shape=jax.ShapeDtypeStruct((rows, channels), jnp.bfloat16),
        in_specs=[VMEM] * 5,
        out_specs=VMEM,
        scratch_shapes=weight_scratch(LAYER + ROW, LAYER, channels)
        + [
            pltpu.VMEM((16, LAYER + T), jnp.int32),
            pltpu.VMEM((9 * T, CHUNK_W), jnp.bfloat16),
            pltpu.VMEM((9 * T, CHUNK_W), jnp.bfloat16),
            pltpu.VMEM((27 * T, channels), jnp.float32),
        ],
        compiler_params=pltpu.CompilerParams(vmem_limit_bytes=VMEM_LIMIT),
        cost_estimate=pl.CostEstimate(flops=3 * 10**9, bytes_accessed=4 * 10**6, transcendentals=0),
        name="weight_gradient_halo",
    )(feats, grads, low, neigh, partial)


def conv_kernel(voxels, layer, make_wt, f_ref, g_ref, low_ref, high_ref, nb_ref, w_hbm, *rest):
    if make_wt:
        conv_ref, gin_ref, wt, xe, nb, w_ref, rel, relt, gf, gg, sems = rest[-11:]
    else:
        wt_hbm = rest[0]
        conv_ref, gin_ref, xe, nb, w_ref, wt, rel, relt, gf, gg, sems = rest[-11:]
    channels = f_ref.shape[1]
    step = pl.program_id(0)
    layers = voxels // LAYER

    copies = []
    first, last = max(layer - 1, 0), min(layer + 1, layers - 1)
    rows = pl.ds(first * LAYER, (last - first + 1) * LAYER)
    to = pl.ds(ROW + (first - layer + 1) * LAYER, (last - first + 1) * LAYER)
    copies.append((f_ref.at[rows, :], xe.at[to, pl.ds(0, channels)]))
    copies.append((g_ref.at[rows, :], xe.at[to, pl.ds(channels, channels)]))
    if layer == 0:
        copies.append((low_ref, xe.at[pl.ds(ROW, LAYER), :]))
    if layer == layers - 1:
        copies.append((high_ref, xe.at[pl.ds(ROW + 2 * LAYER, LAYER), :]))
    copies.append((nb_ref.at[:, :, pl.ds(layer * LAYER, LAYER)], nb))
    copies.append((w_hbm, w_ref))
    if not make_wt:
        copies.append((wt_hbm, wt))
    copies = [
        pltpu.make_async_copy(source, target, sems.at[i])
        for i, (source, target) in enumerate(copies)
    ]
    late = 1 if make_wt else 2

    @pl.when(step == 0)
    def _():
        for copy in reversed(copies[:-late]):
            copy.start()
        for copy in copies[-late:]:
            copy.start()
        edge = jnp.zeros((ROW, 2 * channels), jnp.bfloat16)
        xe[0:ROW, :] = edge
        xe[ROW + 3 * LAYER :, :] = edge
        rel[27:, :] = jnp.full((5, LAYER), -1, jnp.int32)
        copies[-late - 1].wait()
        for k in range(27):
            rel[k : k + 1, :] = row_in_scene_window(nb[k], ROW * offset_of(k)[1])
        for t in range(LAYER // T):
            relt[t * T : (t + 1) * T, :] = rel[:, t * T : (t + 1) * T].T.astype(jnp.bfloat16)
        for copy in copies[: -late - 1]:
            copy.wait()

    spot = lax.broadcasted_iota(jnp.int32, (T, T), 1).astype(jnp.bfloat16)
    base = pl.multiple_of(step * CHUNK_C, CHUNK_C)
    for h in range(CHUNK_C // T):
        rows = slice(h * T, (h + 1) * T)
        mine = relt[pl.ds(pl.multiple_of(base + h * T, T), T), :]
        for dz in (-1, 0, 1):
            for dy in (-1, 0, 1):
                start = base + (h * T + ROW + ROW * dy + LAYER * (dz + 1))
                window = xe[pl.ds(pl.multiple_of(start, ROW), T), :]
                first = 9 * (dz + 1) + 3 * (dy + 1)
                ks = [k for k in range(first, first + 3) if k != 13]
                hot = jnp.concatenate([one_hot(mine[:, k : k + 1] == spot) for k in ks], axis=0)
                picked = jnp.dot(hot, window, preferred_element_type=jnp.float32)
                picked = picked.astype(jnp.bfloat16)
                for q, k in enumerate(ks):
                    part = picked[q * T : (q + 1) * T]
                    gf[rows, k * T : (k + 1) * T] = part[:, :channels]
                    gg[rows, k * T : (k + 1) * T] = part[:, channels:]
                if first <= 13 < first + 3:
                    gf[rows, 13 * T : 14 * T] = window[:, :channels]
                    gg[rows, 13 * T : 14 * T] = window[:, channels:]

    @pl.when(step == 0)
    def _():
        for copy in copies[-late:]:
            copy.wait()
        if make_wt:
            for k in range(27):
                wt[k * T : (k + 1) * T, :] = w_ref[(26 - k) * T : (27 - k) * T, :].T

    conv_ref[...] = jnp.dot(gf[...], w_ref[...], preferred_element_type=jnp.float32).astype(jnp.bfloat16)
    gin_ref[...] = jnp.dot(gg[...], wt[...], preferred_element_type=jnp.float32).astype(jnp.bfloat16)


def conv_layer(feats, grads, low, high, neigh, weight, layer, earlier):
    voxels, channels = feats.shape
    out = jax.ShapeDtypeStruct((voxels, channels), jnp.bfloat16)
    turned = jax.ShapeDtypeStruct(weight.shape, jnp.bfloat16)
    steps = LAYER // CHUNK_C
    block = pl.BlockSpec((CHUNK_C, channels), lambda i: (i + layer * steps, 0))
    make_wt = earlier is None
    operands = [feats, grads, low, high, neigh, weight]
    if not make_wt:
        conv_out, grad_in, wt = earlier
        operands += [wt, conv_out, grad_in]
    weights = pltpu.VMEM((27 * T, channels), jnp.bfloat16)
    results = pl.pallas_call(
        functools.partial(conv_kernel, voxels, layer, make_wt),
        grid=(steps,),
        out_shape=(out, out) + ((turned,) if make_wt else ()),
        in_specs=[pl.BlockSpec(memory_space=pltpu.HBM)] * len(operands),
        out_specs=(block, block) + ((VMEM,) if make_wt else ()),
        input_output_aliases={} if make_wt else {7: 0, 8: 1},
        scratch_shapes=[
            pltpu.VMEM((2 * ROW + 3 * LAYER, 2 * channels), jnp.bfloat16),
            pltpu.VMEM((27, 1, LAYER), jnp.int32),
        ]
        + [weights] * (1 if make_wt else 2)
        + [
            pltpu.VMEM((32, LAYER), jnp.int32),
            pltpu.VMEM((LAYER, 32), jnp.bfloat16),
            pltpu.VMEM((CHUNK_C, 27 * T), jnp.bfloat16),
            pltpu.VMEM((CHUNK_C, 27 * T), jnp.bfloat16),
            pltpu.SemaphoreType.DMA((8,)),
        ],
        compiler_params=pltpu.CompilerParams(vmem_limit_bytes=CONV_VMEM_LIMIT),
        cost_estimate=pl.CostEstimate(flops=10**10, bytes_accessed=6 * 10**6, transcendentals=0),
        name="conv_layer_%d" % layer,
    )(*operands)
    return tuple(results) if make_wt else (results[0], results[1], wt)


def sum_and_spread_kernel(parts_ref, out_ref):
    total = parts_ref[0].astype(jnp.float32)
    for i in range(1, parts_ref.shape[0]):
        total += parts_ref[i].astype(jnp.float32)
    total = total.astype(out_ref.dtype)
    for i in range(out_ref.shape[0]):
        out_ref[i] = total


def sum_and_spread(parts, axis):
    copies = pl.pallas_call(
        sum_and_spread_kernel,
        out_shape=jax.ShapeDtypeStruct((lax.axis_size(axis),) + parts.shape[1:], parts.dtype),
        in_specs=[VMEM],
        out_specs=VMEM,
        compiler_params=pltpu.CompilerParams(vmem_limit_bytes=VMEM_LIMIT),
        name="sum_for_" + axis,
    )(parts)
    return lax.all_to_all(copies, axis, 0, 0, tiled=True)


def widen_kernel(in_ref, out_ref):
    out_ref[...] = in_ref[...].astype(out_ref.dtype)


def widen(rows, count):
    channels = rows.shape[1]
    block = pl.BlockSpec((count // 3, channels), lambda i: (i, 0))
    return pl.pallas_call(
        widen_kernel,
        grid=(3,),
        out_shape=jax.ShapeDtypeStruct((count, channels), jnp.float32),
        in_specs=[block],
        out_specs=block,
        compiler_params=pltpu.CompilerParams(vmem_limit_bytes=VMEM_LIMIT),
        name="widen",
    )(rows)


def local(features, neighbours, weight, grad_out):
    feats, grads = features[0], grad_out[0]
    neigh = jnp.swapaxes(neighbours, 0, 1)
    voxels, channels = feats.shape
    space, dp = lax.axis_size("space"), lax.axis_size("dp")
    up = [(i, i + 1) for i in range(space - 1)]
    down = [(i + 1, i) for i in range(space - 1)]
    last = jnp.concatenate([feats[voxels - LAYER :], grads[voxels - LAYER :]], axis=1)
    first = jnp.concatenate([feats[:LAYER], grads[:LAYER]], axis=1)
    low = lax.ppermute(last, "space", up)
    high = lax.ppermute(first, "space", down)

    scale = 1.0 / math.sqrt(dp * space * voxels)
    share = -(-27 * channels // (16 * dp)) * 16
    inner = grad_w_inner(feats, grads, neigh)
    partial = grad_w_halo(feats, grads, low, neigh, inner, scale, share * dp)
    flat_weight = weight.reshape(27 * channels, channels)
    layers = voxels // LAYER
    order = list(range(1, layers)) + [0]

    def conv(done, count):
        for _ in range(count):
            done = conv_layer(feats, grads, low, high, neigh, flat_weight, order.pop(0), done)
        return done

    pieces = lax.all_to_all(partial.reshape(dp, share, channels), "dp", 0, 0, tiled=True)
    done = conv(None, 1)
    pieces, done = lax.optimization_barrier((pieces, done))
    pieces = sum_and_spread(pieces, "space")
    done = conv(done, 1)
    pieces, done = lax.optimization_barrier((pieces, done))
    whole = sum_and_spread(pieces, "dp")
    conv_out, grad_in, _ = conv(done, len(order))
    grad_w = widen(whole.reshape(dp * share, channels), 27 * channels)
    return conv_out[None], grad_in[None], grad_w.reshape(27, channels, channels)


def solution(mesh):
    in_specs = (P("dp", "space", None), P("dp", None, "space"), P(), P("dp", "space", None))
    out_specs = (P("dp", "space", None), P("dp", "space", None), P())
    return jax.shard_map(local, mesh=mesh, in_specs=in_specs, out_specs=out_specs, check_vma=False)
```

```python
import functools
import math

import jax
import jax.numpy as jnp
from jax import lax
from jax.experimental import pallas as pl
from jax.experimental.pallas import tpu as pltpu
from jax.sharding import PartitionSpec as P

PSIDE = 64
ROW = PSIDE // 4
LAYER = PSIDE * ROW
T = 128
CHUNK_W = 512
CHUNK_C = 512
VMEM_LIMIT = 28 * 1024 * 1024
CONV_VMEM_LIMIT = 58 * 1024 * 1024
VMEM = pl.BlockSpec(memory_space=pltpu.VMEM)


def offset_of(k):
    return k // 9 - 1, (k // 3) % 3 - 1, k % 3 - 1


def row_in_scene_window(neighbours, shift):
    return jnp.where(neighbours >= 0, (neighbours - shift) & (T - 1), -1)


def one_hot(hit):
    return jnp.where(hit, jnp.ones((), jnp.bfloat16), jnp.zeros((), jnp.bfloat16))


def fill_padded(pad, ref, voxels):
    edge = jnp.zeros((ROW, ref.shape[1]), jnp.bfloat16)
    pad[0:ROW, :] = edge
    pad[ROW + voxels : 2 * ROW + voxels, :] = edge
    pad[ROW : ROW + voxels, :] = ref[0:voxels, :]


def fill_places(rel, nb_ref, ks, tiles):
    lane = lax.broadcasted_iota(jnp.int32, (tiles, T), 1)
    none = jnp.full((1, T), -1, jnp.int32)
    for k in ks:
        dy = offset_of(k)[1]
        own = row_in_scene_window(nb_ref[k, 0:tiles, :], 0)
        if dy == -1:
            turned = pltpu.roll(own, T - ROW, 1)
            after = jnp.concatenate([turned[1:], none], axis=0)
            own = jnp.where(lane < T - ROW, turned, after)
        elif dy == 1:
            turned = pltpu.roll(own, ROW, 1)
            before = jnp.concatenate([none, turned[:-1]], axis=0)
            own = jnp.where(lane < ROW, before, turned)
        rel[k, :, :] = own


def add_weight_terms(o, ks, window_of, rel, fpad, gpad, gf, gg, acc):
    channels = fpad.shape[1]
    base = pl.multiple_of(o * CHUNK_W, CHUNK_W)
    spot = lax.broadcasted_iota(jnp.int32, (T, T), 0)
    for h in range(CHUNK_W // T):
        tile = o * (CHUNK_W // T) + h
        window = window_of(tile)
        for p in range(0, len(ks), 2):
            pair = ks[p : p + 2]
            hot = jnp.concatenate(
                [one_hot(rel[k, pl.ds(tile, 1), :] == spot) for k in pair], axis=1
            )
            picked = jnp.dot(window, hot, preferred_element_type=jnp.float32)
            picked = picked.astype(jnp.bfloat16)
            for q in range(len(pair)):
                at = (p + q) * T
                part = picked[:, q * T : (q + 1) * T]
                gf[at : at + T, h * T : (h + 1) * T] = part[:channels]
                gg[at : at + T, h * T : (h + 1) * T] = part[channels:]
    for dy in (-1, 0, 1):
        group = [k for k in ks if offset_of(k)[1] == dy]
        if not group:
            continue
        lo = ks.index(group[0]) * T
        hi = lo + len(group) * T
        rows = pl.ds(pl.multiple_of(base + ROW - ROW * dy, ROW), CHUNK_W)
        acc[group[0] * T : (group[-1] + 1) * T, :] += jnp.dot(
            gf[lo:hi, :], gpad[rows, :], preferred_element_type=jnp.float32
        )
        acc[(14 + group[0]) * T : (15 + group[-1]) * T, :] += jnp.dot(
            gg[lo:hi, :], fpad[rows, :], preferred_element_type=jnp.float32
        )


def weight_inner_kernel(voxels, f_ref, g_ref, nb_ref, acc, xt, fpad, gpad, rel, gf, gg):
    channels = f_ref.shape[1]
    fill_padded(fpad, f_ref, voxels)
    fill_padded(gpad, g_ref, voxels)
    fill_places(rel, nb_ref, range(13), voxels // T)
    acc[...] = jnp.zeros_like(acc)

    @pl.loop(0, voxels // CHUNK_W)
    def _(o):
        def turn(tile):
            cols = pl.ds(pl.multiple_of(tile * T, T), T)
            xt[0:channels, cols] = f_ref[cols, :].T
            xt[channels : 2 * channels, cols] = g_ref[cols, :].T
            return xt[:, cols]

        add_weight_terms(o, [9, 10, 11, 12], turn, rel, fpad, gpad, gf, gg, acc)
        base = pl.multiple_of(o * CHUNK_W, CHUNK_W)
        rows = pl.ds(pl.multiple_of(base + ROW, ROW), CHUNK_W)
        acc[13 * T : 14 * T, :] += jnp.dot(
            xt[0:channels, pl.ds(base, CHUNK_W)], gpad[rows, :], preferred_element_type=jnp.float32
        )

    @pl.loop(LAYER // CHUNK_W, voxels // CHUNK_W)
    def _(o):
        def below(tile):
            return xt[:, pl.ds(pl.multiple_of(tile * T - LAYER, T), T)]

        add_weight_terms(o, list(range(9)), below, rel, fpad, gpad, gf, gg, acc)


def weight_halo_kernel(scale, f_ref, g_ref, low_ref, nb_ref, in_ref, out_ref, fpad, gpad, rel, gf, gg, acc):
    voxels = LAYER + ROW
    fill_padded(fpad, f_ref, voxels)
    fill_padded(gpad, g_ref, voxels)
    fill_places(rel, nb_ref, range(9), LAYER // T)
    acc[...] = in_ref[...]

    @pl.loop(0, LAYER // CHUNK_W)
    def _(o):
        def halo(tile):
            return low_ref[pl.ds(pl.multiple_of(tile * T, T), T), :].T

        add_weight_terms(o, list(range(9)), halo, rel, fpad, gpad, gf, gg, acc)

    for k in range(14):
        out_ref[k * T : (k + 1) * T, :] = (acc[k * T : (k + 1) * T, :] * scale).astype(out_ref.dtype)
    for k in range(13):
        out_ref[(26 - k) * T : (27 - k) * T, :] = (
            acc[(14 + k) * T : (15 + k) * T, :].T * scale
        ).astype(out_ref.dtype)
    if out_ref.shape[0] > 27 * T:
        out_ref[27 * T :, :] = jnp.zeros((out_ref.shape[0] - 27 * T, out_ref.shape[1]), out_ref.dtype)


def weight_scratch(rows, tiles, channels):
    return [
        pltpu.VMEM((rows + 2 * ROW, channels), jnp.bfloat16),
        pltpu.VMEM((rows + 2 * ROW, channels), jnp.bfloat16),
        pltpu.VMEM((13, tiles, T), jnp.int32),
        pltpu.VMEM((9 * T, CHUNK_W), jnp.bfloat16),
        pltpu.VMEM((9 * T, CHUNK_W), jnp.bfloat16),
    ]


def grad_w_inner(feats, grads, neigh):
    voxels, channels = feats.shape
    return pl.pallas_call(
        functools.partial(weight_inner_kernel, voxels),
        out_shape=jax.ShapeDtypeStruct((27 * T, channels), jnp.float32),
        in_specs=[VMEM] * 3,
        out_specs=VMEM,
        scratch_shapes=[pltpu.VMEM((2 * channels, voxels), jnp.bfloat16)]
        + weight_scratch(voxels, voxels // T, channels),
        compiler_params=pltpu.CompilerParams(vmem_limit_bytes=VMEM_LIMIT),
        cost_estimate=pl.CostEstimate(flops=8 * 10**9, bytes_accessed=4 * 10**6, transcendentals=0),
        name="weight_gradient_inner",
    )(feats, grads, neigh)


def grad_w_halo(feats, grads, low, neigh, partial, scale, rows):
    voxels, channels = feats.shape
    return pl.pallas_call(
        functools.partial(weight_halo_kernel, scale),
        out_shape=jax.ShapeDtypeStruct((rows, channels), jnp.bfloat16),
        in_specs=[VMEM] * 5,
        out_specs=VMEM,
        scratch_shapes=weight_scratch(LAYER + ROW, LAYER // T, channels)
        + [pltpu.VMEM((27 * T, channels), jnp.float32)],
        compiler_params=pltpu.CompilerParams(vmem_limit_bytes=VMEM_LIMIT),
        cost_estimate=pl.CostEstimate(flops=3 * 10**9, bytes_accessed=4 * 10**6, transcendentals=0),
        name="weight_gradient_halo",
    )(feats, grads, low, neigh, partial)


def conv_kernel(voxels, layer, make_wt, f_ref, g_ref, nb_ref, w_hbm, *rest):
    if make_wt:
        conv_ref, gin_ref, wt, xe, nb, w_ref, shift, gf, gg, sems = rest[-10:]
    else:
        wt_hbm = rest[0]
        conv_ref, gin_ref, xe, nb, w_ref, wt, shift, gf, gg, sems = rest[-10:]
    halos = list(rest[(0 if make_wt else 3):])
    channels = f_ref.shape[1]
    step = pl.program_id(0)
    layers = voxels // LAYER

    copies = []
    first, last = max(layer - 1, 0), min(layer + 1, layers - 1)
    rows = pl.ds(first * LAYER, (last - first + 1) * LAYER)
    to = pl.ds(ROW + (first - layer + 1) * LAYER, (last - first + 1) * LAYER)
    copies.append((f_ref.at[rows, :], xe.at[to, pl.ds(0, channels)]))
    copies.append((g_ref.at[rows, :], xe.at[to, pl.ds(channels, channels)]))
    if layer == 0:
        copies.append((halos.pop(0), xe.at[pl.ds(ROW, LAYER), :]))
    if layer == layers - 1:
        copies.append((halos.pop(0), xe.at[pl.ds(ROW + 2 * LAYER, LAYER), :]))
    copies.append((nb_ref.at[:, pl.ds(layer * (LAYER // T), LAYER // T), :], nb))
    copies.append((w_hbm, w_ref))
    if not make_wt:
        copies.append((wt_hbm, wt))
    copies = [
        pltpu.make_async_copy(source, target, sems.at[i])
        for i, (source, target) in enumerate(copies)
    ]
    late = 1 if make_wt else 2

    @pl.when(step == 0)
    def _():
        for copy in reversed(copies[:-late]):
            copy.start()
        for copy in copies[-late:]:
            copy.start()
        edge = jnp.zeros((ROW, 2 * channels), jnp.bfloat16)
        xe[0:ROW, :] = edge
        xe[ROW + 3 * LAYER :, :] = edge
        shift[27:, :] = jnp.zeros((5, T), jnp.int32)
        for k in range(27):
            shift[k : k + 1, :] = jnp.full((1, T), ROW * offset_of(k)[1], jnp.int32)
        for copy in copies[:-late]:
            copy.wait()

    spot = lax.broadcasted_iota(jnp.int32, (T, T), 1).astype(jnp.bfloat16)
    base = pl.multiple_of(step * CHUNK_C, CHUNK_C)
    for h in range(CHUNK_C // T):
        rows = slice(h * T, (h + 1) * T)
        mine = nb[:, step * (CHUNK_C // T) + h, :]
        mine = jnp.concatenate([mine, jnp.full((5, T), -1, jnp.int32)], axis=0)
        mine = row_in_scene_window(mine, shift[...]).T.astype(jnp.bfloat16)
        for dz in (-1, 0, 1):
            for dy in (-1, 0, 1):
                start = base + (h * T + ROW + ROW * dy + LAYER * (dz + 1))
                window = xe[pl.ds(pl.multiple_of(start, ROW), T), :]
                first = 9 * (dz + 1) + 3 * (dy + 1)
                ks = [k for k in range(first, first + 3) if k != 13]
                hot = jnp.concatenate([one_hot(mine[:, k : k + 1] == spot) for k in ks], axis=0)
                picked = jnp.dot(hot, window, preferred_element_type=jnp.float32)
                picked = picked.astype(jnp.bfloat16)
                for q, k in enumerate(ks):
                    part = picked[q * T : (q + 1) * T]
                    gf[rows, k * T : (k + 1) * T] = part[:, :channels]
                    gg[rows, k * T : (k + 1) * T] = part[:, channels:]
                if first <= 13 < first + 3:
                    gf[rows, 13 * T : 14 * T] = window[:, :channels]
                    gg[rows, 13 * T : 14 * T] = window[:, channels:]

    @pl.when(step == 0)
    def _():
        for copy in copies[-late:]:
            copy.wait()
        if make_wt:
            for k in range(27):
                wt[k * T : (k + 1) * T, :] = w_ref[(26 - k) * T : (27 - k) * T, :].T

    conv_ref[...] = jnp.dot(gf[...], w_ref[...], preferred_element_type=jnp.float32).astype(jnp.bfloat16)
    gin_ref[...] = jnp.dot(gg[...], wt[...], preferred_element_type=jnp.float32).astype(jnp.bfloat16)


def conv_layer(feats, grads, low, high, neigh, weight, layer, earlier):
    voxels, channels = feats.shape
    out = jax.ShapeDtypeStruct((voxels, channels), jnp.bfloat16)
    turned = jax.ShapeDtypeStruct(weight.shape, jnp.bfloat16)
    steps = LAYER // CHUNK_C
    block = pl.BlockSpec((CHUNK_C, channels), lambda i: (i + layer * steps, 0))
    make_wt = earlier is None
    operands = [feats, grads, neigh, weight]
    if not make_wt:
        conv_out, grad_in, wt = earlier
        operands += [wt, conv_out, grad_in]
    if layer == 0:
        operands.append(low)
    if layer == voxels // LAYER - 1:
        operands.append(high)
    weights = pltpu.VMEM((27 * T, channels), jnp.bfloat16)
    results = pl.pallas_call(
        functools.partial(conv_kernel, voxels, layer, make_wt),
        grid=(steps,),
        out_shape=(out, out) + ((turned,) if make_wt else ()),
        in_specs=[pl.BlockSpec(memory_space=pltpu.HBM)] * len(operands),
        out_specs=(block, block) + ((VMEM,) if make_wt else ()),
        input_output_aliases={} if make_wt else {5: 0, 6: 1},
        scratch_shapes=[
            pltpu.VMEM((2 * ROW + 3 * LAYER, 2 * channels), jnp.bfloat16),
            pltpu.VMEM((27, LAYER // T, T), jnp.int32),
        ]
        + [weights] * (1 if make_wt else 2)
        + [
            pltpu.VMEM((32, T), jnp.int32),
            pltpu.VMEM((CHUNK_C, 27 * T), jnp.bfloat16),
            pltpu.VMEM((CHUNK_C, 27 * T), jnp.bfloat16),
            pltpu.SemaphoreType.DMA((8,)),
        ],
        compiler_params=pltpu.CompilerParams(vmem_limit_bytes=CONV_VMEM_LIMIT),
        cost_estimate=pl.CostEstimate(flops=10**10, bytes_accessed=6 * 10**6, transcendentals=0),
        name="conv_layer_%d" % layer,
    )(*operands)
    return tuple(results) if make_wt else (results[0], results[1], wt)


def sum_and_spread_kernel(parts_ref, out_ref):
    total = parts_ref[0].astype(jnp.float32)
    for i in range(1, parts_ref.shape[0]):
        total += parts_ref[i].astype(jnp.float32)
    total = total.astype(out_ref.dtype)
    for i in range(out_ref.shape[0]):
        out_ref[i] = total


def sum_and_spread(parts, axis):
    copies = pl.pallas_call(
        sum_and_spread_kernel,
        out_shape=jax.ShapeDtypeStruct((lax.axis_size(axis),) + parts.shape[1:], parts.dtype),
        in_specs=[VMEM],
        out_specs=VMEM,
        compiler_params=pltpu.CompilerParams(vmem_limit_bytes=VMEM_LIMIT),
        name="sum_for_" + axis,
    )(parts)
    return lax.all_to_all(copies, axis, 0, 0, tiled=True)


def widen_kernel(in_ref, out_ref):
    out_ref[...] = in_ref[...].astype(out_ref.dtype)


def widen(rows, count):
    channels = rows.shape[1]
    block = pl.BlockSpec((count // 3, channels), lambda i: (i, 0))
    return pl.pallas_call(
        widen_kernel,
        grid=(3,),
        out_shape=jax.ShapeDtypeStruct((count, channels), jnp.float32),
        in_specs=[block],
        out_specs=block,
        compiler_params=pltpu.CompilerParams(vmem_limit_bytes=VMEM_LIMIT),
        name="widen",
    )(rows)


def local(features, neighbours, weight, grad_out):
    feats, grads = features[0], grad_out[0]
    voxels, channels = feats.shape
    neigh = neighbours.reshape(27, voxels // T, T)
    space, dp = lax.axis_size("space"), lax.axis_size("dp")
    up = [(i, i + 1) for i in range(space - 1)]
    down = [(i + 1, i) for i in range(space - 1)]
    last = jnp.concatenate([feats[voxels - LAYER :], grads[voxels - LAYER :]], axis=1)
    first = jnp.concatenate([feats[:LAYER], grads[:LAYER]], axis=1)
    low = lax.ppermute(last, "space", up)
    high = lax.ppermute(first, "space", down)

    scale = 1.0 / math.sqrt(dp * space * voxels)
    share = -(-27 * channels // (16 * dp)) * 16
    inner = grad_w_inner(feats, grads, neigh)
    partial = grad_w_halo(feats, grads, low, neigh, inner, scale, share * dp)
    partial, flat_weight = lax.optimization_barrier(
        (partial, weight.reshape(27 * channels, channels))
    )
    layers = voxels // LAYER
    order = list(range(1, layers)) + [0]

    def conv(done, count):
        for _ in range(count):
            done = conv_layer(feats, grads, low, high, neigh, flat_weight, order.pop(0), done)
        return done

    pieces = lax.all_to_all(partial.reshape(dp, share, channels), "dp", 0, 0, tiled=True)
    done = conv(None, 1)
    pieces, done = lax.optimization_barrier((pieces, done))
    pieces = sum_and_spread(pieces, "space")
    done = conv(done, 1)
    pieces, done = lax.optimization_barrier((pieces, done))
    whole = sum_and_spread(pieces, "dp")
    conv_out, grad_in, _ = conv(done, len(order))
    grad_w = widen(whole.reshape(dp * share, channels), 27 * channels)
    return conv_out[None], grad_in[None], grad_w.reshape(27, channels, channels)


def solution(mesh):
    in_specs = (P("dp", "space", None), P("dp", None, "space"), P(), P("dp", "space", None))
    out_specs = (P("dp", "space", None), P("dp", "space", None), P())
    return jax.shard_map(local, mesh=mesh, in_specs=in_specs, out_specs=out_specs, check_vma=False)
```

```python
import functools
import math

import jax
import jax.numpy as jnp
from jax import lax
from jax.experimental import pallas as pl
from jax.experimental.pallas import tpu as pltpu
from jax.sharding import PartitionSpec as P

PSIDE = 64
ROW = PSIDE // 4
LAYER = PSIDE * ROW
T = 128
CHUNK_W = 512
CHUNK_C = 256
VMEM_LIMIT = 28 * 1024 * 1024
CONV_VMEM_LIMIT = 58 * 1024 * 1024
VMEM = pl.BlockSpec(memory_space=pltpu.VMEM)


def offset_of(k):
    return k // 9 - 1, (k // 3) % 3 - 1, k % 3 - 1


def row_in_scene_window(neighbours, shift):
    return jnp.where(neighbours >= 0, (neighbours - shift) & (T - 1), -1)


def one_hot(hit):
    return jnp.where(hit, jnp.ones((), jnp.bfloat16), jnp.zeros((), jnp.bfloat16))


def fill_padded(pad, ref, voxels):
    edge = jnp.zeros((ROW, ref.shape[1]), jnp.bfloat16)
    pad[0:ROW, :] = edge
    pad[ROW + voxels : 2 * ROW + voxels, :] = edge
    pad[ROW : ROW + voxels, :] = ref[0:voxels, :]


def fill_places(rel, nb_ref, ks, tiles):
    lane = lax.broadcasted_iota(jnp.int32, (tiles, T), 1)
    none = jnp.full((1, T), -1, jnp.int32)
    for k in ks:
        dy = offset_of(k)[1]
        own = row_in_scene_window(nb_ref[k, 0:tiles, :], 0)
        if dy == -1:
            turned = pltpu.roll(own, T - ROW, 1)
            after = jnp.concatenate([turned[1:], none], axis=0)
            own = jnp.where(lane < T - ROW, turned, after)
        elif dy == 1:
            turned = pltpu.roll(own, ROW, 1)
            before = jnp.concatenate([none, turned[:-1]], axis=0)
            own = jnp.where(lane < ROW, before, turned)
        rel[k, :, :] = own


def add_weight_terms(o, ks, window_of, rel, fpad, gpad, gf, gg, acc):
    channels = fpad.shape[1]
    base = pl.multiple_of(o * CHUNK_W, CHUNK_W)
    spot = lax.broadcasted_iota(jnp.int32, (T, T), 0)
    for h in range(CHUNK_W // T):
        tile = o * (CHUNK_W // T) + h
        window = window_of(tile)
        for p in range(0, len(ks), 2):
            pair = ks[p : p + 2]
            hot = jnp.concatenate(
                [one_hot(rel[k, pl.ds(tile, 1), :] == spot) for k in pair], axis=1
            )
            picked = jnp.dot(window, hot, preferred_element_type=jnp.float32)
            picked = picked.astype(jnp.bfloat16)
            for q in range(len(pair)):
                at = (p + q) * T
                part = picked[:, q * T : (q + 1) * T]
                gf[at : at + T, h * T : (h + 1) * T] = part[:channels]
                gg[at : at + T, h * T : (h + 1) * T] = part[channels:]
    for dy in (-1, 0, 1):
        group = [k for k in ks if offset_of(k)[1] == dy]
        if not group:
            continue
        lo = ks.index(group[0]) * T
        hi = lo + len(group) * T
        rows = pl.ds(pl.multiple_of(base + ROW - ROW * dy, ROW), CHUNK_W)
        acc[group[0] * T : (group[-1] + 1) * T, :] += jnp.dot(
            gf[lo:hi, :], gpad[rows, :], preferred_element_type=jnp.float32
        )
        acc[(14 + group[0]) * T : (15 + group[-1]) * T, :] += jnp.dot(
            gg[lo:hi, :], fpad[rows, :], preferred_element_type=jnp.float32
        )


def weight_inner_kernel(voxels, f_ref, g_ref, nb_ref, acc, xt, fpad, gpad, rel, gf, gg):
    channels = f_ref.shape[1]
    fill_padded(fpad, f_ref, voxels)
    fill_padded(gpad, g_ref, voxels)
    fill_places(rel, nb_ref, range(13), voxels // T)
    acc[...] = jnp.zeros_like(acc)

    @pl.loop(0, voxels // CHUNK_W)
    def _(o):
        def turn(tile):
            cols = pl.ds(pl.multiple_of(tile * T, T), T)
            xt[0:channels, cols] = f_ref[cols, :].T
            xt[channels : 2 * channels, cols] = g_ref[cols, :].T
            return xt[:, cols]

        add_weight_terms(o, [9, 10, 11, 12], turn, rel, fpad, gpad, gf, gg, acc)
        base = pl.multiple_of(o * CHUNK_W, CHUNK_W)
        rows = pl.ds(pl.multiple_of(base + ROW, ROW), CHUNK_W)
        acc[13 * T : 14 * T, :] += jnp.dot(
            xt[0:channels, pl.ds(base, CHUNK_W)], gpad[rows, :], preferred_element_type=jnp.float32
        )

    @pl.loop(LAYER // CHUNK_W, voxels // CHUNK_W)
    def _(o):
        def below(tile):
            return xt[:, pl.ds(pl.multiple_of(tile * T - LAYER, T), T)]

        add_weight_terms(o, list(range(9)), below, rel, fpad, gpad, gf, gg, acc)


def weight_halo_kernel(scale, f_ref, g_ref, low_ref, nb_ref, in_ref, out_ref, fpad, gpad, rel, gf, gg, acc):
    voxels = LAYER + ROW
    fill_padded(fpad, f_ref, voxels)
    fill_padded(gpad, g_ref, voxels)
    fill_places(rel, nb_ref, range(9), LAYER // T)
    acc[...] = in_ref[...]

    @pl.loop(0, LAYER // CHUNK_W)
    def _(o):
        def halo(tile):
            return low_ref[pl.ds(pl.multiple_of(tile * T, T), T), :].T

        add_weight_terms(o, list(range(9)), halo, rel, fpad, gpad, gf, gg, acc)

    for k in range(14):
        out_ref[k * T : (k + 1) * T, :] = (acc[k * T : (k + 1) * T, :] * scale).astype(out_ref.dtype)
    for k in range(13):
        out_ref[(26 - k) * T : (27 - k) * T, :] = (
            acc[(14 + k) * T : (15 + k) * T, :].T * scale
        ).astype(out_ref.dtype)
    if out_ref.shape[0] > 27 * T:
        out_ref[27 * T :, :] = jnp.zeros((out_ref.shape[0] - 27 * T, out_ref.shape[1]), out_ref.dtype)


def weight_scratch(rows, tiles, channels):
    return [
        pltpu.VMEM((rows + 2 * ROW, channels), jnp.bfloat16),
        pltpu.VMEM((rows + 2 * ROW, channels), jnp.bfloat16),
        pltpu.VMEM((13, tiles, T), jnp.int32),
        pltpu.VMEM((9 * T, CHUNK_W), jnp.bfloat16),
        pltpu.VMEM((9 * T, CHUNK_W), jnp.bfloat16),
    ]


def grad_w_inner(feats, grads, neigh):
    voxels, channels = feats.shape
    return pl.pallas_call(
        functools.partial(weight_inner_kernel, voxels),
        out_shape=jax.ShapeDtypeStruct((27 * T, channels), jnp.float32),
        in_specs=[VMEM] * 3,
        out_specs=VMEM,
        scratch_shapes=[pltpu.VMEM((2 * channels, voxels), jnp.bfloat16)]
        + weight_scratch(voxels, voxels // T, channels),
        compiler_params=pltpu.CompilerParams(vmem_limit_bytes=VMEM_LIMIT),
        cost_estimate=pl.CostEstimate(flops=8 * 10**9, bytes_accessed=4 * 10**6, transcendentals=0),
        name="weight_gradient_inner",
    )(feats, grads, neigh)


def grad_w_halo(feats, grads, low, neigh, partial, scale, rows):
    voxels, channels = feats.shape
    return pl.pallas_call(
        functools.partial(weight_halo_kernel, scale),
        out_shape=jax.ShapeDtypeStruct((rows, channels), jnp.bfloat16),
        in_specs=[VMEM] * 5,
        out_specs=VMEM,
        scratch_shapes=weight_scratch(LAYER + ROW, LAYER // T, channels)
        + [pltpu.VMEM((27 * T, channels), jnp.float32)],
        compiler_params=pltpu.CompilerParams(vmem_limit_bytes=VMEM_LIMIT),
        cost_estimate=pl.CostEstimate(flops=3 * 10**9, bytes_accessed=4 * 10**6, transcendentals=0),
        name="weight_gradient_halo",
    )(feats, grads, low, neigh, partial)


def conv_kernel(voxels, layer, make_wt, f_ref, g_ref, nb_ref, w_hbm, *rest):
    if make_wt:
        conv_ref, gin_ref, wt, xe, nb, w_ref, shift, gf, gg, gf2, gg2, sems = rest[-12:]
    else:
        wt_hbm = rest[0]
        conv_ref, gin_ref, xe, nb, w_ref, wt, shift, gf, gg, gf2, gg2, sems = rest[-12:]
    halos = list(rest[(0 if make_wt else 3):])
    channels = f_ref.shape[1]
    layers = voxels // LAYER

    first, last = max(layer - 1, 0), min(layer + 1, layers - 1)
    rows = pl.ds(first * LAYER, (last - first + 1) * LAYER)
    to = pl.ds(ROW + (first - layer + 1) * LAYER, (last - first + 1) * LAYER)
    copies = [
        (nb_ref.at[:, pl.ds(layer * (LAYER // T), LAYER // T), :], nb),
        (f_ref.at[rows, :], xe.at[to, pl.ds(0, channels)]),
        (g_ref.at[rows, :], xe.at[to, pl.ds(channels, channels)]),
    ]
    if layer == 0:
        copies.append((halos.pop(0), xe.at[pl.ds(ROW, LAYER), :]))
    if layer == layers - 1:
        copies.append((halos.pop(0), xe.at[pl.ds(ROW + 2 * LAYER, LAYER), :]))
    early = len(copies)
    copies.append((w_hbm, w_ref))
    if not make_wt:
        copies.append((wt_hbm, wt))
    copies = [
        pltpu.make_async_copy(source, target, sems.at[i])
        for i, (source, target) in enumerate(copies)
    ]
    for copy in copies:
        copy.start()
    edge = jnp.zeros((ROW, 2 * channels), jnp.bfloat16)
    xe[0:ROW, :] = edge
    xe[ROW + 3 * LAYER :, :] = edge
    shift[27:, :] = jnp.zeros((5, T), jnp.int32)
    for k in range(27):
        shift[k : k + 1, :] = jnp.full((1, T), ROW * offset_of(k)[1], jnp.int32)
    for copy in copies[:early]:
        copy.wait()

    spot = lax.broadcasted_iota(jnp.int32, (T, T), 1).astype(jnp.bfloat16)
    buffers = ((gf, gg), (gf2, gg2))

    def places(tile):
        mine = jnp.concatenate([nb[:, tile, :], jnp.full((5, T), -1, jnp.int32)], axis=0)
        return row_in_scene_window(mine, shift[...]).T.astype(jnp.bfloat16)

    def gather(chunk, h, mine, dz, dy):
        to_f, to_g = buffers[chunk % 2]
        rows = slice(h * T, (h + 1) * T)
        start = chunk * CHUNK_C + h * T + ROW + ROW * dy + LAYER * (dz + 1)
        window = xe[start : start + T, :]
        first = 9 * (dz + 1) + 3 * (dy + 1)
        ks = [k for k in range(first, first + 3) if k != 13]
        hot = jnp.concatenate([one_hot(mine[:, k : k + 1] == spot) for k in ks], axis=0)
        picked = jnp.dot(hot, window, preferred_element_type=jnp.float32)
        picked = picked.astype(jnp.bfloat16)
        for q, k in enumerate(ks):
            part = picked[q * T : (q + 1) * T]
            to_f[rows, k * T : (k + 1) * T] = part[:, :channels]
            to_g[rows, k * T : (k + 1) * T] = part[:, channels:]
        if first <= 13 < first + 3:
            to_f[rows, 13 * T : 14 * T] = window[:, :channels]
            to_g[rows, 13 * T : 14 * T] = window[:, channels:]

    def product(chunk):
        rows = slice(chunk * CHUNK_C, (chunk + 1) * CHUNK_C)
        for out, picked, kernels in zip((conv_ref, gin_ref), buffers[chunk % 2], (w_ref, wt)):
            total = None
            for part in range(3):
                span = slice(part * 9 * T, (part + 1) * 9 * T)
                term = jnp.dot(picked[:, span], kernels[span, :], preferred_element_type=jnp.float32)
                total = term if total is None else total + term
                if part == 2:
                    out[rows, :] = total.astype(jnp.bfloat16)
                yield

    pending = iter(())
    for chunk in range(LAYER // CHUNK_C):
        turn = 0
        for h in range(CHUNK_C // T):
            mine = places(chunk * (CHUNK_C // T) + h)
            for dz in (-1, 0, 1):
                for dy in (-1, 0, 1):
                    gather(chunk, h, mine, dz, dy)
                    turn += 1
                    if turn % 3 == 0:
                        next(pending, None)
        for _ in pending:
            pass
        if chunk == 0:
            for copy in copies[early:]:
                copy.wait()
            if make_wt:
                for k in range(27):
                    wt[k * T : (k + 1) * T, :] = w_ref[(26 - k) * T : (27 - k) * T, :].T
        pending = product(chunk)
    for _ in pending:
        pass


def conv_layer(feats, grads, low, high, neigh, weight, layer, earlier):
    voxels, channels = feats.shape
    out = jax.ShapeDtypeStruct((voxels, channels), jnp.bfloat16)
    turned = jax.ShapeDtypeStruct(weight.shape, jnp.bfloat16)
    block = pl.BlockSpec((LAYER, channels), lambda i: (layer, 0))
    make_wt = earlier is None
    operands = [feats, grads, neigh, weight]
    if not make_wt:
        conv_out, grad_in, wt = earlier
        operands += [wt, conv_out, grad_in]
    if layer == 0:
        operands.append(low)
    if layer == voxels // LAYER - 1:
        operands.append(high)
    weights = pltpu.VMEM((27 * T, channels), jnp.bfloat16)
    results = pl.pallas_call(
        functools.partial(conv_kernel, voxels, layer, make_wt),
        grid=(1,),
        out_shape=(out, out) + ((turned,) if make_wt else ()),
        in_specs=[pl.BlockSpec(memory_space=pltpu.HBM)] * len(operands),
        out_specs=(block, block) + ((VMEM,) if make_wt else ()),
        input_output_aliases={} if make_wt else {5: 0, 6: 1},
        scratch_shapes=[
            pltpu.VMEM((2 * ROW + 3 * LAYER, 2 * channels), jnp.bfloat16),
            pltpu.VMEM((27, LAYER // T, T), jnp.int32),
        ]
        + [weights] * (1 if make_wt else 2)
        + [
            pltpu.VMEM((32, T), jnp.int32),
        ]
        + [pltpu.VMEM((CHUNK_C, 27 * T), jnp.bfloat16)] * 4
        + [
            pltpu.SemaphoreType.DMA((8,)),
        ],
        compiler_params=pltpu.CompilerParams(vmem_limit_bytes=CONV_VMEM_LIMIT),
        cost_estimate=pl.CostEstimate(flops=10**10, bytes_accessed=6 * 10**6, transcendentals=0),
        name="conv_layer_%d" % layer,
    )(*operands)
    return tuple(results) if make_wt else (results[0], results[1], wt)


def sum_parts_kernel(parts_ref, out_ref):
    total = parts_ref[0].astype(jnp.float32)
    for i in range(1, parts_ref.shape[0]):
        total += parts_ref[i].astype(jnp.float32)
    out_ref[...] = total


def sum_parts(parts):
    return pl.pallas_call(
        sum_parts_kernel,
        out_shape=jax.ShapeDtypeStruct(parts.shape[1:], jnp.float32),
        in_specs=[VMEM],
        out_specs=VMEM,
        compiler_params=pltpu.CompilerParams(vmem_limit_bytes=VMEM_LIMIT),
        name="sum_parts",
    )(parts)


def spread_kernel(part_ref, out_ref):
    part = part_ref[...].astype(out_ref.dtype)
    for i in range(out_ref.shape[0]):
        out_ref[i] = part


def spread(part, axis):
    copies = pl.pallas_call(
        spread_kernel,
        out_shape=jax.ShapeDtypeStruct((lax.axis_size(axis),) + part.shape, jnp.bfloat16),
        in_specs=[VMEM],
        out_specs=VMEM,
        compiler_params=pltpu.CompilerParams(vmem_limit_bytes=VMEM_LIMIT),
        name="spread",
    )(part)
    return lax.all_to_all(copies, axis, 0, 0, tiled=True)


def widen_kernel(in_ref, out_ref):
    out_ref[...] = in_ref[...].astype(out_ref.dtype)


def widen(rows, count):
    channels = rows.shape[1]
    block = pl.BlockSpec((count // 3, channels), lambda i: (i, 0))
    return pl.pallas_call(
        widen_kernel,
        grid=(3,),
        out_shape=jax.ShapeDtypeStruct((count, channels), jnp.float32),
        in_specs=[block],
        out_specs=block,
        compiler_params=pltpu.CompilerParams(vmem_limit_bytes=VMEM_LIMIT),
        name="widen",
    )(rows)


def local(features, neighbours, weight, grad_out):
    feats, grads = features[0], grad_out[0]
    voxels, channels = feats.shape
    neigh = neighbours.reshape(27, voxels // T, T)
    space, dp = lax.axis_size("space"), lax.axis_size("dp")
    up = [(i, i + 1) for i in range(space - 1)]
    down = [(i + 1, i) for i in range(space - 1)]
    last = jnp.concatenate([feats[voxels - LAYER :], grads[voxels - LAYER :]], axis=1)
    first = jnp.concatenate([feats[:LAYER], grads[:LAYER]], axis=1)
    low = lax.ppermute(last, "space", up)
    high = lax.ppermute(first, "space", down)

    scale = 1.0 / math.sqrt(dp * space * voxels)
    share = -(-27 * channels // (16 * dp)) * 16
    inner = grad_w_inner(feats, grads, neigh)
    partial = grad_w_halo(feats, grads, low, neigh, inner, scale, share * dp)
    partial, flat_weight = lax.optimization_barrier(
        (partial, weight.reshape(27 * channels, channels))
    )
    layers = voxels // LAYER
    order = list(range(1, layers)) + [0]

    def conv(done, count):
        for _ in range(count):
            done = conv_layer(feats, grads, low, high, neigh, flat_weight, order.pop(0), done)
        return done

    pieces = lax.all_to_all(partial.reshape(dp, share, channels), "dp", 0, 0, tiled=True)
    done = conv(None, 1)
    pieces, done = lax.optimization_barrier((pieces, done))
    total = lax.psum(sum_parts(pieces), "space")
    done = conv(done, 1)
    total, done = lax.optimization_barrier((total, done))
    whole = spread(total, "dp")
    conv_out, grad_in, _ = conv(done, len(order))
    grad_w = widen(whole.reshape(dp * share, channels), 27 * channels)
    return conv_out[None], grad_in[None], grad_w.reshape(27, channels, channels)


def solution(mesh):
    in_specs = (P("dp", "space", None), P("dp", None, "space"), P(), P("dp", "space", None))
    out_specs = (P("dp", "space", None), P("dp", "space", None), P())
    return jax.shard_map(local, mesh=mesh, in_specs=in_specs, out_specs=out_specs, check_vma=False)
```

```python
import functools
import math

import jax
import jax.numpy as jnp
from jax import lax
from jax.experimental import pallas as pl
from jax.experimental.pallas import tpu as pltpu
from jax.sharding import PartitionSpec as P

PSIDE = 64
ROW = PSIDE // 4
LAYER = PSIDE * ROW
T = 128
CHUNK_W = 512
CHUNK_C = 256
VMEM_LIMIT = 28 * 1024 * 1024
CONV_VMEM_LIMIT = 58 * 1024 * 1024
VMEM = pl.BlockSpec(memory_space=pltpu.VMEM)


def offset_of(k):
    return k // 9 - 1, (k // 3) % 3 - 1, k % 3 - 1


def row_in_scene_window(neighbours, shift):
    return jnp.where(neighbours >= 0, (neighbours - shift) & (T - 1), -1)


def one_hot(hit):
    return jnp.where(hit, jnp.ones((), jnp.bfloat16), jnp.zeros((), jnp.bfloat16))


def beside(xe, first, f_ref, g_ref, rows):
    channels = f_ref.shape[1]
    xe[first : first + rows, 0:channels] = f_ref[0:rows, :]
    xe[first : first + rows, channels:] = g_ref[0:rows, :]


def fill_edges(xe, shift):
    edge = jnp.zeros((ROW, xe.shape[1]), jnp.bfloat16)
    xe[0:ROW, :] = edge
    xe[xe.shape[0] - ROW :, :] = edge
    shift[...] = jnp.zeros_like(shift)
    for k in range(27):
        if offset_of(k)[1]:
            shift[k : k + 1, :] = jnp.full((1, T), ROW * offset_of(k)[1], jnp.int32)


def add_weight_terms(o, ks, source, center, f_ref, g_ref, nb_ref, xe, shift, gf, gg, acc):
    channels = f_ref.shape[1]
    spot = lax.broadcasted_iota(jnp.int32, (T, T), 1).astype(jnp.bfloat16)
    base = pl.multiple_of(o * CHUNK_W, CHUNK_W)
    pads = jnp.full((5, T), -1, jnp.int32)
    for h in range(CHUNK_W // T):
        rows = slice(h * T, (h + 1) * T)
        mine = jnp.concatenate([nb_ref[:, o * (CHUNK_W // T) + h, :], pads], axis=0)
        mine = row_in_scene_window(mine, shift[...]).T.astype(jnp.bfloat16)
        for dz, dy in sorted({offset_of(k)[:2] for k in ks}):
            some = [k for k in ks if offset_of(k)[:2] == (dz, dy)]
            start = base + (source + h * T + ROW * dy + LAYER * dz)
            window = xe[pl.ds(pl.multiple_of(start, ROW), T), :]
            hot = jnp.concatenate([one_hot(mine[:, k : k + 1] == spot) for k in some], axis=0)
            picked = jnp.dot(hot, window, preferred_element_type=jnp.float32)
            picked = picked.astype(jnp.bfloat16)
            for q, k in enumerate(some):
                part = picked[q * T : (q + 1) * T]
                gf[rows, k * T : (k + 1) * T] = part[:, :channels]
                gg[rows, k * T : (k + 1) * T] = part[:, channels:]
    here = pl.ds(base, CHUNK_W)
    if center:
        gg[:, 13 * T :] = g_ref[here, :]
    span = slice(ks[0] * T, (ks[-1] + 1) * T)
    acc[:, span] += jnp.dot(g_ref[here, :].T, gf[:, span], preferred_element_type=jnp.float32)
    last = ks[-1] + 1 + (1 if center else 0)
    span = slice(ks[0] * T, last * T)
    to = slice((13 + ks[0]) * T, (13 + last) * T)
    acc[:, to] += jnp.dot(f_ref[here, :].T, gg[:, span], preferred_element_type=jnp.float32)


def weight_inner_kernel(voxels, f_ref, g_ref, nb_ref, acc, xe, shift, gf, gg):
    beside(xe, ROW, f_ref, g_ref, voxels)
    fill_edges(xe, shift)
    acc[...] = jnp.zeros_like(acc)
    rest = (f_ref, g_ref, nb_ref, xe, shift, gf, gg, acc)

    @pl.loop(0, LAYER // CHUNK_W)
    def _(o):
        add_weight_terms(o, list(range(9, 13)), ROW, True, *rest)

    @pl.loop(LAYER // CHUNK_W, voxels // CHUNK_W)
    def _(o):
        add_weight_terms(o, list(range(13)), ROW, True, *rest)


def weight_halo_kernel(scale, f_ref, g_ref, low_ref, nb_ref, in_ref, out_ref, xe, shift, gf, gg, acc):
    xe[ROW : ROW + LAYER, :] = low_ref[...]
    fill_edges(xe, shift)
    acc[...] = in_ref[...]
    rest = (f_ref, g_ref, nb_ref, xe, shift, gf, gg, acc)

    @pl.loop(0, LAYER // CHUNK_W)
    def _(o):
        add_weight_terms(o, list(range(9)), ROW + LAYER, False, *rest)

    for k in range(13):
        out_ref[k * T : (k + 1) * T, :] = (acc[:, k * T : (k + 1) * T].T * scale).astype(out_ref.dtype)
    for k in range(14):
        out_ref[(26 - k) * T : (27 - k) * T, :] = (
            acc[:, (13 + k) * T : (14 + k) * T] * scale
        ).astype(out_ref.dtype)
    if out_ref.shape[0] > 27 * T:
        out_ref[27 * T :, :] = jnp.zeros((out_ref.shape[0] - 27 * T, out_ref.shape[1]), out_ref.dtype)


def weight_scratch(rows, channels):
    return [
        pltpu.VMEM((rows + 2 * ROW, 2 * channels), jnp.bfloat16),
        pltpu.VMEM((32, T), jnp.int32),
        pltpu.VMEM((CHUNK_W, 13 * T), jnp.bfloat16),
        pltpu.VMEM((CHUNK_W, 14 * T), jnp.bfloat16),
    ]


def grad_w_inner(feats, grads, neigh):
    voxels, channels = feats.shape
    return pl.pallas_call(
        functools.partial(weight_inner_kernel, voxels),
        out_shape=jax.ShapeDtypeStruct((channels, 27 * T), jnp.float32),
        in_specs=[VMEM] * 3,
        out_specs=VMEM,
        scratch_shapes=weight_scratch(voxels, channels),
        compiler_params=pltpu.CompilerParams(vmem_limit_bytes=VMEM_LIMIT),
        cost_estimate=pl.CostEstimate(flops=8 * 10**9, bytes_accessed=4 * 10**6, transcendentals=0),
        name="weight_gradient_inner",
    )(feats, grads, neigh)


def grad_w_halo(feats, grads, low, neigh, partial, scale, rows):
    channels = feats.shape[1]
    return pl.pallas_call(
        functools.partial(weight_halo_kernel, scale),
        out_shape=jax.ShapeDtypeStruct((rows, channels), jnp.bfloat16),
        in_specs=[VMEM] * 5,
        out_specs=VMEM,
        scratch_shapes=weight_scratch(LAYER, channels)
        + [pltpu.VMEM((channels, 27 * T), jnp.float32)],
        compiler_params=pltpu.CompilerParams(vmem_limit_bytes=VMEM_LIMIT),
        cost_estimate=pl.CostEstimate(flops=3 * 10**9, bytes_accessed=4 * 10**6, transcendentals=0),
        name="weight_gradient_halo",
    )(feats, grads, low, neigh, partial)


def conv_kernel(voxels, layer, make_wt, f_ref, g_ref, nb_ref, w_hbm, *rest):
    if make_wt:
        conv_ref, gin_ref, wt, xe, nb, w_ref, rel, gf, gg, gf2, gg2, sems = rest[-12:]
    else:
        wt_hbm = rest[0]
        conv_ref, gin_ref, xe, nb, wt, rel, gf, gg, gf2, gg2, sems = rest[-11:]
    halos = list(rest[(0 if make_wt else 3):])
    channels = f_ref.shape[1]
    layers = voxels // LAYER

    first, last = max(layer - 1, 0), min(layer + 1, layers - 1)
    rows = pl.ds(first * LAYER, (last - first + 1) * LAYER)
    to = pl.ds(ROW + (first - layer + 1) * LAYER, (last - first + 1) * LAYER)
    copies = [
        (nb_ref.at[:, pl.ds(layer * (LAYER // T), LAYER // T), :], nb),
        (f_ref.at[rows, :], xe.at[to, pl.ds(0, channels)]),
        (g_ref.at[rows, :], xe.at[to, pl.ds(channels, channels)]),
    ]
    if layer == 0:
        copies.append((halos.pop(0), xe.at[pl.ds(ROW, LAYER), :]))
    if layer == layers - 1:
        copies.append((halos.pop(0), xe.at[pl.ds(ROW + 2 * LAYER, LAYER), :]))
    early = len(copies)
    copies.append((w_hbm, w_ref) if make_wt else (wt_hbm, wt))
    copies = [
        pltpu.make_async_copy(source, target, sems.at[i])
        for i, (source, target) in enumerate(copies)
    ]
    for copy in copies:
        copy.start()
    edge = jnp.zeros((ROW, 2 * channels), jnp.bfloat16)
    xe[0:ROW, :] = edge
    xe[ROW + 3 * LAYER :, :] = edge
    copies[0].wait()
    for k in range(27):
        rel[k, :, :] = row_in_scene_window(nb[k], ROW * offset_of(k)[1])
    for copy in copies[1:early]:
        copy.wait()

    spot = lax.broadcasted_iota(jnp.int32, (T, T), 0).astype(jnp.bfloat16)
    none = jnp.zeros((T, T), jnp.bfloat16)
    buffers = ((gf, gg), (gf2, gg2))

    def hot(tile, k):
        row = jnp.broadcast_to(rel[k, tile : tile + 1, :], (ROW, T)).astype(jnp.bfloat16)
        return one_hot(jnp.concatenate([row] * (T // ROW), axis=0) == spot)

    def gathers(chunk):
        to_f, to_g = buffers[chunk % 2]
        for h in range(CHUNK_C // T):
            tile = chunk * (CHUNK_C // T) + h
            cols = slice(h * T, (h + 1) * T)
            kept = []

            def put(k, part):
                to_f[k * T : (k + 1) * T, cols] = part[:channels]
                to_g[k * T : (k + 1) * T, cols] = part[channels:]

            def put_pair(source, right, pair):
                picked = jnp.dot(source, right, preferred_element_type=jnp.float32)
                picked = picked.astype(jnp.bfloat16)
                put(pair[0], picked[:, :T])
                put(pair[1], picked[:, T:])

            for dz in (-1, 0, 1):
                for dy in (-1, 0, 1):
                    start = tile * T + ROW + ROW * dy + LAYER * (dz + 1)
                    window = xe[start : start + T, :].T
                    first = 9 * (dz + 1) + 3 * (dy + 1)
                    pair = (first, first + 2)
                    right = jnp.concatenate([hot(tile, k) for k in pair], axis=1)
                    put_pair(window, right, pair)
                    if first + 1 == 13:
                        put(13, window)
                    else:
                        kept.append((first + 1, window))
                    if len(kept) == 2:
                        (k0, window0), (k1, window1) = kept
                        right = jnp.concatenate(
                            [
                                jnp.concatenate([hot(tile, k0), none], axis=1),
                                jnp.concatenate([none, hot(tile, k1)], axis=1),
                            ],
                            axis=0,
                        )
                        put_pair(jnp.concatenate([window0, window1], axis=1), right, (k0, k1))
                        kept = []
                    yield

    def product(chunk):
        rows = slice(chunk * CHUNK_C, (chunk + 1) * CHUNK_C)
        kernels = (slice(0, channels), slice(channels, 2 * channels))
        for out, picked, side in zip((conv_ref, gin_ref), buffers[chunk % 2], kernels):
            total = None
            for part in range(3):
                span = slice(part * 9 * T, (part + 1) * 9 * T)
                term = jnp.dot(wt[side, span], picked[span, :], preferred_element_type=jnp.float32)
                total = term if total is None else total + term
                if part == 2:
                    out[rows, :] = total.T.astype(jnp.bfloat16)
                yield

    pending = iter(())
    for chunk in range(LAYER // CHUNK_C):
        for turn, _ in enumerate(gathers(chunk)):
            if turn % 3 == 2:
                next(pending, None)
        for _ in pending:
            pass
        if chunk == 0:
            for copy in copies[early:]:
                copy.wait()
            if make_wt:
                for k in range(27):
                    span = slice(k * T, (k + 1) * T)
                    wt[0:channels, span] = w_ref[span, :].T
                    wt[channels:, span] = w_ref[(26 - k) * T : (27 - k) * T, :]
        pending = product(chunk)
    for _ in pending:
        pass


def conv_layer(feats, grads, low, high, neigh, weight, layer, earlier):
    voxels, channels = feats.shape
    out = jax.ShapeDtypeStruct((voxels, channels), jnp.bfloat16)
    turned = jax.ShapeDtypeStruct((2 * channels, 27 * channels), jnp.bfloat16)
    block = pl.BlockSpec((LAYER, channels), lambda i: (layer, 0))
    make_wt = earlier is None
    operands = [feats, grads, neigh, weight]
    if not make_wt:
        conv_out, grad_in, wt = earlier
        operands += [wt, conv_out, grad_in]
    if layer == 0:
        operands.append(low)
    if layer == voxels // LAYER - 1:
        operands.append(high)
    weights = pltpu.VMEM(weight.shape if make_wt else turned.shape, jnp.bfloat16)
    results = pl.pallas_call(
        functools.partial(conv_kernel, voxels, layer, make_wt),
        grid=(1,),
        out_shape=(out, out) + ((turned,) if make_wt else ()),
        in_specs=[pl.BlockSpec(memory_space=pltpu.HBM)] * len(operands),
        out_specs=(block, block) + ((VMEM,) if make_wt else ()),
        input_output_aliases={} if make_wt else {5: 0, 6: 1},
        scratch_shapes=[
            pltpu.VMEM((2 * ROW + 3 * LAYER, 2 * channels), jnp.bfloat16),
            pltpu.VMEM((27, LAYER // T, T), jnp.int32),
        ]
        + [weights, pltpu.VMEM((27, LAYER // T, T), jnp.int32)]
        + [pltpu.VMEM((27 * T, CHUNK_C), jnp.bfloat16)] * 4
        + [
            pltpu.SemaphoreType.DMA((8,)),
        ],
        compiler_params=pltpu.CompilerParams(vmem_limit_bytes=CONV_VMEM_LIMIT),
        cost_estimate=pl.CostEstimate(flops=10**10, bytes_accessed=6 * 10**6, transcendentals=0),
        name="conv_layer_%d" % layer,
    )(*operands)
    return tuple(results) if make_wt else (results[0], results[1], wt)


def sum_and_spread_kernel(parts_ref, out_ref):
    total = parts_ref[0].astype(jnp.float32)
    for i in range(1, parts_ref.shape[0]):
        total += parts_ref[i].astype(jnp.float32)
    total = total.astype(out_ref.dtype)
    for i in range(out_ref.shape[0]):
        out_ref[i] = total


def sum_and_spread(parts, axis):
    copies = pl.pallas_call(
        sum_and_spread_kernel,
        out_shape=jax.ShapeDtypeStruct((lax.axis_size(axis),) + parts.shape[1:], parts.dtype),
        in_specs=[VMEM],
        out_specs=VMEM,
        compiler_params=pltpu.CompilerParams(vmem_limit_bytes=VMEM_LIMIT),
        name="sum_for_" + axis,
    )(parts)
    return lax.all_to_all(copies, axis, 0, 0, tiled=True)


def widen_kernel(in_ref, out_ref):
    out_ref[...] = in_ref[...].astype(out_ref.dtype)


def widen(rows, count):
    channels = rows.shape[1]
    block = pl.BlockSpec((count // 3, channels), lambda i: (i, 0))
    return pl.pallas_call(
        widen_kernel,
        grid=(3,),
        out_shape=jax.ShapeDtypeStruct((count, channels), jnp.float32),
        in_specs=[block],
        out_specs=block,
        compiler_params=pltpu.CompilerParams(vmem_limit_bytes=VMEM_LIMIT),
        name="widen",
    )(rows)


def local(features, neighbours, weight, grad_out):
    feats, grads = features[0], grad_out[0]
    voxels, channels = feats.shape
    neigh = neighbours.reshape(27, voxels // T, T)
    space, dp = lax.axis_size("space"), lax.axis_size("dp")
    up = [(i, i + 1) for i in range(space - 1)]
    down = [(i + 1, i) for i in range(space - 1)]
    last = jnp.concatenate([feats[voxels - LAYER :], grads[voxels - LAYER :]], axis=1)
    first = jnp.concatenate([feats[:LAYER], grads[:LAYER]], axis=1)
    low = lax.ppermute(last, "space", up)
    high = lax.ppermute(first, "space", down)

    scale = 1.0 / math.sqrt(dp * space * voxels)
    share = -(-27 * channels // (16 * dp)) * 16
    inner = grad_w_inner(feats, grads, neigh)
    partial = grad_w_halo(feats, grads, low, neigh, inner, scale, share * dp)
    partial, flat_weight = lax.optimization_barrier(
        (partial, weight.reshape(27 * channels, channels))
    )
    layers = voxels // LAYER
    order = list(range(1, layers)) + [0]

    def conv(done, count):
        for _ in range(count):
            done = conv_layer(feats, grads, low, high, neigh, flat_weight, order.pop(0), done)
        return done

    pieces = lax.all_to_all(partial.reshape(dp, share, channels), "dp", 0, 0, tiled=True)
    done = conv(None, 1)
    pieces, done = lax.optimization_barrier((pieces, done))
    pieces = sum_and_spread(pieces, "space")
    done = conv(done, 1)
    pieces, done = lax.optimization_barrier((pieces, done))
    whole = sum_and_spread(pieces, "dp")
    conv_out, grad_in, _ = conv(done, len(order))
    grad_w = widen(whole.reshape(dp * share, channels), 27 * channels)
    return conv_out[None], grad_in[None], grad_w.reshape(27, channels, channels)


def solution(mesh):
    in_specs = (P("dp", "space", None), P("dp", None, "space"), P(), P("dp", "space", None))
    out_specs = (P("dp", "space", None), P("dp", "space", None), P())
    return jax.shard_map(local, mesh=mesh, in_specs=in_specs, out_specs=out_specs, check_vma=False)
```

```python
import functools
import math

import jax
import jax.numpy as jnp
from jax import lax
from jax.experimental import pallas as pl
from jax.experimental.pallas import tpu as pltpu
from jax.sharding import PartitionSpec as P

PSIDE = 64
ROW = PSIDE // 4
LAYER = PSIDE * ROW
T = 128
CHUNK_W = 512
CHUNK_C = 256
VMEM_LIMIT = 28 * 1024 * 1024
CONV_VMEM_LIMIT = 58 * 1024 * 1024
VMEM = pl.BlockSpec(memory_space=pltpu.VMEM)
SMEM = pl.BlockSpec(memory_space=pltpu.SMEM)


def offset_of(k):
    return k // 9 - 1, (k // 3) % 3 - 1, k % 3 - 1


def row_in_scene_window(neighbours, shift):
    return jnp.where(neighbours >= 0, (neighbours - shift) & (T - 1), -1)


def one_hot(hit):
    return jnp.where(hit, jnp.ones((), jnp.bfloat16), jnp.zeros((), jnp.bfloat16))


def beside(xe, first, f_ref, g_ref, rows):
    channels = f_ref.shape[1]
    xe[first : first + rows, 0:channels] = f_ref[0:rows, :]
    xe[first : first + rows, channels:] = g_ref[0:rows, :]


def fill_edges(xe, shift):
    edge = jnp.zeros((ROW, xe.shape[1]), jnp.bfloat16)
    xe[0:ROW, :] = edge
    xe[xe.shape[0] - ROW :, :] = edge
    shift[...] = jnp.zeros_like(shift)
    for k in range(27):
        if offset_of(k)[1]:
            shift[k : k + 1, :] = jnp.full((1, T), ROW * offset_of(k)[1], jnp.int32)


def add_weight_terms(o, ks, source, center, f_ref, g_ref, nb_ref, xe, shift, gf, gg, acc):
    channels = f_ref.shape[1]
    spot = lax.broadcasted_iota(jnp.int32, (T, T), 1).astype(jnp.bfloat16)
    base = pl.multiple_of(o * CHUNK_W, CHUNK_W)
    pads = jnp.full((5, T), -1, jnp.int32)
    for h in range(CHUNK_W // T):
        rows = slice(h * T, (h + 1) * T)
        mine = jnp.concatenate([nb_ref[:, o * (CHUNK_W // T) + h, :], pads], axis=0)
        mine = row_in_scene_window(mine, shift[...]).T.astype(jnp.bfloat16)
        for dz, dy in sorted({offset_of(k)[:2] for k in ks}):
            some = [k for k in ks if offset_of(k)[:2] == (dz, dy)]
            start = base + (source + h * T + ROW * dy + LAYER * dz)
            window = xe[pl.ds(pl.multiple_of(start, ROW), T), :]
            hot = jnp.concatenate([one_hot(mine[:, k : k + 1] == spot) for k in some], axis=0)
            picked = jnp.dot(hot, window, preferred_element_type=jnp.float32)
            picked = picked.astype(jnp.bfloat16)
            for q, k in enumerate(some):
                part = picked[q * T : (q + 1) * T]
                gf[rows, k * T : (k + 1) * T] = part[:, :channels]
                gg[rows, k * T : (k + 1) * T] = part[:, channels:]
    here = pl.ds(base, CHUNK_W)
    if center:
        gg[:, 13 * T :] = g_ref[here, :]
    span = slice(ks[0] * T, (ks[-1] + 1) * T)
    acc[:, span] += jnp.dot(g_ref[here, :].T, gf[:, span], preferred_element_type=jnp.float32)
    last = ks[-1] + 1 + (1 if center else 0)
    span = slice(ks[0] * T, last * T)
    to = slice((13 + ks[0]) * T, (13 + last) * T)
    acc[:, to] += jnp.dot(f_ref[here, :].T, gg[:, span], preferred_element_type=jnp.float32)


def weight_inner_kernel(voxels, f_ref, g_ref, nb_ref, acc, xe, shift, gf, gg):
    beside(xe, ROW, f_ref, g_ref, voxels)
    fill_edges(xe, shift)
    acc[...] = jnp.zeros_like(acc)
    rest = (f_ref, g_ref, nb_ref, xe, shift, gf, gg, acc)

    @pl.loop(0, LAYER // CHUNK_W)
    def _(o):
        add_weight_terms(o, list(range(9, 13)), ROW, True, *rest)

    @pl.loop(LAYER // CHUNK_W, voxels // CHUNK_W)
    def _(o):
        add_weight_terms(o, list(range(13)), ROW, True, *rest)


def weight_halo_kernel(scale, parity_ref, f_ref, g_ref, low_ref, nb_ref, in_ref, mine_ref, other_ref, xe, shift, gf, gg, acc, out_ref):
    xe[ROW : ROW + LAYER, :] = low_ref[...]
    fill_edges(xe, shift)
    acc[...] = in_ref[...]
    rest = (f_ref, g_ref, nb_ref, xe, shift, gf, gg, acc)

    @pl.loop(0, LAYER // CHUNK_W)
    def _(o):
        add_weight_terms(o, list(range(9)), ROW + LAYER, False, *rest)

    for k in range(13):
        out_ref[k * T : (k + 1) * T, :] = (acc[:, k * T : (k + 1) * T].T * scale).astype(out_ref.dtype)
    for k in range(14):
        out_ref[(26 - k) * T : (27 - k) * T, :] = (
            acc[:, (13 + k) * T : (14 + k) * T] * scale
        ).astype(out_ref.dtype)
    if out_ref.shape[0] > 27 * T:
        out_ref[27 * T :, :] = jnp.zeros((out_ref.shape[0] - 27 * T, out_ref.shape[1]), out_ref.dtype)
    half = out_ref.shape[0] // 2
    parity = parity_ref[0]
    mine_ref[...] = out_ref[pl.ds(pl.multiple_of(parity * half, 16), half), :]
    other_ref[...] = out_ref[pl.ds(pl.multiple_of((1 - parity) * half, 16), half), :]


def weight_scratch(rows, channels):
    return [
        pltpu.VMEM((rows + 2 * ROW, 2 * channels), jnp.bfloat16),
        pltpu.VMEM((32, T), jnp.int32),
        pltpu.VMEM((CHUNK_W, 13 * T), jnp.bfloat16),
        pltpu.VMEM((CHUNK_W, 14 * T), jnp.bfloat16),
    ]


def grad_w_inner(feats, grads, neigh):
    voxels, channels = feats.shape
    return pl.pallas_call(
        functools.partial(weight_inner_kernel, voxels),
        out_shape=jax.ShapeDtypeStruct((channels, 27 * T), jnp.float32),
        in_specs=[VMEM] * 3,
        out_specs=VMEM,
        scratch_shapes=weight_scratch(voxels, channels),
        compiler_params=pltpu.CompilerParams(vmem_limit_bytes=VMEM_LIMIT),
        cost_estimate=pl.CostEstimate(flops=8 * 10**9, bytes_accessed=4 * 10**6, transcendentals=0),
        name="weight_gradient_inner",
    )(feats, grads, neigh)


def grad_w_halo(feats, grads, low, neigh, partial, parity, scale, rows):
    channels = feats.shape[1]
    out = jax.ShapeDtypeStruct((rows // 2, channels), jnp.bfloat16)
    return pl.pallas_call(
        functools.partial(weight_halo_kernel, scale),
        out_shape=(out, out),
        in_specs=[SMEM] + [VMEM] * 5,
        out_specs=(VMEM, VMEM),
        scratch_shapes=weight_scratch(LAYER, channels)
        + [
            pltpu.VMEM((channels, 27 * T), jnp.float32),
            pltpu.VMEM((rows, channels), jnp.bfloat16),
        ],
        compiler_params=pltpu.CompilerParams(vmem_limit_bytes=VMEM_LIMIT),
        cost_estimate=pl.CostEstimate(flops=3 * 10**9, bytes_accessed=4 * 10**6, transcendentals=0),
        name="weight_gradient_halo",
    )(parity, feats, grads, low, neigh, partial)


def stack_kernel(voxels, f_ref, g_ref, last_ref, first_ref, sems):
    channels = f_ref.shape[1]
    copies = []
    for out, start in ((last_ref, voxels - LAYER), (first_ref, 0)):
        for ref, lane in ((f_ref, 0), (g_ref, channels)):
            copies.append(
                pltpu.make_async_copy(
                    ref.at[pl.ds(start, LAYER), :],
                    out.at[:, pl.ds(lane, channels)],
                    sems.at[len(copies)],
                )
            )
    for copy in copies:
        copy.start()
    for copy in copies:
        copy.wait()


def stack_edges(feats, grads):
    voxels, channels = feats.shape
    out = jax.ShapeDtypeStruct((LAYER, 2 * channels), jnp.bfloat16)
    return pl.pallas_call(
        functools.partial(stack_kernel, voxels),
        out_shape=(out, out),
        in_specs=[pl.BlockSpec(memory_space=pltpu.HBM)] * 2,
        out_specs=(pl.BlockSpec(memory_space=pltpu.HBM),) * 2,
        scratch_shapes=[pltpu.SemaphoreType.DMA((4,))],
        name="stack_edges",
    )(feats, grads)


def conv_kernel(voxels, layer, make_wt, f_ref, g_ref, nb_ref, w_hbm, *rest):
    if make_wt:
        conv_ref, gin_ref, wt, xe, nb, w_ref, rel, gf, gg, gf2, gg2, sems = rest[-12:]
    else:
        wt_hbm = rest[0]
        conv_ref, gin_ref, xe, nb, wt, rel, gf, gg, gf2, gg2, sems = rest[-11:]
    halos = list(rest[(0 if make_wt else 3):])
    channels = f_ref.shape[1]
    layers = voxels // LAYER

    first, last = max(layer - 1, 0), min(layer + 1, layers - 1)
    rows = pl.ds(first * LAYER, (last - first + 1) * LAYER)
    to = pl.ds(ROW + (first - layer + 1) * LAYER, (last - first + 1) * LAYER)
    copies = [
        (nb_ref.at[:, pl.ds(layer * (LAYER // T), LAYER // T), :], nb),
        (f_ref.at[rows, :], xe.at[to, pl.ds(0, channels)]),
        (g_ref.at[rows, :], xe.at[to, pl.ds(channels, channels)]),
    ]
    if layer == 0:
        copies.append((halos.pop(0), xe.at[pl.ds(ROW, LAYER), :]))
    if layer == layers - 1:
        copies.append((halos.pop(0), xe.at[pl.ds(ROW + 2 * LAYER, LAYER), :]))
    early = len(copies)
    copies.append((w_hbm, w_ref) if make_wt else (wt_hbm, wt))
    copies = [
        pltpu.make_async_copy(source, target, sems.at[i])
        for i, (source, target) in enumerate(copies)
    ]
    for copy in copies:
        copy.start()
    edge = jnp.zeros((ROW, 2 * channels), jnp.bfloat16)
    xe[0:ROW, :] = edge
    xe[ROW + 3 * LAYER :, :] = edge
    copies[0].wait()
    for k in range(27):
        rel[k, :, :] = row_in_scene_window(nb[k], ROW * offset_of(k)[1])
    for copy in copies[1:early]:
        copy.wait()

    spot = lax.broadcasted_iota(jnp.int32, (T, T), 0).astype(jnp.bfloat16)
    none = jnp.zeros((T, T), jnp.bfloat16)
    buffers = ((gf, gg), (gf2, gg2))

    def hot(tile, k):
        row = jnp.broadcast_to(rel[k, tile : tile + 1, :], (ROW, T)).astype(jnp.bfloat16)
        return one_hot(jnp.concatenate([row] * (T // ROW), axis=0) == spot)

    def gathers(chunk):
        to_f, to_g = buffers[chunk % 2]
        for h in range(CHUNK_C // T):
            tile = chunk * (CHUNK_C // T) + h
            cols = slice(h * T, (h + 1) * T)
            kept = []

            def put(k, part):
                to_f[k * T : (k + 1) * T, cols] = part[:channels]
                to_g[k * T : (k + 1) * T, cols] = part[channels:]

            def put_pair(source, right, pair):
                picked = jnp.dot(source, right, preferred_element_type=jnp.float32)
                picked = picked.astype(jnp.bfloat16)
                put(pair[0], picked[:, :T])
                put(pair[1], picked[:, T:])

            for dz in (-1, 0, 1):
                for dy in (-1, 0, 1):
                    start = tile * T + ROW + ROW * dy + LAYER * (dz + 1)
                    window = xe[start : start + T, :].T
                    first = 9 * (dz + 1) + 3 * (dy + 1)
                    pair = (first, first + 2)
                    right = jnp.concatenate([hot(tile, k) for k in pair], axis=1)
                    put_pair(window, right, pair)
                    if first + 1 == 13:
                        put(13, window)
                    else:
                        kept.append((first + 1, window))
                    if len(kept) == 2:
                        (k0, window0), (k1, window1) = kept
                        right = jnp.concatenate(
                            [
                                jnp.concatenate([hot(tile, k0), none], axis=1),
                                jnp.concatenate([none, hot(tile, k1)], axis=1),
                            ],
                            axis=0,
                        )
                        put_pair(jnp.concatenate([window0, window1], axis=1), right, (k0, k1))
                        kept = []
                    yield

    def product(chunk):
        rows = slice(chunk * CHUNK_C, (chunk + 1) * CHUNK_C)
        kernels = (slice(0, channels), slice(channels, 2 * channels))
        for out, picked, side in zip((conv_ref, gin_ref), buffers[chunk % 2], kernels):
            total = None
            for part in range(3):
                span = slice(part * 9 * T, (part + 1) * 9 * T)
                term = jnp.dot(wt[side, span], picked[span, :], preferred_element_type=jnp.float32)
                total = term if total is None else total + term
                if part == 2:
                    out[rows, :] = total.T.astype(jnp.bfloat16)
                yield

    pending = iter(())
    for chunk in range(LAYER // CHUNK_C):
        for turn, _ in enumerate(gathers(chunk)):
            if turn % 3 == 2:
                next(pending, None)
        for _ in pending:
            pass
        if chunk == 0:
            for copy in copies[early:]:
                copy.wait()
            if make_wt:
                for k in range(27):
                    span = slice(k * T, (k + 1) * T)
                    wt[0:channels, span] = w_ref[span, :].T
                    wt[channels:, span] = w_ref[(26 - k) * T : (27 - k) * T, :]
        pending = product(chunk)
    for _ in pending:
        pass


def conv_layer(feats, grads, low, high, neigh, weight, layer, earlier):
    voxels, channels = feats.shape
    out = jax.ShapeDtypeStruct((voxels, channels), jnp.bfloat16)
    turned = jax.ShapeDtypeStruct((2 * channels, 27 * channels), jnp.bfloat16)
    block = pl.BlockSpec((LAYER, channels), lambda i: (layer, 0))
    make_wt = earlier is None
    operands = [feats, grads, neigh, weight]
    if not make_wt:
        conv_out, grad_in, wt = earlier
        operands += [wt, conv_out, grad_in]
    if layer == 0:
        operands.append(low)
    if layer == voxels // LAYER - 1:
        operands.append(high)
    weights = pltpu.VMEM(weight.shape if make_wt else turned.shape, jnp.bfloat16)
    results = pl.pallas_call(
        functools.partial(conv_kernel, voxels, layer, make_wt),
        grid=(1,),
        out_shape=(out, out) + ((turned,) if make_wt else ()),
        in_specs=[pl.BlockSpec(memory_space=pltpu.HBM)] * len(operands),
        out_specs=(block, block) + ((VMEM,) if make_wt else ()),
        input_output_aliases={} if make_wt else {5: 0, 6: 1},
        scratch_shapes=[
            pltpu.VMEM((2 * ROW + 3 * LAYER, 2 * channels), jnp.bfloat16),
            pltpu.VMEM((27, LAYER // T, T), jnp.int32),
        ]
        + [weights, pltpu.VMEM((27, LAYER // T, T), jnp.int32)]
        + [pltpu.VMEM((27 * T, CHUNK_C), jnp.bfloat16)] * 4
        + [
            pltpu.SemaphoreType.DMA((8,)),
        ],
        compiler_params=pltpu.CompilerParams(vmem_limit_bytes=CONV_VMEM_LIMIT),
        cost_estimate=pl.CostEstimate(flops=10**10, bytes_accessed=6 * 10**6, transcendentals=0),
        name="conv_layer_%d" % layer,
    )(*operands)
    return tuple(results) if make_wt else (results[0], results[1], wt)


def sum_kernel(*refs):
    *parts, out_ref = refs
    terms = [ref[i] for ref in parts for i in range(ref.shape[0])]
    total = terms[0].astype(jnp.float32)
    for term in terms[1:]:
        total += term.astype(jnp.float32)
    total = total.astype(out_ref.dtype)
    for i in range(out_ref.shape[0]):
        out_ref[i] = total


def sum_parts(parts, copies, name):
    shape = parts[0].shape[1:]
    return pl.pallas_call(
        sum_kernel,
        out_shape=jax.ShapeDtypeStruct((copies,) + shape, parts[0].dtype),
        in_specs=[VMEM] * len(parts),
        out_specs=VMEM,
        compiler_params=pltpu.CompilerParams(vmem_limit_bytes=VMEM_LIMIT),
        name=name,
    )(*parts)


def widen_kernel(side_ref, in_ref, *rest):
    out_ref = rest[-1]
    out_ref[...] = in_ref[...].astype(out_ref.dtype)


def widen(rows, side, count, earlier, name):
    half, channels = rows.shape
    block = (half // 2, channels)
    return pl.pallas_call(
        widen_kernel,
        grid_spec=pltpu.PrefetchScalarGridSpec(
            num_scalar_prefetch=1,
            grid=(2,),
            in_specs=[pl.BlockSpec(block, lambda i, side: (i, 0))]
            + [pl.BlockSpec(memory_space=pl.ANY)] * len(earlier),
            out_specs=pl.BlockSpec(block, lambda i, side: (side[0] * 2 + i, 0)),
        ),
        out_shape=jax.ShapeDtypeStruct((count, channels), jnp.float32),
        input_output_aliases={2 + i: i for i in range(len(earlier))},
        compiler_params=pltpu.CompilerParams(vmem_limit_bytes=VMEM_LIMIT),
        name=name,
    )(side, rows, *earlier)


def local(features, neighbours, weight, grad_out):
    feats, grads = features[0], grad_out[0]
    voxels, channels = feats.shape
    neigh = neighbours.reshape(27, voxels // T, T)
    space, dp = lax.axis_size("space"), lax.axis_size("dp")
    up = [(i, i + 1) for i in range(space - 1)]
    down = [(i + 1, i) for i in range(space - 1)]
    last, first = stack_edges(feats, grads)
    low = lax.ppermute(last, "space", up)
    high = lax.ppermute(first, "space", down)

    scale = 1.0 / math.sqrt(dp * space * voxels)
    share = -(-27 * channels // (16 * dp)) * 16
    parity = (lax.axis_index("dp") % 2).astype(jnp.int32).reshape(1)
    inner = grad_w_inner(feats, grads, neigh)
    mine, other = grad_w_halo(feats, grads, low, neigh, inner, parity, scale, share * dp)
    swap = [(i, i ^ 1) for i in range(dp)]
    alike = [list(range(0, dp, 2)), list(range(1, dp, 2))]
    other = lax.ppermute(other, "dp", swap)
    mine = sum_parts((mine[None], other[None]), 1, "sum_of_pair")
    mine, flat_weight = lax.optimization_barrier(
        (mine, weight.reshape(27 * channels, channels))
    )
    layers = voxels // LAYER
    order = list(range(1, layers)) + [0]

    def conv(done, count):
        for _ in range(count):
            done = conv_layer(feats, grads, low, high, neigh, flat_weight, order.pop(0), done)
        return done

    def exchange(pieces):
        return lax.all_to_all(pieces, "dp", 0, 0, axis_index_groups=alike, tiled=True)

    pieces = exchange(mine.reshape(dp // 2, share, channels))
    done = conv(None, 1)
    pieces, done = lax.optimization_barrier((pieces, done))
    pieces = lax.all_to_all(sum_parts((pieces,), space, "sum_for_space"), "space", 0, 0, tiled=True)
    done = conv(done, 1)
    pieces, done = lax.optimization_barrier((pieces, done))
    pieces = exchange(sum_parts((pieces,), dp // 2, "sum_for_dp"))
    done = conv(done, len(order))
    pieces, done = lax.optimization_barrier((pieces, done))
    mine = pieces.reshape(dp // 2 * share, channels)
    other = lax.ppermute(mine, "dp", swap)
    grad_w = widen(mine, parity, 27 * channels, (), "widen_own_half")
    grad_w = widen(other, 1 - parity, 27 * channels, (grad_w,), "widen_other_half")
    conv_out, grad_in, _ = done
    return conv_out[None], grad_in[None], grad_w.reshape(27, channels, channels)


def solution(mesh):
    in_specs = (P("dp", "space", None), P("dp", None, "space"), P(), P("dp", "space", None))
    out_specs = (P("dp", "space", None), P("dp", "space", None), P())
    return jax.shard_map(local, mesh=mesh, in_specs=in_specs, out_specs=out_specs, check_vma=False)
```

```python
import functools
import math

import jax
import jax.numpy as jnp
from jax import lax
from jax.experimental import pallas as pl
from jax.experimental.pallas import tpu as pltpu
from jax.sharding import PartitionSpec as P

PSIDE = 64
ROW = PSIDE // 4
LAYER = PSIDE * ROW
T = 128
CHUNK_W = 512
CHUNK_C = 256
VMEM_LIMIT = 28 * 1024 * 1024
CONV_VMEM_LIMIT = 58 * 1024 * 1024
VMEM = pl.BlockSpec(memory_space=pltpu.VMEM)
SMEM = pl.BlockSpec(memory_space=pltpu.SMEM)


def offset_of(k):
    return k // 9 - 1, (k // 3) % 3 - 1, k % 3 - 1


def row_in_scene_window(neighbours, shift):
    return jnp.where(neighbours >= 0, (neighbours - shift) & (T - 1), -1)


def one_hot(hit):
    return jnp.where(hit, jnp.ones((), jnp.bfloat16), jnp.zeros((), jnp.bfloat16))


def beside(xe, first, f_ref, g_ref, rows):
    channels = f_ref.shape[1]
    xe[first : first + rows, 0:channels] = f_ref[0:rows, :]
    xe[first : first + rows, channels:] = g_ref[0:rows, :]


def fill_edges(xe, shift):
    edge = jnp.zeros((ROW, xe.shape[1]), jnp.bfloat16)
    xe[0:ROW, :] = edge
    xe[xe.shape[0] - ROW :, :] = edge
    shift[...] = jnp.zeros_like(shift)
    for k in range(27):
        if offset_of(k)[1]:
            shift[k : k + 1, :] = jnp.full((1, T), ROW * offset_of(k)[1], jnp.int32)


def add_weight_terms(o, ks, source, center, f_ref, g_ref, nb_ref, xe, shift, gf, gg, acc):
    channels = f_ref.shape[1]
    spot = lax.broadcasted_iota(jnp.int32, (T, T), 1).astype(jnp.bfloat16)
    base = pl.multiple_of(o * CHUNK_W, CHUNK_W)
    pads = jnp.full((5, T), -1, jnp.int32)
    for h in range(CHUNK_W // T):
        rows = slice(h * T, (h + 1) * T)
        mine = jnp.concatenate([nb_ref[:, o * (CHUNK_W // T) + h, :], pads], axis=0)
        mine = row_in_scene_window(mine, shift[...]).T.astype(jnp.bfloat16)
        for dz, dy in sorted({offset_of(k)[:2] for k in ks}):
            some = [k for k in ks if offset_of(k)[:2] == (dz, dy)]
            start = base + (source + h * T + ROW * dy + LAYER * dz)
            window = xe[pl.ds(pl.multiple_of(start, ROW), T), :]
            hot = jnp.concatenate([one_hot(mine[:, k : k + 1] == spot) for k in some], axis=0)
            picked = jnp.dot(hot, window, preferred_element_type=jnp.float32)
            picked = picked.astype(jnp.bfloat16)
            for q, k in enumerate(some):
                part = picked[q * T : (q + 1) * T]
                gf[rows, k * T : (k + 1) * T] = part[:, :channels]
                gg[rows, k * T : (k + 1) * T] = part[:, channels:]
    here = pl.ds(base, CHUNK_W)
    if center:
        gg[:, 13 * T :] = g_ref[here, :]
    span = slice(ks[0] * T, (ks[-1] + 1) * T)
    acc[:, span] += jnp.dot(g_ref[here, :].T, gf[:, span], preferred_element_type=jnp.float32)
    last = ks[-1] + 1 + (1 if center else 0)
    span = slice(ks[0] * T, last * T)
    to = slice((13 + ks[0]) * T, (13 + last) * T)
    acc[:, to] += jnp.dot(f_ref[here, :].T, gg[:, span], preferred_element_type=jnp.float32)


def weight_inner_kernel(voxels, f_ref, g_ref, nb_ref, acc, xe, shift, gf, gg):
    beside(xe, ROW, f_ref, g_ref, voxels)
    fill_edges(xe, shift)
    acc[...] = jnp.zeros_like(acc)
    rest = (f_ref, g_ref, nb_ref, xe, shift, gf, gg, acc)

    @pl.loop(0, LAYER // CHUNK_W)
    def _(o):
        add_weight_terms(o, list(range(9, 13)), ROW, True, *rest)

    @pl.loop(LAYER // CHUNK_W, voxels // CHUNK_W)
    def _(o):
        add_weight_terms(o, list(range(13)), ROW, True, *rest)


def weight_halo_kernel(scale, parity_ref, f_ref, g_ref, low_ref, nb_ref, in_ref, mine_ref, other_ref, xe, shift, gf, gg, acc, out_ref):
    xe[ROW : ROW + LAYER, :] = low_ref[...]
    fill_edges(xe, shift)
    acc[...] = in_ref[...]
    rest = (f_ref, g_ref, nb_ref, xe, shift, gf, gg, acc)

    @pl.loop(0, LAYER // CHUNK_W)
    def _(o):
        add_weight_terms(o, list(range(9)), ROW + LAYER, False, *rest)

    for k in range(13):
        out_ref[k * T : (k + 1) * T, :] = (acc[:, k * T : (k + 1) * T].T * scale).astype(out_ref.dtype)
    for k in range(14):
        out_ref[(26 - k) * T : (27 - k) * T, :] = (
            acc[:, (13 + k) * T : (14 + k) * T] * scale
        ).astype(out_ref.dtype)
    if out_ref.shape[0] > 27 * T:
        out_ref[27 * T :, :] = jnp.zeros((out_ref.shape[0] - 27 * T, out_ref.shape[1]), out_ref.dtype)
    half = out_ref.shape[0] // 2
    parity = parity_ref[0]
    mine_ref[...] = out_ref[pl.ds(pl.multiple_of(parity * half, 16), half), :]
    other_ref[...] = out_ref[pl.ds(pl.multiple_of((1 - parity) * half, 16), half), :]


def weight_scratch(rows, channels):
    return [
        pltpu.VMEM((rows + 2 * ROW, 2 * channels), jnp.bfloat16),
        pltpu.VMEM((32, T), jnp.int32),
        pltpu.VMEM((CHUNK_W, 13 * T), jnp.bfloat16),
        pltpu.VMEM((CHUNK_W, 14 * T), jnp.bfloat16),
    ]


def grad_w_inner(feats, grads, neigh):
    voxels, channels = feats.shape
    return pl.pallas_call(
        functools.partial(weight_inner_kernel, voxels),
        out_shape=jax.ShapeDtypeStruct((channels, 27 * T), jnp.float32),
        in_specs=[VMEM] * 3,
        out_specs=VMEM,
        scratch_shapes=weight_scratch(voxels, channels),
        compiler_params=pltpu.CompilerParams(vmem_limit_bytes=VMEM_LIMIT),
        cost_estimate=pl.CostEstimate(flops=8 * 10**9, bytes_accessed=4 * 10**6, transcendentals=0),
        name="weight_gradient_inner",
    )(feats, grads, neigh)


def grad_w_halo(feats, grads, low, neigh, partial, parity, scale, rows):
    channels = feats.shape[1]
    out = jax.ShapeDtypeStruct((rows // 2, channels), jnp.bfloat16)
    return pl.pallas_call(
        functools.partial(weight_halo_kernel, scale),
        out_shape=(out, out),
        in_specs=[SMEM] + [VMEM] * 5,
        out_specs=(VMEM, VMEM),
        scratch_shapes=weight_scratch(LAYER, channels)
        + [
            pltpu.VMEM((channels, 27 * T), jnp.float32),
            pltpu.VMEM((rows, channels), jnp.bfloat16),
        ],
        compiler_params=pltpu.CompilerParams(vmem_limit_bytes=VMEM_LIMIT),
        cost_estimate=pl.CostEstimate(flops=3 * 10**9, bytes_accessed=4 * 10**6, transcendentals=0),
        name="weight_gradient_halo",
    )(parity, feats, grads, low, neigh, partial)


def rows_needed(run):
    first, end = run
    return (
        first - LAYER - (ROW if first % LAYER else 0),
        end + LAYER + (ROW if end % LAYER else 0),
    )


def conv_kernel(voxels, run, make_wt, f_ref, g_ref, nb_ref, w_hbm, *rest):
    if make_wt:
        conv_hbm, gin_hbm, wt, w_ref, *scratch = rest[-14:]
    else:
        wt_hbm = rest[0]
        conv_hbm, gin_hbm, wt, *scratch = rest[-13:]
    conv_ref, gin_ref, xe, nb, rel, gf, gg, gf2, gg2, sems = scratch
    halos = list(rest[(0 if make_wt else 3) :])
    channels = f_ref.shape[1]
    size = run[1] - run[0]

    origin = run[0] - LAYER - ROW
    low, high = rows_needed(run)
    main = (max(low, 0), min(high, voxels))
    rows = pl.ds(main[0], main[1] - main[0])
    to = pl.ds(main[0] - origin, main[1] - main[0])
    copies = [
        (nb_ref, nb),
        (f_ref.at[rows, :], xe.at[to, pl.ds(0, channels)]),
        (g_ref.at[rows, :], xe.at[to, pl.ds(channels, channels)]),
    ]
    if low < 0:
        copies.append(
            (halos.pop(0).at[pl.ds(LAYER + low, -low), :], xe.at[pl.ds(low - origin, -low), :])
        )
    if high > voxels:
        copies.append(
            (
                halos.pop(0).at[pl.ds(0, high - voxels), :],
                xe.at[pl.ds(voxels - origin, high - voxels), :],
            )
        )
    early = len(copies)
    copies.append((w_hbm, w_ref) if make_wt else (wt_hbm, wt))
    copies = [
        pltpu.make_async_copy(source, target, sems.at[i])
        for i, (source, target) in enumerate(copies)
    ]
    for copy in copies:
        copy.start()
    edge = jnp.zeros((ROW, 2 * channels), jnp.bfloat16)
    if low - origin:
        xe[0:ROW, :] = edge
    if high - origin < xe.shape[0]:
        xe[xe.shape[0] - ROW :, :] = edge
    copies[0].wait()
    for k in range(27):
        rel[k, :, :] = row_in_scene_window(nb[k], ROW * offset_of(k)[1])
    first_tile = run[0] // T
    for copy in copies[1:early]:
        copy.wait()

    spot = lax.broadcasted_iota(jnp.int32, (T, T), 0).astype(jnp.bfloat16)
    none = jnp.zeros((T, T), jnp.bfloat16)
    buffers = ((gf, gg), (gf2, gg2))

    def hot(tile, k):
        row = rel[k, first_tile + tile : first_tile + tile + 1, :]
        row = jnp.broadcast_to(row, (ROW, T)).astype(jnp.bfloat16)
        return one_hot(jnp.concatenate([row] * (T // ROW), axis=0) == spot)

    def gathers(chunk):
        to_f, to_g = buffers[chunk % 2]
        for h in range(CHUNK_C // T):
            tile = chunk * (CHUNK_C // T) + h
            cols = slice(h * T, (h + 1) * T)
            kept = []

            def put(k, part):
                to_f[k * T : (k + 1) * T, cols] = part[:channels]
                to_g[k * T : (k + 1) * T, cols] = part[channels:]

            def put_pair(source, right, pair):
                picked = jnp.dot(source, right, preferred_element_type=jnp.float32)
                picked = picked.astype(jnp.bfloat16)
                put(pair[0], picked[:, :T])
                put(pair[1], picked[:, T:])

            for dz in (-1, 0, 1):
                for dy in (-1, 0, 1):
                    start = tile * T + ROW + ROW * dy + LAYER * (dz + 1)
                    window = xe[start : start + T, :].T
                    first = 9 * (dz + 1) + 3 * (dy + 1)
                    pair = (first, first + 2)
                    right = jnp.concatenate([hot(tile, k) for k in pair], axis=1)
                    put_pair(window, right, pair)
                    if first + 1 == 13:
                        put(13, window)
                    else:
                        kept.append((first + 1, window))
                    if len(kept) == 2:
                        (k0, window0), (k1, window1) = kept
                        right = jnp.concatenate(
                            [
                                jnp.concatenate([hot(tile, k0), none], axis=1),
                                jnp.concatenate([none, hot(tile, k1)], axis=1),
                            ],
                            axis=0,
                        )
                        put_pair(jnp.concatenate([window0, window1], axis=1), right, (k0, k1))
                        kept = []
                    yield

    def product(chunk):
        rows = slice(chunk * CHUNK_C, (chunk + 1) * CHUNK_C)
        kernels = (slice(0, channels), slice(channels, 2 * channels))
        outs = ((conv_ref, conv_hbm), (gin_ref, gin_hbm))
        for (out, out_hbm), picked, side in zip(outs, buffers[chunk % 2], kernels):
            total = None
            for part in range(3):
                span = slice(part * 9 * T, (part + 1) * 9 * T)
                term = jnp.dot(wt[side, span], picked[span, :], preferred_element_type=jnp.float32)
                total = term if total is None else total + term
                if part == 2:
                    out[rows, :] = total.T.astype(jnp.bfloat16)
                    copy = pltpu.make_async_copy(
                        out.at[rows, :],
                        out_hbm.at[pl.ds(run[0] + chunk * CHUNK_C, CHUNK_C), :],
                        sems.at[len(copies) + len(written)],
                    )
                    copy.start()
                    written.append(copy)
                yield

    written = []
    pending = iter(())
    for chunk in range(size // CHUNK_C):
        for turn, _ in enumerate(gathers(chunk)):
            if turn % 3 == 2:
                next(pending, None)
        for _ in pending:
            pass
        if chunk == 0:
            for copy in copies[early:]:
                copy.wait()
            if make_wt:
                for k in range(27):
                    span = slice(k * T, (k + 1) * T)
                    wt[0:channels, span] = w_ref[span, :].T
                    wt[channels:, span] = w_ref[(26 - k) * T : (27 - k) * T, :]
        pending = product(chunk)
    for _ in pending:
        pass
    for copy in written:
        copy.wait()


def conv_run(feats, grads, low, high, neigh, weight, run, earlier, name):
    voxels, channels = feats.shape
    out = jax.ShapeDtypeStruct((voxels, channels), jnp.bfloat16)
    turned = jax.ShapeDtypeStruct((2 * channels, 27 * channels), jnp.bfloat16)
    make_wt = earlier is None
    operands = [feats, grads, neigh, weight]
    if not make_wt:
        conv_out, grad_in, wt = earlier
        operands += [wt, conv_out, grad_in]
    first, end = rows_needed(run)
    if first < 0:
        operands.append(low)
    if end > voxels:
        operands.append(high)
    hbm = pl.BlockSpec(memory_space=pltpu.HBM)
    size = run[1] - run[0]
    results = pl.pallas_call(
        functools.partial(conv_kernel, voxels, run, make_wt),
        out_shape=(out, out) + ((turned,) if make_wt else ()),
        in_specs=[hbm] * len(operands),
        out_specs=(hbm, hbm) + ((VMEM,) if make_wt else ()),
        input_output_aliases={} if make_wt else {5: 0, 6: 1},
        scratch_shapes=[
            pltpu.VMEM(weight.shape if make_wt else turned.shape, jnp.bfloat16),
            pltpu.VMEM((size, channels), jnp.bfloat16),
            pltpu.VMEM((size, channels), jnp.bfloat16),
            pltpu.VMEM((size + 2 * (LAYER + ROW), 2 * channels), jnp.bfloat16),
            pltpu.VMEM(neigh.shape, jnp.int32),
            pltpu.VMEM(neigh.shape, jnp.int32),
        ]
        + [pltpu.VMEM((27 * T, CHUNK_C), jnp.bfloat16)] * 4
        + [pltpu.SemaphoreType.DMA((8 + 2 * size // CHUNK_C,))],
        compiler_params=pltpu.CompilerParams(vmem_limit_bytes=CONV_VMEM_LIMIT),
        cost_estimate=pl.CostEstimate(flops=10**10, bytes_accessed=6 * 10**6, transcendentals=0),
        name=name,
    )(*operands)
    return tuple(results) if make_wt else (results[0], results[1], wt)


def sum_kernel(*refs):
    *parts, out_ref = refs
    terms = [ref[i] for ref in parts for i in range(ref.shape[0])]
    total = terms[0].astype(jnp.float32)
    for term in terms[1:]:
        total += term.astype(jnp.float32)
    total = total.astype(out_ref.dtype)
    for i in range(out_ref.shape[0]):
        out_ref[i] = total


def sum_parts(parts, copies, name):
    shape = parts[0].shape[1:]
    return pl.pallas_call(
        sum_kernel,
        out_shape=jax.ShapeDtypeStruct((copies,) + shape, parts[0].dtype),
        in_specs=[VMEM] * len(parts),
        out_specs=VMEM,
        compiler_params=pltpu.CompilerParams(vmem_limit_bytes=VMEM_LIMIT),
        name=name,
    )(*parts)


def widen_kernel(side_ref, in_ref, *rest):
    out_ref = rest[-1]
    out_ref[...] = in_ref[...].astype(out_ref.dtype)


def widen(rows, side, count, earlier, name):
    half, channels = rows.shape
    block = (half // 2, channels)
    return pl.pallas_call(
        widen_kernel,
        grid_spec=pltpu.PrefetchScalarGridSpec(
            num_scalar_prefetch=1,
            grid=(2,),
            in_specs=[pl.BlockSpec(block, lambda i, side: (i, 0))]
            + [pl.BlockSpec(memory_space=pl.ANY)] * len(earlier),
            out_specs=pl.BlockSpec(block, lambda i, side: (side[0] * 2 + i, 0)),
        ),
        out_shape=jax.ShapeDtypeStruct((count, channels), jnp.float32),
        input_output_aliases={2 + i: i for i in range(len(earlier))},
        compiler_params=pltpu.CompilerParams(vmem_limit_bytes=VMEM_LIMIT),
        name=name,
    )(side, rows, *earlier)


def local(features, neighbours, weight, grad_out):
    feats, grads = features[0], grad_out[0]
    voxels, channels = feats.shape
    neigh = neighbours.reshape(27, voxels // T, T)
    space, dp = lax.axis_size("space"), lax.axis_size("dp")
    up = [(i, i + 1) for i in range(space - 1)]
    down = [(i + 1, i) for i in range(space - 1)]
    last = jnp.concatenate([feats[voxels - LAYER :], grads[voxels - LAYER :]], axis=1)
    first = jnp.concatenate([feats[:LAYER], grads[:LAYER]], axis=1)
    low = lax.ppermute(last, "space", up)
    high = lax.ppermute(first, "space", down)

    scale = 1.0 / math.sqrt(dp * space * voxels)
    share = -(-27 * channels // (16 * dp)) * 16
    parity = (lax.axis_index("dp") % 2).astype(jnp.int32).reshape(1)
    inner = grad_w_inner(feats, grads, neigh)
    mine, other = grad_w_halo(feats, grads, low, neigh, inner, parity, scale, share * dp)
    swap = [(i, i ^ 1) for i in range(dp)]
    alike = [list(range(0, dp, 2)), list(range(1, dp, 2))]
    other = lax.ppermute(other, "dp", swap)
    mine = sum_parts((mine[None], other[None]), 1, "sum_of_pair")
    mine, flat_weight = lax.optimization_barrier(
        (mine, weight.reshape(27 * channels, channels))
    )
    chunks = voxels // CHUNK_C
    ends = [0, chunks // 4 * CHUNK_C, chunks * 2 // 3 * CHUNK_C, voxels]

    def conv(done, part):
        run = (ends[part], ends[part + 1])
        name = "conv_run_%d" % part
        return conv_run(feats, grads, low, high, neigh, flat_weight, run, done, name)

    def exchange(pieces):
        return lax.all_to_all(pieces, "dp", 0, 0, axis_index_groups=alike, tiled=True)

    pieces = exchange(mine.reshape(dp // 2, share, channels))
    done = conv(None, 0)
    pieces, done, high = lax.optimization_barrier((pieces, done, high))
    pieces = lax.all_to_all(sum_parts((pieces,), space, "sum_for_space"), "space", 0, 0, tiled=True)
    done = conv(done, 1)
    pieces, done = lax.optimization_barrier((pieces, done))
    pieces = exchange(sum_parts((pieces,), dp // 2, "sum_for_dp"))
    done = conv(done, 2)
    pieces, done = lax.optimization_barrier((pieces, done))
    mine = pieces.reshape(dp // 2 * share, channels)
    other = lax.ppermute(mine, "dp", swap)
    grad_w = widen(mine, parity, 27 * channels, (), "widen_own_half")
    grad_w = widen(other, 1 - parity, 27 * channels, (grad_w,), "widen_other_half")
    conv_out, grad_in, _ = done
    return conv_out[None], grad_in[None], grad_w.reshape(27, channels, channels)


def solution(mesh):
    in_specs = (P("dp", "space", None), P("dp", None, "space"), P(), P("dp", "space", None))
    out_specs = (P("dp", "space", None), P("dp", "space", None), P())
    return jax.shard_map(local, mesh=mesh, in_specs=in_specs, out_specs=out_specs, check_vma=False)
```

```python
import functools
import math

import jax
import jax.numpy as jnp
from jax import lax
from jax.experimental import pallas as pl
from jax.experimental.pallas import tpu as pltpu
from jax.sharding import PartitionSpec as P

PSIDE = 64
ROW = PSIDE // 4
LAYER = PSIDE * ROW
T = 128
CHUNK_W = 256
CHUNK_C = 256
VMEM_LIMIT = 28 * 1024 * 1024
FULL_VMEM_LIMIT = 58 * 1024 * 1024
VMEM = pl.BlockSpec(memory_space=pltpu.VMEM)
SMEM = pl.BlockSpec(memory_space=pltpu.SMEM)
HBM = pl.BlockSpec(memory_space=pltpu.HBM)


def offset_of(k):
    return k // 9 - 1, (k // 3) % 3 - 1, k % 3 - 1


def row_in_scene_window(neighbours, shift):
    return jnp.where(neighbours >= 0, (neighbours - shift) & (T - 1), -1)


def one_hot(hit):
    return jnp.where(hit, jnp.ones((), jnp.bfloat16), jnp.zeros((), jnp.bfloat16))


def beside(xe, first, f_ref, g_ref, rows):
    channels = f_ref.shape[1]
    xe[first : first + rows, 0:channels] = f_ref[0:rows, :]
    xe[first : first + rows, channels:] = g_ref[0:rows, :]


def fill_edges(xe, shift):
    edge = jnp.zeros((ROW, xe.shape[1]), jnp.bfloat16)
    xe[0:ROW, :] = edge
    xe[xe.shape[0] - ROW :, :] = edge
    shift[...] = jnp.zeros_like(shift)
    for k in range(27):
        if offset_of(k)[1]:
            shift[k : k + 1, :] = jnp.full((1, T), ROW * offset_of(k)[1], jnp.int32)


def weight_terms(chunks, ks_of, source, f_ref, g_ref, nb_ref, xe, shift, buffers, acc, aside):
    channels = f_ref.shape[1]
    spot = lax.broadcasted_iota(jnp.int32, (T, T), 1).astype(jnp.bfloat16)
    pads = jnp.full((5, T), -1, jnp.int32)

    def gathers(chunk):
        to_f, to_g = buffers[chunk % 2]
        ks = ks_of(chunk)
        for h in range(CHUNK_W // T):
            tile = chunk * (CHUNK_W // T) + h
            rows = slice(h * T, (h + 1) * T)
            mine = jnp.concatenate([nb_ref[:, tile, :], pads], axis=0)
            mine = row_in_scene_window(mine, shift[...]).T.astype(jnp.bfloat16)
            for dz, dy in sorted({offset_of(k)[:2] for k in ks if k < 13}):
                some = [k for k in ks if k < 13 and offset_of(k)[:2] == (dz, dy)]
                start = tile * T + source + ROW * dy + LAYER * dz
                window = xe[start : start + T, :]
                hot = jnp.concatenate([one_hot(mine[:, k : k + 1] == spot) for k in some], axis=0)
                picked = jnp.dot(hot, window, preferred_element_type=jnp.float32)
                picked = picked.astype(jnp.bfloat16)
                for q, k in enumerate(some):
                    part = picked[q * T : (q + 1) * T]
                    to_f[rows, k * T : (k + 1) * T] = part[:, :channels]
                    to_g[rows, k * T : (k + 1) * T] = part[:, channels:]
                yield

    def product(chunk):
        here = slice(chunk * CHUNK_W, (chunk + 1) * CHUNK_W)
        picked_f, picked_g = buffers[chunk % 2]
        ks = ks_of(chunk)
        if 13 in ks:
            picked_g[:, 13 * T :] = g_ref[here, :]
        for ref, picked, side, end in ((g_ref, picked_f, 0, 13), (f_ref, picked_g, 13, 14)):
            left = ref[here, :].T
            for group in (range(0, 4), range(4, 8), range(8, end)):
                group = [k for k in group if k in ks]
                if group:
                    span = slice(group[0] * T, (group[-1] + 1) * T)
                    to = slice((side + group[0]) * T, (side + group[-1] + 1) * T)
                    acc[:, to] += jnp.dot(left, picked[:, span], preferred_element_type=jnp.float32)
                    yield

    pending = iter(())
    for chunk in chunks:
        for turn, _ in enumerate(gathers(chunk)):
            next(pending, None)
            if turn % 2:
                next(aside, None)
        for _ in pending:
            pass
        pending = product(chunk)
    for _ in pending:
        pass
    for _ in aside:
        pass


def weight_inner_kernel(voxels, f_ref, g_ref, nb_ref, w_hbm, acc, wt_hbm, xe, shift, w_ref, wt, gf, gg, gf2, gg2, sems):
    channels = f_ref.shape[1]
    fetch = pltpu.make_async_copy(w_hbm, w_ref, sems.at[0])
    fetch.start()
    beside(xe, ROW, f_ref, g_ref, voxels)
    fill_edges(xe, shift)
    acc[...] = jnp.zeros_like(acc)
    store = pltpu.make_async_copy(wt, wt_hbm, sems.at[1])

    def turn_weights():
        fetch.wait()
        for k in range(27):
            span = slice(k * T, (k + 1) * T)
            wt[0:channels, span] = w_ref[span, :].T
            wt[channels:, span] = w_ref[(26 - k) * T : (27 - k) * T, :]
            if k % 2:
                yield
        store.start()

    def ks_of(chunk):
        return range(9 if chunk < LAYER // CHUNK_W else 0, 14)

    chunks = range(voxels // CHUNK_W)
    buffers = ((gf, gg), (gf2, gg2))
    weight_terms(chunks, ks_of, ROW, f_ref, g_ref, nb_ref, xe, shift, buffers, acc, turn_weights())
    store.wait()


def weight_halo_kernel(scale, parity_ref, f_ref, g_ref, low_ref, nb_ref, in_ref, mine_ref, other_ref, xe, shift, gf, gg, gf2, gg2, acc, out_ref):
    channels = f_ref.shape[1]
    xe[ROW : ROW + LAYER, 0:channels] = low_ref[0]
    xe[ROW : ROW + LAYER, channels:] = low_ref[1]
    fill_edges(xe, shift)
    acc[...] = jnp.zeros_like(acc)
    chunks = range(LAYER // CHUNK_W)
    buffers = ((gf, gg), (gf2, gg2))
    weight_terms(
        chunks, lambda _: range(9), ROW + LAYER, f_ref, g_ref, nb_ref, xe, shift, buffers, acc, iter(())
    )

    def total(block, touched):
        span = slice(block * T, (block + 1) * T)
        return (in_ref[:, span] + acc[:, span] if touched else in_ref[:, span]) * scale

    for k in range(13):
        out_ref[k * T : (k + 1) * T, :] = total(k, k < 9).T.astype(out_ref.dtype)
    for k in range(14):
        out_ref[(26 - k) * T : (27 - k) * T, :] = total(13 + k, k < 9).astype(out_ref.dtype)
    if out_ref.shape[0] > 27 * T:
        out_ref[27 * T :, :] = jnp.zeros((out_ref.shape[0] - 27 * T, out_ref.shape[1]), out_ref.dtype)
    half = out_ref.shape[0] // 2
    parity = parity_ref[0]
    mine_ref[...] = out_ref[pl.ds(pl.multiple_of(parity * half, 16), half), :]
    other_ref[...] = out_ref[pl.ds(pl.multiple_of((1 - parity) * half, 16), half), :]


def rows_scratch(rows, channels):
    return [
        pltpu.VMEM((rows + 2 * ROW, 2 * channels), jnp.bfloat16),
        pltpu.VMEM((32, T), jnp.int32),
    ]


def gathered_scratch():
    return [
        pltpu.VMEM((CHUNK_W, 13 * T), jnp.bfloat16),
        pltpu.VMEM((CHUNK_W, 14 * T), jnp.bfloat16),
    ] * 2


def grad_w_inner(feats, grads, neigh, weight):
    voxels, channels = feats.shape
    turned = (2 * channels, 27 * channels)
    return pl.pallas_call(
        functools.partial(weight_inner_kernel, voxels),
        out_shape=(
            jax.ShapeDtypeStruct((channels, 27 * T), jnp.float32),
            jax.ShapeDtypeStruct(turned, jnp.bfloat16),
        ),
        in_specs=[VMEM] * 3 + [HBM],
        out_specs=(VMEM, HBM),
        scratch_shapes=rows_scratch(voxels, channels)
        + [pltpu.VMEM(weight.shape, jnp.bfloat16), pltpu.VMEM(turned, jnp.bfloat16)]
        + gathered_scratch()
        + [pltpu.SemaphoreType.DMA((2,))],
        compiler_params=pltpu.CompilerParams(vmem_limit_bytes=VMEM_LIMIT),
        cost_estimate=pl.CostEstimate(flops=8 * 10**9, bytes_accessed=4 * 10**6, transcendentals=0),
        name="weight_gradient_inner",
    )(feats, grads, neigh, weight)


def grad_w_halo(feats, grads, low, neigh, partial, parity, scale, rows):
    channels = feats.shape[1]
    out = jax.ShapeDtypeStruct((rows // 2, channels), jnp.bfloat16)
    return pl.pallas_call(
        functools.partial(weight_halo_kernel, scale),
        out_shape=(out, out),
        in_specs=[SMEM] + [VMEM] * 5,
        out_specs=(VMEM, VMEM),
        scratch_shapes=rows_scratch(LAYER, channels)
        + gathered_scratch()
        + [
            pltpu.VMEM((channels, 27 * T), jnp.float32),
            pltpu.VMEM((rows, channels), jnp.bfloat16),
        ],
        compiler_params=pltpu.CompilerParams(vmem_limit_bytes=VMEM_LIMIT),
        cost_estimate=pl.CostEstimate(flops=3 * 10**9, bytes_accessed=4 * 10**6, transcendentals=0),
        name="weight_gradient_halo",
    )(parity, feats, grads, low, neigh, partial)


def stack_kernel(f_last, g_last, f_first, g_first, last, first):
    last[0] = f_last[...]
    last[1] = g_last[...]
    first[0] = f_first[...]
    first[1] = g_first[...]


def stack_edges(feats, grads):
    voxels, channels = feats.shape
    out = jax.ShapeDtypeStruct((2, LAYER, channels), jnp.bfloat16)
    end = pl.BlockSpec((LAYER, channels), lambda i: (voxels // LAYER - 1, 0))
    start = pl.BlockSpec((LAYER, channels), lambda i: (0, 0))
    return pl.pallas_call(
        stack_kernel,
        grid=(1,),
        out_shape=(out, out),
        in_specs=[end, end, start, start],
        out_specs=(VMEM, VMEM),
        compiler_params=pltpu.CompilerParams(vmem_limit_bytes=FULL_VMEM_LIMIT),
        name="stack_edges",
    )(feats, grads, feats, grads)


def rows_needed(run):
    first, end = run
    return (
        first - LAYER - (ROW if first % LAYER else 0),
        end + LAYER + (ROW if end % LAYER else 0),
    )


def conv_kernel(voxels, run, halos, f_ref, g_ref, nb_ref, wt_hbm, *rest):
    halos = list(rest[:halos])
    conv_hbm, gin_hbm, wt, conv_ref, gin_ref, xe, nb, rel, gf, gg, gf2, gg2, sems = rest[-13:]
    channels = f_ref.shape[1]
    size = run[1] - run[0]

    origin = run[0] - LAYER - ROW
    low, high = rows_needed(run)
    main = (max(low, 0), min(high, voxels))
    rows = pl.ds(main[0], main[1] - main[0])
    to = pl.ds(main[0] - origin, main[1] - main[0])
    copies = [
        (nb_ref, nb),
        (f_ref.at[rows, :], xe.at[to, pl.ds(0, channels)]),
        (g_ref.at[rows, :], xe.at[to, pl.ds(channels, channels)]),
    ]
    parts = []
    if low < 0:
        parts.append((pl.ds(LAYER + low, -low), pl.ds(low - origin, -low)))
    if high > voxels:
        parts.append((pl.ds(0, high - voxels), pl.ds(voxels - origin, high - voxels)))
    for halo, (rows, to) in zip(halos, parts):
        for side in range(2):
            lanes = pl.ds(side * channels, channels)
            copies.append((halo.at[side, rows, :], xe.at[to, lanes]))
    early = len(copies)
    copies.append((wt_hbm, wt))
    copies = [
        pltpu.make_async_copy(source, target, sems.at[i])
        for i, (source, target) in enumerate(copies)
    ]
    for copy in copies:
        copy.start()
    edge = jnp.zeros((ROW, 2 * channels), jnp.bfloat16)
    if low - origin:
        xe[0:ROW, :] = edge
    if high - origin < xe.shape[0]:
        xe[xe.shape[0] - ROW :, :] = edge
    copies[0].wait()
    for k in range(27):
        rel[k, :, :] = row_in_scene_window(nb[k], ROW * offset_of(k)[1])
    first_tile = run[0] // T
    for copy in copies[1:early]:
        copy.wait()

    spot = lax.broadcasted_iota(jnp.int32, (T, T), 0).astype(jnp.bfloat16)
    none = jnp.zeros((T, T), jnp.bfloat16)
    buffers = ((gf, gg), (gf2, gg2))

    def hot(tile, k):
        row = rel[k, first_tile + tile : first_tile + tile + 1, :]
        row = jnp.broadcast_to(row, (ROW, T)).astype(jnp.bfloat16)
        return one_hot(jnp.concatenate([row] * (T // ROW), axis=0) == spot)

    def gathers(chunk):
        to_f, to_g = buffers[chunk % 2]
        for h in range(CHUNK_C // T):
            tile = chunk * (CHUNK_C // T) + h
            cols = slice(h * T, (h + 1) * T)
            kept = []

            def put(k, part):
                to_f[k * T : (k + 1) * T, cols] = part[:channels]
                to_g[k * T : (k + 1) * T, cols] = part[channels:]

            def put_pair(source, right, pair):
                picked = jnp.dot(source, right, preferred_element_type=jnp.float32)
                picked = picked.astype(jnp.bfloat16)
                put(pair[0], picked[:, :T])
                put(pair[1], picked[:, T:])

            for dz in (-1, 0, 1):
                for dy in (-1, 0, 1):
                    start = tile * T + ROW + ROW * dy + LAYER * (dz + 1)
                    window = xe[start : start + T, :].T
                    first = 9 * (dz + 1) + 3 * (dy + 1)
                    pair = (first, first + 2)
                    right = jnp.concatenate([hot(tile, k) for k in pair], axis=1)
                    put_pair(window, right, pair)
                    if first + 1 == 13:
                        put(13, window)
                    else:
                        kept.append((first + 1, window))
                    if len(kept) == 2:
                        (k0, window0), (k1, window1) = kept
                        right = jnp.concatenate(
                            [
                                jnp.concatenate([hot(tile, k0), none], axis=1),
                                jnp.concatenate([none, hot(tile, k1)], axis=1),
                            ],
                            axis=0,
                        )
                        put_pair(jnp.concatenate([window0, window1], axis=1), right, (k0, k1))
                        kept = []
                    yield

    def product(chunk):
        rows = slice(chunk * CHUNK_C, (chunk + 1) * CHUNK_C)
        kernels = (slice(0, channels), slice(channels, 2 * channels))
        outs = ((conv_ref, conv_hbm), (gin_ref, gin_hbm))
        for (out, out_hbm), picked, side in zip(outs, buffers[chunk % 2], kernels):
            total = None
            for part in range(3):
                span = slice(part * 9 * T, (part + 1) * 9 * T)
                term = jnp.dot(wt[side, span], picked[span, :], preferred_element_type=jnp.float32)
                total = term if total is None else total + term
                if part == 2:
                    out[rows, :] = total.T.astype(jnp.bfloat16)
                    copy = pltpu.make_async_copy(
                        out.at[rows, :],
                        out_hbm.at[pl.ds(run[0] + chunk * CHUNK_C, CHUNK_C), :],
                        sems.at[len(copies) + len(written)],
                    )
                    copy.start()
                    written.append(copy)
                yield

    written = []
    pending = iter(())
    for chunk in range(size // CHUNK_C):
        for turn, _ in enumerate(gathers(chunk)):
            if turn % 3 == 2:
                next(pending, None)
        for _ in pending:
            pass
        if chunk == 0:
            for copy in copies[early:]:
                copy.wait()
        pending = product(chunk)
    for _ in pending:
        pass
    for copy in written:
        copy.wait()


def conv_run(feats, grads, low, high, neigh, turned, run, earlier, name):
    voxels, channels = feats.shape
    out = jax.ShapeDtypeStruct((voxels, channels), jnp.bfloat16)
    first, end = rows_needed(run)
    halos = ((low,) if first < 0 else ()) + ((high,) if end > voxels else ())
    operands = (feats, grads, neigh, turned) + halos + earlier
    size = run[1] - run[0]
    return pl.pallas_call(
        functools.partial(conv_kernel, voxels, run, len(halos)),
        out_shape=(out, out),
        in_specs=[HBM] * len(operands),
        out_specs=(HBM, HBM),
        input_output_aliases={4 + len(halos) + i: i for i in range(len(earlier))},
        scratch_shapes=[
            pltpu.VMEM(turned.shape, jnp.bfloat16),
            pltpu.VMEM((size, channels), jnp.bfloat16),
            pltpu.VMEM((size, channels), jnp.bfloat16),
            pltpu.VMEM((size + 2 * (LAYER + ROW), 2 * channels), jnp.bfloat16),
            pltpu.VMEM(neigh.shape, jnp.int32),
            pltpu.VMEM(neigh.shape, jnp.int32),
        ]
        + [pltpu.VMEM((27 * T, CHUNK_C), jnp.bfloat16)] * 4
        + [pltpu.SemaphoreType.DMA((8 + 2 * size // CHUNK_C,))],
        compiler_params=pltpu.CompilerParams(vmem_limit_bytes=FULL_VMEM_LIMIT),
        cost_estimate=pl.CostEstimate(flops=10**10, bytes_accessed=6 * 10**6, transcendentals=0),
        name=name,
    )(*operands)


def sum_kernel(*refs):
    *parts, out_ref = refs
    terms = [ref[i] for ref in parts for i in range(ref.shape[0])]
    total = terms[0].astype(jnp.float32)
    for term in terms[1:]:
        total += term.astype(jnp.float32)
    total = total.astype(out_ref.dtype)
    for i in range(out_ref.shape[0]):
        out_ref[i] = total


def sum_parts(parts, copies, name):
    shape = parts[0].shape[1:]
    return pl.pallas_call(
        sum_kernel,
        out_shape=jax.ShapeDtypeStruct((copies,) + shape, parts[0].dtype),
        in_specs=[VMEM] * len(parts),
        out_specs=VMEM,
        compiler_params=pltpu.CompilerParams(vmem_limit_bytes=VMEM_LIMIT),
        name=name,
    )(*parts)


def widen_kernel(side_ref, in_ref, *rest):
    out_ref = rest[-1]
    out_ref[...] = in_ref[...].astype(out_ref.dtype)


def widen(rows, side, count, earlier, name):
    half, channels = rows.shape
    block = (half // 2, channels)
    return pl.pallas_call(
        widen_kernel,
        grid_spec=pltpu.PrefetchScalarGridSpec(
            num_scalar_prefetch=1,
            grid=(2,),
            in_specs=[pl.BlockSpec(block, lambda i, side: (i, 0))]
            + [pl.BlockSpec(memory_space=pl.ANY)] * len(earlier),
            out_specs=pl.BlockSpec(block, lambda i, side: (side[0] * 2 + i, 0)),
        ),
        out_shape=jax.ShapeDtypeStruct((count, channels), jnp.float32),
        input_output_aliases={2 + i: i for i in range(len(earlier))},
        compiler_params=pltpu.CompilerParams(vmem_limit_bytes=VMEM_LIMIT),
        name=name,
    )(side, rows, *earlier)


def local(features, neighbours, weight, grad_out):
    feats, grads = features[0], grad_out[0]
    voxels, channels = feats.shape
    neigh = neighbours.reshape(27, voxels // T, T)
    space, dp = lax.axis_size("space"), lax.axis_size("dp")
    up = [(i, i + 1) for i in range(space - 1)]
    down = [(i + 1, i) for i in range(space - 1)]
    last, first = stack_edges(feats, grads)
    low = lax.ppermute(last, "space", up)
    high = lax.ppermute(first, "space", down)

    scale = 1.0 / math.sqrt(dp * space * voxels)
    share = -(-27 * channels // (16 * dp)) * 16
    parity = (lax.axis_index("dp") % 2).astype(jnp.int32).reshape(1)
    inner, turned = grad_w_inner(feats, grads, neigh, weight.reshape(27 * channels, channels))
    low, high, inner = lax.optimization_barrier((low, high, inner))
    mine, other = grad_w_halo(feats, grads, low, neigh, inner, parity, scale, share * dp)
    swap = [(i, i ^ 1) for i in range(dp)]
    alike = [list(range(0, dp, 2)), list(range(1, dp, 2))]
    other = lax.ppermute(other, "dp", swap)
    mine = sum_parts((mine[None], other[None]), 1, "sum_of_pair")
    mine, turned = lax.optimization_barrier((mine, turned))
    chunks = voxels // CHUNK_C
    ends = [0, chunks // 4 * CHUNK_C, chunks * 3 // 4 * CHUNK_C, voxels]

    def conv(done, part):
        run = (ends[part], ends[part + 1])
        name = "conv_run_%d" % part
        return conv_run(feats, grads, low, high, neigh, turned, run, done, name)

    def exchange(pieces):
        return lax.all_to_all(pieces, "dp", 0, 0, axis_index_groups=alike, tiled=True)

    pieces = exchange(mine.reshape(dp // 2, share, channels))
    done = conv((), 0)
    pieces, done = lax.optimization_barrier((pieces, done))
    pieces = lax.all_to_all(sum_parts((pieces,), space, "sum_for_space"), "space", 0, 0, tiled=True)
    done = conv(done, 1)
    pieces, done = lax.optimization_barrier((pieces, done))
    pieces = exchange(sum_parts((pieces,), dp // 2, "sum_for_dp"))
    done = conv(done, 2)
    pieces, done = lax.optimization_barrier((pieces, done))
    mine = pieces.reshape(dp // 2 * share, channels)
    other = lax.ppermute(mine, "dp", swap)
    grad_w = widen(mine, parity, 27 * channels, (), "widen_own_half")
    grad_w = widen(other, 1 - parity, 27 * channels, (grad_w,), "widen_other_half")
    conv_out, grad_in = done
    return conv_out[None], grad_in[None], grad_w.reshape(27, channels, channels)


def solution(mesh):
    in_specs = (P("dp", "space", None), P("dp", None, "space"), P(), P("dp", "space", None))
    out_specs = (P("dp", "space", None), P("dp", "space", None), P())
    return jax.shard_map(local, mesh=mesh, in_specs=in_specs, out_specs=out_specs, check_vma=False)
```

```python
import functools
import math

import jax
import jax.numpy as jnp
from jax import lax
from jax.experimental import pallas as pl
from jax.experimental.pallas import tpu as pltpu
from jax.sharding import PartitionSpec as P

PSIDE = 64
ROW = PSIDE // 4
LAYER = PSIDE * ROW
T = 128
CHUNK_W = 256
CHUNK_C = 256
VMEM_LIMIT = 28 * 1024 * 1024
FULL_VMEM_LIMIT = 58 * 1024 * 1024
VMEM = pl.BlockSpec(memory_space=pltpu.VMEM)
SMEM = pl.BlockSpec(memory_space=pltpu.SMEM)
HBM = pl.BlockSpec(memory_space=pltpu.HBM)


def offset_of(k):
    return k // 9 - 1, (k // 3) % 3 - 1, k % 3 - 1


def row_in_scene_window(neighbours, shift):
    return jnp.where(neighbours >= 0, (neighbours - shift) & (T - 1), -1)


def one_hot(hit):
    return jnp.where(hit, jnp.ones((), jnp.bfloat16), jnp.zeros((), jnp.bfloat16))


def fill_edges(xe):
    edge = jnp.zeros((ROW, xe.shape[1]), jnp.bfloat16)
    xe[0:ROW, :] = edge
    xe[xe.shape[0] - ROW :, :] = edge


def one_hot_columns(rel, k, tile):
    spot = lax.broadcasted_iota(jnp.int32, (T, T), 0).astype(jnp.bfloat16)
    row = jnp.broadcast_to(rel[k, tile : tile + 1, :], (ROW, T)).astype(jnp.bfloat16)
    return one_hot(jnp.concatenate([row] * (T // ROW), axis=0) == spot)


def gather_columns(tiles, ks, xe, origin, rel, first_tile, to_f, to_g):
    channels = xe.shape[1] // 2
    none = jnp.zeros((T, T), jnp.bfloat16)
    kept = []

    def put(k, cols, part):
        to_f[k * T : (k + 1) * T, cols] = part[:channels]
        to_g[k * T : (k + 1) * T, cols] = part[channels:]

    def put_dot(source, right, places):
        picked = jnp.dot(source, right, preferred_element_type=jnp.float32).astype(jnp.bfloat16)
        for q, (k, cols) in enumerate(places):
            put(k, cols, picked[:, q * T : (q + 1) * T])

    for h, tile in enumerate(tiles):
        cols = slice(h * T, (h + 1) * T)
        for dz, dy in sorted({offset_of(k)[:2] for k in ks}):
            some = [k for k in ks if offset_of(k)[:2] == (dz, dy)]
            start = origin + tile * T + ROW * dy + LAYER * dz
            window = xe[start : start + T, :].T
            if 13 in some:
                put(13, cols, window)
                some.remove(13)
            if len(some) > 1:
                pair = (some.pop(0), some.pop())
                right = [one_hot_columns(rel, k, first_tile + tile) for k in pair]
                put_dot(window, jnp.concatenate(right, axis=1), [(k, cols) for k in pair])
            for k in some:
                kept.append((k, cols, window, one_hot_columns(rel, k, first_tile + tile)))
            if len(kept) == 2:
                (k0, cols0, window0, hot0), (k1, cols1, window1, hot1) = kept
                right = jnp.concatenate(
                    [
                        jnp.concatenate([hot0, none], axis=1),
                        jnp.concatenate([none, hot1], axis=1),
                    ],
                    axis=0,
                )
                both = jnp.concatenate([window0, window1], axis=1)
                put_dot(both, right, [(k0, cols0), (k1, cols1)])
                kept = []
            yield
    for k, cols, window, hot in kept:
        put_dot(window, hot, [(k, cols)])


def weight_terms(chunks, ks_of, origin, f_ref, g_ref, xe, rel, buffers, acc):
    def product(chunk):
        here = slice(chunk * CHUNK_W, (chunk + 1) * CHUNK_W)
        picked_f, picked_g = buffers[chunk % 2]
        ks = ks_of(chunk)
        left_f, left_g = f_ref[here, :].T, g_ref[here, :].T
        if 13 in ks:
            picked_g[13 * T :, :] = left_g
        for left, picked, side, end in ((left_g, picked_f, 0, 13), (left_f, picked_g, 13, 14)):
            for group in (range(0, 4), range(4, 8), range(8, end)):
                group = [k for k in group if k in ks]
                if group:
                    span = slice(group[0] * T, (group[-1] + 1) * T)
                    to = slice((side + group[0]) * T, (side + group[-1] + 1) * T)
                    acc[:, to] += lax.dot_general(
                        left,
                        picked[span, :],
                        (((1,), (1,)), ((), ())),
                        preferred_element_type=jnp.float32,
                    )
                    yield

    pending = iter(())
    per = CHUNK_W // T
    for chunk in chunks:
        tiles = range(chunk * per, (chunk + 1) * per)
        ks = [k for k in ks_of(chunk) if k < 13]
        for _ in gather_columns(tiles, ks, xe, origin, rel, 0, *buffers[chunk % 2]):
            next(pending, None)
        for _ in pending:
            pass
        pending = product(chunk)
    for _ in pending:
        pass


def weight_inner_kernel(voxels, f_ref, g_ref, nb_ref, acc, xe, rel, gf, gg, gf2, gg2):
    channels = f_ref.shape[1]
    xe[ROW : ROW + voxels, 0:channels] = f_ref[...]
    xe[ROW : ROW + voxels, channels:] = g_ref[...]
    fill_edges(xe)
    for k in range(13):
        rel[k, :, :] = row_in_scene_window(nb_ref[k], ROW * offset_of(k)[1])
    acc[...] = jnp.zeros_like(acc)

    def ks_of(chunk):
        return range(9 if chunk < LAYER // CHUNK_W else 0, 14)

    chunks = range(voxels // CHUNK_W)
    weight_terms(chunks, ks_of, ROW, f_ref, g_ref, xe, rel, ((gf, gg), (gf2, gg2)), acc)


def weight_halo_kernel(scale, parity_ref, f_ref, g_ref, low_ref, nb_ref, in_ref, mine_ref, other_ref, xe, rel, gf, gg, gf2, gg2, acc, out_ref):
    channels = f_ref.shape[1]
    xe[ROW : ROW + LAYER, 0:channels] = low_ref[0]
    xe[ROW : ROW + LAYER, channels:] = low_ref[1]
    fill_edges(xe)
    for k in range(9):
        rel[k, :, :] = row_in_scene_window(nb_ref[k, 0 : LAYER // T, :], ROW * offset_of(k)[1])
    acc[...] = jnp.zeros_like(acc)
    chunks = range(LAYER // CHUNK_W)
    buffers = ((gf, gg), (gf2, gg2))
    weight_terms(chunks, lambda _: range(9), ROW + LAYER, f_ref, g_ref, xe, rel, buffers, acc)

    def total(block, touched):
        span = slice(block * T, (block + 1) * T)
        return (in_ref[:, span] + acc[:, span] if touched else in_ref[:, span]) * scale

    for k in range(13):
        out_ref[k * T : (k + 1) * T, :] = total(k, k < 9).T.astype(out_ref.dtype)
    for k in range(14):
        out_ref[(26 - k) * T : (27 - k) * T, :] = total(13 + k, k < 9).astype(out_ref.dtype)
    if out_ref.shape[0] > 27 * T:
        out_ref[27 * T :, :] = jnp.zeros((out_ref.shape[0] - 27 * T, out_ref.shape[1]), out_ref.dtype)
    half = out_ref.shape[0] // 2
    parity = parity_ref[0]
    mine_ref[...] = out_ref[pl.ds(pl.multiple_of(parity * half, 16), half), :]
    other_ref[...] = out_ref[pl.ds(pl.multiple_of((1 - parity) * half, 16), half), :]


def weight_scratch(rows, channels):
    return [
        pltpu.VMEM((rows + 2 * ROW, 2 * channels), jnp.bfloat16),
        pltpu.VMEM((13, rows // T, T), jnp.int32),
    ] + [
        pltpu.VMEM((13 * T, CHUNK_W), jnp.bfloat16),
        pltpu.VMEM((14 * T, CHUNK_W), jnp.bfloat16),
    ] * 2


def grad_w_inner(feats, grads, neigh):
    voxels, channels = feats.shape
    return pl.pallas_call(
        functools.partial(weight_inner_kernel, voxels),
        out_shape=jax.ShapeDtypeStruct((channels, 27 * T), jnp.float32),
        in_specs=[VMEM] * 3,
        out_specs=VMEM,
        scratch_shapes=weight_scratch(voxels, channels),
        compiler_params=pltpu.CompilerParams(vmem_limit_bytes=VMEM_LIMIT),
        cost_estimate=pl.CostEstimate(flops=8 * 10**9, bytes_accessed=4 * 10**6, transcendentals=0),
        name="weight_gradient_inner",
    )(feats, grads, neigh)


def grad_w_halo(feats, grads, low, neigh, partial, parity, scale, rows):
    channels = feats.shape[1]
    out = jax.ShapeDtypeStruct((rows // 2, channels), jnp.bfloat16)
    return pl.pallas_call(
        functools.partial(weight_halo_kernel, scale),
        out_shape=(out, out),
        in_specs=[SMEM] + [VMEM] * 5,
        out_specs=(VMEM, VMEM),
        scratch_shapes=weight_scratch(LAYER, channels)
        + [
            pltpu.VMEM((channels, 27 * T), jnp.float32),
            pltpu.VMEM((rows, channels), jnp.bfloat16),
        ],
        compiler_params=pltpu.CompilerParams(vmem_limit_bytes=VMEM_LIMIT),
        cost_estimate=pl.CostEstimate(flops=3 * 10**9, bytes_accessed=4 * 10**6, transcendentals=0),
        name="weight_gradient_halo",
    )(parity, feats, grads, low, neigh, partial)


def stack_kernel(f_ref, g_ref, out_ref):
    out_ref[0] = f_ref[...]
    out_ref[1] = g_ref[...]


def stack_layer(feats, grads, layer, vmem, name):
    channels = feats.shape[1]
    block = pl.BlockSpec((LAYER, channels), lambda i: (layer, 0))
    return pl.pallas_call(
        stack_kernel,
        grid=(1,),
        out_shape=jax.ShapeDtypeStruct((2, LAYER, channels), jnp.bfloat16),
        in_specs=[block, block],
        out_specs=VMEM,
        compiler_params=pltpu.CompilerParams(vmem_limit_bytes=vmem),
        name=name,
    )(feats, grads)


def rows_needed(run):
    first, end = run
    return (
        first - LAYER - (ROW if first % LAYER else 0),
        end + LAYER + (ROW if end % LAYER else 0),
    )


def conv_kernel(voxels, run, halos, make_wt, f_ref, g_ref, nb_ref, w_hbm, *rest):
    halos = list(rest[:halos])
    if make_wt:
        conv_hbm, gin_hbm, wt, w_ref, *scratch = rest[-14:]
    else:
        conv_hbm, gin_hbm, wt, *scratch = rest[-13:]
    conv_ref, gin_ref, xe, nb, rel, gf, gg, gf2, gg2, sems = scratch
    channels = f_ref.shape[1]
    size = run[1] - run[0]

    origin = run[0] - LAYER - ROW
    low, high = rows_needed(run)
    main = (max(low, 0), min(high, voxels))
    rows = pl.ds(main[0], main[1] - main[0])
    to = pl.ds(main[0] - origin, main[1] - main[0])
    copies = [
        (nb_ref, nb),
        (f_ref.at[rows, :], xe.at[to, pl.ds(0, channels)]),
        (g_ref.at[rows, :], xe.at[to, pl.ds(channels, channels)]),
    ]
    parts = []
    if low < 0:
        parts.append((pl.ds(LAYER + low, -low), pl.ds(low - origin, -low)))
    if high > voxels:
        parts.append((pl.ds(0, high - voxels), pl.ds(voxels - origin, high - voxels)))
    for halo, (rows, to) in zip(halos, parts):
        for side in range(2):
            lanes = pl.ds(side * channels, channels)
            copies.append((halo.at[side, rows, :], xe.at[to, lanes]))
    early = len(copies)
    copies.append((w_hbm, w_ref if make_wt else wt))
    copies = [
        pltpu.make_async_copy(source, target, sems.at[i])
        for i, (source, target) in enumerate(copies)
    ]
    for copy in copies:
        copy.start()
    edge = jnp.zeros((ROW, 2 * channels), jnp.bfloat16)
    if low - origin:
        xe[0:ROW, :] = edge
    if high - origin < xe.shape[0]:
        xe[xe.shape[0] - ROW :, :] = edge
    copies[0].wait()
    for k in range(27):
        rel[k, :, :] = row_in_scene_window(nb[k], ROW * offset_of(k)[1])
    for copy in copies[1:early]:
        copy.wait()

    buffers = ((gf, gg), (gf2, gg2))

    def product(chunk):
        rows = slice(chunk * CHUNK_C, (chunk + 1) * CHUNK_C)
        kernels = (slice(0, channels), slice(channels, 2 * channels))
        outs = ((conv_ref, conv_hbm), (gin_ref, gin_hbm))
        for (out, out_hbm), picked, side in zip(outs, buffers[chunk % 2], kernels):
            total = None
            for part in range(3):
                span = slice(part * 9 * T, (part + 1) * 9 * T)
                term = jnp.dot(wt[side, span], picked[span, :], preferred_element_type=jnp.float32)
                total = term if total is None else total + term
                if part == 2:
                    out[rows, :] = total.T.astype(jnp.bfloat16)
                    copy = pltpu.make_async_copy(
                        out.at[rows, :],
                        out_hbm.at[pl.ds(run[0] + chunk * CHUNK_C, CHUNK_C), :],
                        sems.at[len(copies) + len(written)],
                    )
                    copy.start()
                    written.append(copy)
                yield

    written = []
    pending = iter(())
    per = CHUNK_C // T
    for chunk in range(size // CHUNK_C):
        tiles = range(chunk * per, (chunk + 1) * per)
        center, first_tile = run[0] - origin, run[0] // T
        moves = gather_columns(
            tiles, range(27), xe, center, rel, first_tile, *buffers[chunk % 2]
        )
        for turn, _ in enumerate(moves):
            if turn % 3 == 2:
                next(pending, None)
        for _ in pending:
            pass
        if chunk == 0:
            for copy in copies[early:]:
                copy.wait()
            if make_wt:
                for k in range(27):
                    span = slice(k * T, (k + 1) * T)
                    wt[0:channels, span] = w_ref[span, :].T
                    wt[channels:, span] = w_ref[(26 - k) * T : (27 - k) * T, :]
        pending = product(chunk)
    for _ in pending:
        pass
    for copy in written:
        copy.wait()


def conv_run(feats, grads, low, high, neigh, weight, run, earlier, name):
    voxels, channels = feats.shape
    out = jax.ShapeDtypeStruct((voxels, channels), jnp.bfloat16)
    first, end = rows_needed(run)
    halos = ((low,) if first < 0 else ()) + ((high,) if end > voxels else ())
    turned = jax.ShapeDtypeStruct((2 * channels, 27 * channels), jnp.bfloat16)
    make_wt = not earlier
    operands = (feats, grads, neigh, weight if make_wt else earlier[2]) + halos + earlier[:2]
    size = run[1] - run[0]
    results = pl.pallas_call(
        functools.partial(conv_kernel, voxels, run, len(halos), make_wt),
        out_shape=(out, out) + ((turned,) if make_wt else ()),
        in_specs=[HBM] * len(operands),
        out_specs=(HBM, HBM) + ((VMEM,) if make_wt else ()),
        input_output_aliases={4 + len(halos) + i: i for i in range(len(earlier[:2]))},
        scratch_shapes=[
            pltpu.VMEM(weight.shape if make_wt else turned.shape, jnp.bfloat16),
            pltpu.VMEM((size, channels), jnp.bfloat16),
            pltpu.VMEM((size, channels), jnp.bfloat16),
            pltpu.VMEM((size + 2 * (LAYER + ROW), 2 * channels), jnp.bfloat16),
            pltpu.VMEM(neigh.shape, jnp.int32),
            pltpu.VMEM(neigh.shape, jnp.int32),
        ]
        + [pltpu.VMEM((27 * T, CHUNK_C), jnp.bfloat16)] * 4
        + [pltpu.SemaphoreType.DMA((8 + 2 * size // CHUNK_C,))],
        compiler_params=pltpu.CompilerParams(vmem_limit_bytes=FULL_VMEM_LIMIT),
        cost_estimate=pl.CostEstimate(flops=10**10, bytes_accessed=6 * 10**6, transcendentals=0),
        name=name,
    )(*operands)
    return tuple(results) + earlier[2:]


def sum_kernel(*refs):
    *parts, out_ref = refs
    terms = [ref[i] for ref in parts for i in range(ref.shape[0])]
    total = terms[0].astype(jnp.float32)
    for term in terms[1:]:
        total += term.astype(jnp.float32)
    total = total.astype(out_ref.dtype)
    for i in range(out_ref.shape[0]):
        out_ref[i] = total


def sum_parts(parts, copies, name):
    shape = parts[0].shape[1:]
    return pl.pallas_call(
        sum_kernel,
        out_shape=jax.ShapeDtypeStruct((copies,) + shape, parts[0].dtype),
        in_specs=[VMEM] * len(parts),
        out_specs=VMEM,
        compiler_params=pltpu.CompilerParams(vmem_limit_bytes=VMEM_LIMIT),
        name=name,
    )(*parts)


def widen_kernel(side_ref, in_ref, *rest):
    out_ref = rest[-1]
    out_ref[...] = in_ref[...].astype(out_ref.dtype)


def widen(rows, side, count, earlier, name):
    half, channels = rows.shape
    block = (half // 2, channels)
    return pl.pallas_call(
        widen_kernel,
        grid_spec=pltpu.PrefetchScalarGridSpec(
            num_scalar_prefetch=1,
            grid=(2,),
            in_specs=[pl.BlockSpec(block, lambda i, side: (i, 0))]
            + [pl.BlockSpec(memory_space=pl.ANY)] * len(earlier),
            out_specs=pl.BlockSpec(block, lambda i, side: (side[0] * 2 + i, 0)),
        ),
        out_shape=jax.ShapeDtypeStruct((count, channels), jnp.float32),
        input_output_aliases={2 + i: i for i in range(len(earlier))},
        compiler_params=pltpu.CompilerParams(vmem_limit_bytes=VMEM_LIMIT),
        name=name,
    )(side, rows, *earlier)


def local(features, neighbours, weight, grad_out):
    feats, grads = features[0], grad_out[0]
    voxels, channels = feats.shape
    neigh = neighbours.reshape(27, voxels // T, T)
    space, dp = lax.axis_size("space"), lax.axis_size("dp")
    up = [(i, i + 1) for i in range(space - 1)]
    down = [(i + 1, i) for i in range(space - 1)]
    low = lax.ppermute(
        stack_layer(feats, grads, voxels // LAYER - 1, FULL_VMEM_LIMIT, "stack_last_layer"), "space", up
    )

    scale = 1.0 / math.sqrt(dp * space * voxels)
    share = -(-27 * channels // (16 * dp)) * 16
    parity = (lax.axis_index("dp") % 2).astype(jnp.int32).reshape(1)
    inner = grad_w_inner(feats, grads, neigh)
    inner, later_feats, later_grads = lax.optimization_barrier((inner, feats, grads))
    first = stack_layer(later_feats, later_grads, 0, VMEM_LIMIT, "stack_first_layer")
    high = lax.ppermute(first, "space", down)
    inner, first = lax.optimization_barrier((inner, first))
    mine, other = grad_w_halo(feats, grads, low, neigh, inner, parity, scale, share * dp)
    swap = [(i, i ^ 1) for i in range(dp)]
    alike = [list(range(0, dp, 2)), list(range(1, dp, 2))]
    other = lax.ppermute(other, "dp", swap)
    mine = sum_parts((mine[None], other[None]), 1, "sum_of_pair")
    mine, flat_weight = lax.optimization_barrier(
        (mine, weight.reshape(27 * channels, channels))
    )
    chunks = voxels // CHUNK_C
    ends = [0, chunks // 6 * CHUNK_C, chunks * 3 // 4 * CHUNK_C, voxels]

    def conv(done, part):
        run = (ends[part], ends[part + 1])
        name = "conv_run_%d" % part
        return conv_run(feats, grads, low, high, neigh, flat_weight, run, done, name)

    def exchange(pieces):
        return lax.all_to_all(pieces, "dp", 0, 0, axis_index_groups=alike, tiled=True)

    pieces = exchange(mine.reshape(dp // 2, share, channels))
    done = conv((), 0)
    pieces, done = lax.optimization_barrier((pieces, done))
    pieces = lax.all_to_all(sum_parts((pieces,), space, "sum_for_space"), "space", 0, 0, tiled=True)
    done = conv(done, 1)
    pieces, done = lax.optimization_barrier((pieces, done))
    pieces = exchange(sum_parts((pieces,), dp // 2, "sum_for_dp"))
    done = conv(done, 2)
    pieces, done = lax.optimization_barrier((pieces, done))
    mine = pieces.reshape(dp // 2 * share, channels)
    other = lax.ppermute(mine, "dp", swap)
    grad_w = widen(mine, parity, 27 * channels, (), "widen_own_half")
    grad_w = widen(other, 1 - parity, 27 * channels, (grad_w,), "widen_other_half")
    conv_out, grad_in, _ = done
    return conv_out[None], grad_in[None], grad_w.reshape(27, channels, channels)


def solution(mesh):
    in_specs = (P("dp", "space", None), P("dp", None, "space"), P(), P("dp", "space", None))
    out_specs = (P("dp", "space", None), P("dp", "space", None), P())
    return jax.shard_map(local, mesh=mesh, in_specs=in_specs, out_specs=out_specs, check_vma=False)
```

```python
import functools
import math

import jax
import jax.numpy as jnp
from jax import lax
from jax.experimental import pallas as pl
from jax.experimental.pallas import tpu as pltpu
from jax.sharding import PartitionSpec as P

PSIDE = 64
ROW = PSIDE // 4
LAYER = PSIDE * ROW
T = 128
CHUNK_W = 256
CHUNK_C = 256
VMEM_LIMIT = 28 * 1024 * 1024
FULL_VMEM_LIMIT = 58 * 1024 * 1024
VMEM = pl.BlockSpec(memory_space=pltpu.VMEM)
HBM = pl.BlockSpec(memory_space=pltpu.HBM)


def offset_of(k):
    return k // 9 - 1, (k // 3) % 3 - 1, k % 3 - 1


def row_in_scene_window(neighbours, shift):
    return jnp.where(neighbours >= 0, (neighbours - shift) & (T - 1), -1)


def one_hot(hit):
    return jnp.where(hit, jnp.ones((), jnp.bfloat16), jnp.zeros((), jnp.bfloat16))


def own_side():
    return lax.bitwise_and(lax.axis_index("dp"), 1).astype(jnp.int32)


def fill_edges(xe):
    edge = jnp.zeros((ROW, xe.shape[1]), jnp.bfloat16)
    xe[0:ROW, :] = edge
    xe[xe.shape[0] - ROW :, :] = edge


def one_hot_columns(rel, k, tile):
    spot = lax.broadcasted_iota(jnp.int32, (T, T), 0).astype(jnp.bfloat16)
    row = jnp.broadcast_to(rel[k, tile : tile + 1, :], (ROW, T)).astype(jnp.bfloat16)
    return one_hot(jnp.concatenate([row] * (T // ROW), axis=0) == spot)


def gather_columns(tiles, ks, xe, origin, rel, first_tile, to_f, to_g):
    channels = xe.shape[1] // 2
    none = jnp.zeros((T, T), jnp.bfloat16)
    kept = []

    def put(k, cols, part):
        to_f[k * T : (k + 1) * T, cols] = part[:channels]
        to_g[k * T : (k + 1) * T, cols] = part[channels:]

    def put_dot(source, right, places):
        picked = jnp.dot(source, right, preferred_element_type=jnp.float32).astype(jnp.bfloat16)
        for q, (k, cols) in enumerate(places):
            put(k, cols, picked[:, q * T : (q + 1) * T])

    for h, tile in enumerate(tiles):
        cols = slice(h * T, (h + 1) * T)
        for dz, dy in sorted({offset_of(k)[:2] for k in ks}):
            some = [k for k in ks if offset_of(k)[:2] == (dz, dy)]
            start = origin + tile * T + ROW * dy + LAYER * dz
            window = xe[start : start + T, :].T
            if 13 in some:
                put(13, cols, window)
                some.remove(13)
            if len(some) > 1:
                pair = (some.pop(0), some.pop())
                right = [one_hot_columns(rel, k, first_tile + tile) for k in pair]
                put_dot(window, jnp.concatenate(right, axis=1), [(k, cols) for k in pair])
            for k in some:
                kept.append((k, cols, window, one_hot_columns(rel, k, first_tile + tile)))
            if len(kept) == 2:
                (k0, cols0, window0, hot0), (k1, cols1, window1, hot1) = kept
                right = jnp.concatenate(
                    [
                        jnp.concatenate([hot0, none], axis=1),
                        jnp.concatenate([none, hot1], axis=1),
                    ],
                    axis=0,
                )
                both = jnp.concatenate([window0, window1], axis=1)
                put_dot(both, right, [(k0, cols0), (k1, cols1)])
                kept = []
            yield
    for k, cols, window, hot in kept:
        put_dot(window, hot, [(k, cols)])


def weight_terms(chunks, ks_of, origin, f_ref, g_ref, xe, rel, buffers, acc):
    def product(chunk):
        here = slice(chunk * CHUNK_W, (chunk + 1) * CHUNK_W)
        picked_f, picked_g = buffers[chunk % 2]
        ks = ks_of(chunk)
        left_f, left_g = f_ref[here, :].T, g_ref[here, :].T
        if 13 in ks:
            picked_g[13 * T :, :] = left_g
        for left, picked, side, end in ((left_g, picked_f, 0, 13), (left_f, picked_g, 13, 14)):
            for group in (range(0, 4), range(4, 8), range(8, end)):
                group = [k for k in group if k in ks]
                if group:
                    span = slice(group[0] * T, (group[-1] + 1) * T)
                    to = slice((side + group[0]) * T, (side + group[-1] + 1) * T)
                    acc[:, to] += lax.dot_general(
                        left,
                        picked[span, :],
                        (((1,), (1,)), ((), ())),
                        preferred_element_type=jnp.float32,
                    )
                    yield

    pending = iter(())
    per = CHUNK_W // T
    for chunk in chunks:
        tiles = range(chunk * per, (chunk + 1) * per)
        ks = [k for k in ks_of(chunk) if k < 13]
        for _ in gather_columns(tiles, ks, xe, origin, rel, 0, *buffers[chunk % 2]):
            next(pending, None)
        for _ in pending:
            pass
        pending = product(chunk)
    for _ in pending:
        pass


def weight_inner_kernel(voxels, f_ref, g_ref, nb_ref, acc, xe, rel, gf, gg, gf2, gg2):
    channels = f_ref.shape[1]
    xe[ROW : ROW + voxels, 0:channels] = f_ref[...]
    xe[ROW : ROW + voxels, channels:] = g_ref[...]
    fill_edges(xe)
    for k in range(13):
        rel[k, :, :] = row_in_scene_window(nb_ref[k], ROW * offset_of(k)[1])
    acc[...] = jnp.zeros_like(acc)

    def ks_of(chunk):
        return range(9 if chunk < LAYER // CHUNK_W else 0, 14)

    chunks = range(voxels // CHUNK_W)
    weight_terms(chunks, ks_of, ROW, f_ref, g_ref, xe, rel, ((gf, gg), (gf2, gg2)), acc)


def weight_halo_kernel(scale, f_ref, g_ref, low_ref, nb_ref, in_ref, mine_ref, other_ref, xe, rel, gf, gg, gf2, gg2, acc, out_ref):
    channels = f_ref.shape[1]
    xe[ROW : ROW + LAYER, 0:channels] = low_ref[0]
    xe[ROW : ROW + LAYER, channels:] = low_ref[1]
    fill_edges(xe)
    for k in range(9):
        rel[k, :, :] = row_in_scene_window(nb_ref[k, 0 : LAYER // T, :], ROW * offset_of(k)[1])
    acc[...] = jnp.zeros_like(acc)
    chunks = range(LAYER // CHUNK_W)
    buffers = ((gf, gg), (gf2, gg2))
    weight_terms(chunks, lambda _: range(9), ROW + LAYER, f_ref, g_ref, xe, rel, buffers, acc)

    def total(block, touched):
        span = slice(block * T, (block + 1) * T)
        return (in_ref[:, span] + acc[:, span] if touched else in_ref[:, span]) * scale

    for k in range(13):
        out_ref[k * T : (k + 1) * T, :] = total(k, k < 9).T.astype(out_ref.dtype)
    for k in range(14):
        out_ref[(26 - k) * T : (27 - k) * T, :] = total(13 + k, k < 9).astype(out_ref.dtype)
    if out_ref.shape[0] > 27 * T:
        out_ref[27 * T :, :] = jnp.zeros((out_ref.shape[0] - 27 * T, out_ref.shape[1]), out_ref.dtype)
    half = out_ref.shape[0] // 2
    parity = own_side()
    mine_ref[...] = out_ref[pl.ds(pl.multiple_of(parity * half, 16), half), :]
    other_ref[...] = out_ref[pl.ds(pl.multiple_of((1 - parity) * half, 16), half), :]


def weight_scratch(rows, channels):
    return [
        pltpu.VMEM((rows + 2 * ROW, 2 * channels), jnp.bfloat16),
        pltpu.VMEM((13, rows // T, T), jnp.int32),
    ] + [
        pltpu.VMEM((13 * T, CHUNK_W), jnp.bfloat16),
        pltpu.VMEM((14 * T, CHUNK_W), jnp.bfloat16),
    ] * 2


def grad_w_inner(feats, grads, neigh):
    voxels, channels = feats.shape
    return pl.pallas_call(
        functools.partial(weight_inner_kernel, voxels),
        out_shape=jax.ShapeDtypeStruct((channels, 27 * T), jnp.float32),
        in_specs=[VMEM] * 3,
        out_specs=VMEM,
        scratch_shapes=weight_scratch(voxels, channels),
        compiler_params=pltpu.CompilerParams(vmem_limit_bytes=VMEM_LIMIT),
        cost_estimate=pl.CostEstimate(flops=8 * 10**9, bytes_accessed=4 * 10**6, transcendentals=0),
        name="weight_gradient_inner",
    )(feats, grads, neigh)


def grad_w_halo(feats, grads, low, neigh, partial, scale, rows):
    channels = feats.shape[1]
    out = jax.ShapeDtypeStruct((rows // 2, channels), jnp.bfloat16)
    return pl.pallas_call(
        functools.partial(weight_halo_kernel, scale),
        out_shape=(out, out),
        in_specs=[VMEM] * 5,
        out_specs=(VMEM, VMEM),
        scratch_shapes=weight_scratch(LAYER, channels)
        + [
            pltpu.VMEM((channels, 27 * T), jnp.float32),
            pltpu.VMEM((rows, channels), jnp.bfloat16),
        ],
        compiler_params=pltpu.CompilerParams(vmem_limit_bytes=VMEM_LIMIT),
        cost_estimate=pl.CostEstimate(flops=10**8, bytes_accessed=10**5, transcendentals=0),
        name="weight_gradient_halo",
    )(feats, grads, low, neigh, partial)


def stack_kernel(f_ref, g_ref, out_ref):
    out_ref[0] = f_ref[...]
    out_ref[1] = g_ref[...]


def stack_layer(feats, grads, layer, vmem, name):
    channels = feats.shape[1]
    block = pl.BlockSpec((LAYER, channels), lambda i: (layer, 0))
    return pl.pallas_call(
        stack_kernel,
        grid=(1,),
        out_shape=jax.ShapeDtypeStruct((2, LAYER, channels), jnp.bfloat16),
        in_specs=[block, block],
        out_specs=VMEM,
        compiler_params=pltpu.CompilerParams(vmem_limit_bytes=vmem),
        name=name,
    )(feats, grads)


def rows_needed(run):
    first, end = run
    return (
        first - LAYER - (ROW if first % LAYER else 0),
        end + LAYER + (ROW if end % LAYER else 0),
    )


def conv_kernel(voxels, run, halos, make_wt, f_ref, g_ref, nb_ref, w_hbm, *rest):
    halos = list(rest[:halos])
    if make_wt:
        conv_hbm, gin_hbm, wt_hbm, wt, w_ref, *scratch = rest[-15:]
    else:
        conv_hbm, gin_hbm, wt, *scratch = rest[-13:]
    conv_ref, gin_ref, xe, nb, rel, gf, gg, gf2, gg2, sems = scratch
    channels = f_ref.shape[1]
    size = run[1] - run[0]

    origin = run[0] - LAYER - ROW
    low, high = rows_needed(run)
    main = (max(low, 0), min(high, voxels))
    rows = pl.ds(main[0], main[1] - main[0])
    to = pl.ds(main[0] - origin, main[1] - main[0])
    copies = [
        (nb_ref, nb),
        (f_ref.at[rows, :], xe.at[to, pl.ds(0, channels)]),
        (g_ref.at[rows, :], xe.at[to, pl.ds(channels, channels)]),
    ]
    parts = []
    if low < 0:
        parts.append((pl.ds(LAYER + low, -low), pl.ds(low - origin, -low)))
    if high > voxels:
        parts.append((pl.ds(0, high - voxels), pl.ds(voxels - origin, high - voxels)))
    for halo, (rows, to) in zip(halos, parts):
        for side in range(2):
            lanes = pl.ds(side * channels, channels)
            copies.append((halo.at[side, rows, :], xe.at[to, lanes]))
    early = len(copies)
    copies.append((w_hbm, w_ref if make_wt else wt))
    copies = [
        pltpu.make_async_copy(source, target, sems.at[i])
        for i, (source, target) in enumerate(copies)
    ]
    for copy in copies:
        copy.start()
    edge = jnp.zeros((ROW, 2 * channels), jnp.bfloat16)
    if low - origin:
        xe[0:ROW, :] = edge
    if high - origin < xe.shape[0]:
        xe[xe.shape[0] - ROW :, :] = edge
    copies[0].wait()
    for k in range(27):
        rel[k, :, :] = row_in_scene_window(nb[k], ROW * offset_of(k)[1])
    for copy in copies[1:early]:
        copy.wait()

    buffers = ((gf, gg), (gf2, gg2))

    def product(chunk):
        rows = slice(chunk * CHUNK_C, (chunk + 1) * CHUNK_C)
        kernels = (slice(0, channels), slice(channels, 2 * channels))
        outs = ((conv_ref, conv_hbm), (gin_ref, gin_hbm))
        for (out, out_hbm), picked, side in zip(outs, buffers[chunk % 2], kernels):
            total = None
            for part in range(3):
                span = slice(part * 9 * T, (part + 1) * 9 * T)
                term = jnp.dot(wt[side, span], picked[span, :], preferred_element_type=jnp.float32)
                total = term if total is None else total + term
                if part == 2:
                    out[rows, :] = total.T.astype(jnp.bfloat16)
                    copy = pltpu.make_async_copy(
                        out.at[rows, :],
                        out_hbm.at[pl.ds(run[0] + chunk * CHUNK_C, CHUNK_C), :],
                        sems.at[len(copies) + len(written)],
                    )
                    copy.start()
                    written.append(copy)
                yield

    def turn_weights():
        copies[-1].wait()
        for k in range(27):
            span = slice(k * T, (k + 1) * T)
            wt[0:channels, span] = w_ref[span, :].T
            wt[channels:, span] = w_ref[(26 - k) * T : (27 - k) * T, :]
            if k % 2:
                yield
        copy = pltpu.make_async_copy(wt, wt_hbm, sems.at[len(copies)])
        copy.start()
        written.append(copy)

    written = []
    turning = turn_weights()
    pending = iter(())
    per = CHUNK_C // T
    for chunk in range(size // CHUNK_C):
        tiles = range(chunk * per, (chunk + 1) * per)
        center, first_tile = run[0] - origin, run[0] // T
        moves = gather_columns(
            tiles, range(27), xe, center, rel, first_tile, *buffers[chunk % 2]
        )
        for turn, _ in enumerate(moves):
            if turn % 3 == 2:
                next(pending, None)
            if chunk == 0 and make_wt and turn >= 4:
                next(turning, None)
        for _ in pending:
            pass
        if chunk == 0:
            if make_wt:
                for _ in turning:
                    pass
            else:
                copies[-1].wait()
        pending = product(chunk)
    for _ in pending:
        pass
    for copy in written:
        copy.wait()


def conv_run(feats, grads, low, high, neigh, weight, run, earlier, name):
    voxels, channels = feats.shape
    out = jax.ShapeDtypeStruct((voxels, channels), jnp.bfloat16)
    first, end = rows_needed(run)
    halos = ((low,) if first < 0 else ()) + ((high,) if end > voxels else ())
    turned = jax.ShapeDtypeStruct((2 * channels, 27 * channels), jnp.bfloat16)
    make_wt = not earlier
    operands = (feats, grads, neigh, weight if make_wt else earlier[2]) + halos + earlier[:2]
    size = run[1] - run[0]
    results = pl.pallas_call(
        functools.partial(conv_kernel, voxels, run, len(halos), make_wt),
        out_shape=(out, out) + ((turned,) if make_wt else ()),
        in_specs=[HBM] * len(operands),
        out_specs=(HBM, HBM) + ((HBM,) if make_wt else ()),
        input_output_aliases={4 + len(halos) + i: i for i in range(len(earlier[:2]))},
        scratch_shapes=[
            pltpu.VMEM(turned.shape, jnp.bfloat16),
        ]
        + ([pltpu.VMEM(weight.shape, jnp.bfloat16)] if make_wt else [])
        + [
            pltpu.VMEM((size, channels), jnp.bfloat16),
            pltpu.VMEM((size, channels), jnp.bfloat16),
            pltpu.VMEM((size + 2 * (LAYER + ROW), 2 * channels), jnp.bfloat16),
            pltpu.VMEM(neigh.shape, jnp.int32),
            pltpu.VMEM(neigh.shape, jnp.int32),
        ]
        + [pltpu.VMEM((27 * T, CHUNK_C), jnp.bfloat16)] * 4
        + [pltpu.SemaphoreType.DMA((8 + 2 * size // CHUNK_C,))],
        compiler_params=pltpu.CompilerParams(vmem_limit_bytes=FULL_VMEM_LIMIT),
        cost_estimate=pl.CostEstimate(
            flops=10**8 if make_wt else 10**10, bytes_accessed=10**5, transcendentals=0
        ),
        name=name,
    )(*operands)
    return tuple(results) + earlier[2:]


def sum_kernel(*refs):
    *parts, out_ref = refs
    terms = [ref[i] for ref in parts for i in range(ref.shape[0])]
    total = terms[0].astype(jnp.float32)
    for term in terms[1:]:
        total += term.astype(jnp.float32)
    total = total.astype(out_ref.dtype)
    for i in range(out_ref.shape[0]):
        out_ref[i] = total


def sum_parts(parts, copies, name):
    shape = parts[0].shape[1:]
    return pl.pallas_call(
        sum_kernel,
        out_shape=jax.ShapeDtypeStruct((copies,) + shape, parts[0].dtype),
        in_specs=[VMEM] * len(parts),
        out_specs=VMEM,
        compiler_params=pltpu.CompilerParams(vmem_limit_bytes=VMEM_LIMIT),
        name=name,
    )(*parts)


def widen_kernel(in_ref, *rest):
    out_ref = rest[-1]
    out_ref[...] = in_ref[...].astype(out_ref.dtype)


def widen(rows, own, count, earlier, name):
    half, channels = rows.shape
    block = (half // 2, channels)

    def place(i):
        side = own_side() if own else 1 - own_side()
        return side * 2 + i, 0

    return pl.pallas_call(
        widen_kernel,
        grid=(2,),
        in_specs=[pl.BlockSpec(block, lambda i: (i, 0))]
        + [pl.BlockSpec(memory_space=pl.ANY)] * len(earlier),
        out_specs=pl.BlockSpec(block, place),
        out_shape=jax.ShapeDtypeStruct((count, channels), jnp.float32),
        input_output_aliases={1 + i: i for i in range(len(earlier))},
        compiler_params=pltpu.CompilerParams(vmem_limit_bytes=VMEM_LIMIT),
        name=name,
    )(rows, *earlier)


def local(features, neighbours, weight, grad_out):
    feats, grads = features[0], grad_out[0]
    voxels, channels = feats.shape
    neigh = neighbours.reshape(27, voxels // T, T)
    space, dp = lax.axis_size("space"), lax.axis_size("dp")
    up = [(i, i + 1) for i in range(space - 1)]
    down = [(i + 1, i) for i in range(space - 1)]
    low = lax.ppermute(
        stack_layer(feats, grads, voxels // LAYER - 1, FULL_VMEM_LIMIT, "stack_last_layer"), "space", up
    )

    scale = 1.0 / math.sqrt(dp * space * voxels)
    share = -(-27 * channels // (16 * dp)) * 16
    inner = grad_w_inner(feats, grads, neigh)
    inner, later_feats, later_grads = lax.optimization_barrier((inner, feats, grads))
    first = stack_layer(later_feats, later_grads, 0, VMEM_LIMIT, "stack_first_layer")
    high = lax.ppermute(first, "space", down)
    inner, first = lax.optimization_barrier((inner, first))
    mine, other = grad_w_halo(feats, grads, low, neigh, inner, scale, share * dp)
    swap = [(i, i ^ 1) for i in range(dp)]
    alike = [list(range(0, dp, 2)), list(range(1, dp, 2))]
    other = lax.ppermute(other, "dp", swap)
    mine = sum_parts((mine[None], other[None]), 1, "sum_of_pair")
    mine, flat_weight = lax.optimization_barrier(
        (mine, weight.reshape(27 * channels, channels))
    )
    chunks = voxels // CHUNK_C
    ends = [0, chunks // 4 * CHUNK_C, chunks * 3 // 4 * CHUNK_C, voxels]

    def conv(done, part):
        run = (ends[part], ends[part + 1])
        name = "conv_run_%d" % part
        return conv_run(feats, grads, low, high, neigh, flat_weight, run, done, name)

    def exchange(pieces):
        return lax.all_to_all(pieces, "dp", 0, 0, axis_index_groups=alike, tiled=True)

    pieces = exchange(mine.reshape(dp // 2, share, channels))
    done = conv((), 0)
    pieces, done = lax.optimization_barrier((pieces, done))
    pieces = lax.all_to_all(sum_parts((pieces,), space, "sum_for_space"), "space", 0, 0, tiled=True)
    done = conv(done, 1)
    pieces, done = lax.optimization_barrier((pieces, done))
    pieces = exchange(sum_parts((pieces,), dp // 2, "sum_for_dp"))
    done = conv(done, 2)
    pieces, done = lax.optimization_barrier((pieces, done))
    mine = pieces.reshape(dp // 2 * share, channels)
    other = lax.ppermute(mine, "dp", swap)
    grad_w = widen(mine, True, 27 * channels, (), "widen_own_half")
    grad_w = widen(other, False, 27 * channels, (grad_w,), "widen_other_half")
    conv_out, grad_in, _ = done
    return conv_out[None], grad_in[None], grad_w.reshape(27, channels, channels)


def solution(mesh):
    in_specs = (P("dp", "space", None), P("dp", None, "space"), P(), P("dp", "space", None))
    out_specs = (P("dp", "space", None), P("dp", "space", None), P())
    return jax.shard_map(local, mesh=mesh, in_specs=in_specs, out_specs=out_specs, check_vma=False)
```

```python
import functools
import math

import jax
import jax.numpy as jnp
from jax import lax
from jax.experimental import pallas as pl
from jax.experimental.pallas import tpu as pltpu
from jax.sharding import PartitionSpec as P

PSIDE = 64
ROW = PSIDE // 4
LAYER = PSIDE * ROW
T = 128
CHUNK_W = 256
CHUNK_C = 256
VMEM_LIMIT = 28 * 1024 * 1024
FULL_VMEM_LIMIT = 58 * 1024 * 1024
VMEM = pl.BlockSpec(memory_space=pltpu.VMEM)
HBM = pl.BlockSpec(memory_space=pltpu.HBM)


def offset_of(k):
    return k // 9 - 1, (k // 3) % 3 - 1, k % 3 - 1


def row_in_scene_window(neighbours, shift):
    return jnp.where(neighbours >= 0, (neighbours - shift) & (T - 1), -1)


def one_hot(hit):
    return jnp.where(hit, jnp.ones((), jnp.bfloat16), jnp.zeros((), jnp.bfloat16))


def own_side():
    return lax.bitwise_and(lax.axis_index("dp"), 1).astype(jnp.int32)


def fill_edges(xe):
    edge = jnp.zeros((ROW, xe.shape[1]), jnp.bfloat16)
    xe[0:ROW, :] = edge
    xe[xe.shape[0] - ROW :, :] = edge


def one_hot_columns(rel, k, tile):
    spot = lax.broadcasted_iota(jnp.int32, (T, T), 0).astype(jnp.bfloat16)
    row = jnp.broadcast_to(rel[k, tile : tile + 1, :], (ROW, T)).astype(jnp.bfloat16)
    return one_hot(jnp.concatenate([row] * (T // ROW), axis=0) == spot)


def gather_columns(tiles, ks, xe, origin, rel, first_tile, to_f, to_g):
    channels = xe.shape[1] // 2
    none = jnp.zeros((T, T), jnp.bfloat16)
    kept = []

    def put(k, cols, part):
        to_f[k * T : (k + 1) * T, cols] = part[:channels]
        to_g[k * T : (k + 1) * T, cols] = part[channels:]

    def put_dot(source, right, places):
        picked = jnp.dot(source, right, preferred_element_type=jnp.float32).astype(jnp.bfloat16)
        for q, (k, cols) in enumerate(places):
            put(k, cols, picked[:, q * T : (q + 1) * T])

    for h, tile in enumerate(tiles):
        cols = slice(h * T, (h + 1) * T)
        for dz, dy in sorted({offset_of(k)[:2] for k in ks}):
            some = [k for k in ks if offset_of(k)[:2] == (dz, dy)]
            start = origin + tile * T + ROW * dy + LAYER * dz
            window = xe[start : start + T, :].T
            if 13 in some:
                put(13, cols, window)
                some.remove(13)
            if len(some) > 1:
                pair = (some.pop(0), some.pop())
                right = [one_hot_columns(rel, k, first_tile + tile) for k in pair]
                put_dot(window, jnp.concatenate(right, axis=1), [(k, cols) for k in pair])
            for k in some:
                kept.append((k, cols, window, one_hot_columns(rel, k, first_tile + tile)))
            if len(kept) == 2:
                (k0, cols0, window0, hot0), (k1, cols1, window1, hot1) = kept
                right = jnp.concatenate(
                    [
                        jnp.concatenate([hot0, none], axis=1),
                        jnp.concatenate([none, hot1], axis=1),
                    ],
                    axis=0,
                )
                both = jnp.concatenate([window0, window1], axis=1)
                put_dot(both, right, [(k0, cols0), (k1, cols1)])
                kept = []
            yield
    for k, cols, window, hot in kept:
        put_dot(window, hot, [(k, cols)])


def weight_terms(chunks, ks_of, origin, f_ref, g_ref, xe, rel, buffers, acc):
    def product(chunk):
        here = slice(chunk * CHUNK_W, (chunk + 1) * CHUNK_W)
        picked_f, picked_g = buffers[chunk % 2]
        ks = ks_of(chunk)
        left_f, left_g = f_ref[here, :].T, g_ref[here, :].T
        if 13 in ks:
            picked_g[13 * T :, :] = left_g
        for left, picked, side, end in ((left_g, picked_f, 0, 13), (left_f, picked_g, 13, 14)):
            for group in (range(0, 4), range(4, 8), range(8, end)):
                group = [k for k in group if k in ks]
                if group:
                    span = slice(group[0] * T, (group[-1] + 1) * T)
                    to = slice((side + group[0]) * T, (side + group[-1] + 1) * T)
                    acc[:, to] += lax.dot_general(
                        left,
                        picked[span, :],
                        (((1,), (1,)), ((), ())),
                        preferred_element_type=jnp.float32,
                    )
                    yield

    pending = iter(())
    per = CHUNK_W // T
    for chunk in chunks:
        tiles = range(chunk * per, (chunk + 1) * per)
        ks = [k for k in ks_of(chunk) if k < 13]
        for _ in gather_columns(tiles, ks, xe, origin, rel, 0, *buffers[chunk % 2]):
            next(pending, None)
        for _ in pending:
            pass
        pending = product(chunk)
    for _ in pending:
        pass


def weight_inner_kernel(voxels, f_ref, g_ref, nb_ref, acc, xe, rel, gf, gg, gf2, gg2):
    channels = f_ref.shape[1]
    xe[ROW : ROW + voxels, 0:channels] = f_ref[...]
    xe[ROW : ROW + voxels, channels:] = g_ref[...]
    fill_edges(xe)
    for k in range(13):
        rel[k, :, :] = row_in_scene_window(nb_ref[k], ROW * offset_of(k)[1])
    acc[...] = jnp.zeros_like(acc)

    def ks_of(chunk):
        return range(9 if chunk < LAYER // CHUNK_W else 0, 14)

    chunks = range(voxels // CHUNK_W)
    weight_terms(chunks, ks_of, ROW, f_ref, g_ref, xe, rel, ((gf, gg), (gf2, gg2)), acc)


def weight_halo_kernel(scale, f_ref, g_ref, low_ref, nb_ref, in_ref, mine_ref, other_ref, xe, rel, gf, gg, gf2, gg2, acc, out_ref):
    channels = f_ref.shape[1]
    xe[ROW : ROW + LAYER, 0:channels] = low_ref[0]
    xe[ROW : ROW + LAYER, channels:] = low_ref[1]
    fill_edges(xe)
    for k in range(9):
        rel[k, :, :] = row_in_scene_window(nb_ref[k, 0 : LAYER // T, :], ROW * offset_of(k)[1])
    acc[...] = jnp.zeros_like(acc)
    chunks = range(LAYER // CHUNK_W)
    buffers = ((gf, gg), (gf2, gg2))
    weight_terms(chunks, lambda _: range(9), ROW + LAYER, f_ref, g_ref, xe, rel, buffers, acc)

    def total(block, touched):
        span = slice(block * T, (block + 1) * T)
        return (in_ref[:, span] + acc[:, span] if touched else in_ref[:, span]) * scale

    for k in range(13):
        out_ref[k * T : (k + 1) * T, :] = total(k, k < 9).T.astype(out_ref.dtype)
    for k in range(14):
        out_ref[(26 - k) * T : (27 - k) * T, :] = total(13 + k, k < 9).astype(out_ref.dtype)
    if out_ref.shape[0] > 27 * T:
        out_ref[27 * T :, :] = jnp.zeros((out_ref.shape[0] - 27 * T, out_ref.shape[1]), out_ref.dtype)
    half = out_ref.shape[0] // 2
    parity = own_side()
    mine_ref[...] = out_ref[pl.ds(pl.multiple_of(parity * half, 16), half), :]
    other_ref[...] = out_ref[pl.ds(pl.multiple_of((1 - parity) * half, 16), half), :]


def weight_scratch(rows, channels):
    return [
        pltpu.VMEM((rows + 2 * ROW, 2 * channels), jnp.bfloat16),
        pltpu.VMEM((13, rows // T, T), jnp.int32),
    ] + [
        pltpu.VMEM((13 * T, CHUNK_W), jnp.bfloat16),
        pltpu.VMEM((14 * T, CHUNK_W), jnp.bfloat16),
    ] * 2


def grad_w_inner(feats, grads, neigh):
    voxels, channels = feats.shape
    return pl.pallas_call(
        functools.partial(weight_inner_kernel, voxels),
        out_shape=jax.ShapeDtypeStruct((channels, 27 * T), jnp.float32),
        in_specs=[VMEM] * 3,
        out_specs=VMEM,
        scratch_shapes=weight_scratch(voxels, channels),
        compiler_params=pltpu.CompilerParams(vmem_limit_bytes=VMEM_LIMIT),
        cost_estimate=pl.CostEstimate(flops=8 * 10**9, bytes_accessed=4 * 10**6, transcendentals=0),
        name="weight_gradient_inner",
    )(feats, grads, neigh)


def grad_w_halo(feats, grads, low, neigh, partial, scale, rows):
    channels = feats.shape[1]
    out = jax.ShapeDtypeStruct((rows // 2, channels), jnp.bfloat16)
    return pl.pallas_call(
        functools.partial(weight_halo_kernel, scale),
        out_shape=(out, out),
        in_specs=[VMEM] * 5,
        out_specs=(VMEM, VMEM),
        scratch_shapes=weight_scratch(LAYER, channels)
        + [
            pltpu.VMEM((channels, 27 * T), jnp.float32),
            pltpu.VMEM((rows, channels), jnp.bfloat16),
        ],
        compiler_params=pltpu.CompilerParams(vmem_limit_bytes=VMEM_LIMIT),
        cost_estimate=pl.CostEstimate(flops=10**6, bytes_accessed=10**4, transcendentals=0),
        name="weight_gradient_halo",
    )(feats, grads, low, neigh, partial)


def stack_kernel(f_ref, g_ref, out_ref):
    out_ref[0] = f_ref[...]
    out_ref[1] = g_ref[...]


def stack_layer(feats, grads, layer, vmem, name):
    channels = feats.shape[1]
    block = pl.BlockSpec((LAYER, channels), lambda i: (layer, 0))
    return pl.pallas_call(
        stack_kernel,
        grid=(1,),
        out_shape=jax.ShapeDtypeStruct((2, LAYER, channels), jnp.bfloat16),
        in_specs=[block, block],
        out_specs=VMEM,
        compiler_params=pltpu.CompilerParams(vmem_limit_bytes=vmem),
        name=name,
    )(feats, grads)


def rows_needed(run):
    first, end = run
    return (
        first - LAYER - (ROW if first % LAYER else 0),
        end + LAYER + (ROW if end % LAYER else 0),
    )


def conv_kernel(voxels, run, halos, make_wt, f_ref, g_ref, nb_ref, w_hbm, *rest):
    halos = list(rest[:halos])
    if make_wt:
        conv_hbm, gin_hbm, wt_hbm, wt, w_ref, *scratch = rest[-15:]
    else:
        conv_hbm, gin_hbm, wt, *scratch = rest[-13:]
    conv_ref, gin_ref, xe, nb, rel, gf, gg, gf2, gg2, sems = scratch
    channels = f_ref.shape[1]
    size = run[1] - run[0]

    origin = run[0] - LAYER - ROW
    low, high = rows_needed(run)
    main = (max(low, 0), min(high, voxels))
    rows = pl.ds(main[0], main[1] - main[0])
    to = pl.ds(main[0] - origin, main[1] - main[0])
    copies = [
        (nb_ref, nb),
        (f_ref.at[rows, :], xe.at[to, pl.ds(0, channels)]),
        (g_ref.at[rows, :], xe.at[to, pl.ds(channels, channels)]),
    ]
    parts = []
    if low < 0:
        parts.append((pl.ds(LAYER + low, -low), pl.ds(low - origin, -low)))
    if high > voxels:
        parts.append((pl.ds(0, high - voxels), pl.ds(voxels - origin, high - voxels)))
    for halo, (rows, to) in zip(halos, parts):
        for side in range(2):
            lanes = pl.ds(side * channels, channels)
            copies.append((halo.at[side, rows, :], xe.at[to, lanes]))
    early = len(copies)
    copies.append((w_hbm, w_ref if make_wt else wt))
    copies = [
        pltpu.make_async_copy(source, target, sems.at[i])
        for i, (source, target) in enumerate(copies)
    ]
    for copy in copies:
        copy.start()
    edge = jnp.zeros((ROW, 2 * channels), jnp.bfloat16)
    if low - origin:
        xe[0:ROW, :] = edge
    if high - origin < xe.shape[0]:
        xe[xe.shape[0] - ROW :, :] = edge
    copies[0].wait()
    for k in range(27):
        rel[k, :, :] = row_in_scene_window(nb[k], ROW * offset_of(k)[1])
    for copy in copies[1:early]:
        copy.wait()

    buffers = ((gf, gg), (gf2, gg2))

    def product(chunk):
        rows = slice(chunk * CHUNK_C, (chunk + 1) * CHUNK_C)
        kernels = (slice(0, channels), slice(channels, 2 * channels))
        outs = ((conv_ref, conv_hbm), (gin_ref, gin_hbm))
        for (out, out_hbm), picked, side in zip(outs, buffers[chunk % 2], kernels):
            total = None
            for part in range(3):
                span = slice(part * 9 * T, (part + 1) * 9 * T)
                term = jnp.dot(wt[side, span], picked[span, :], preferred_element_type=jnp.float32)
                total = term if total is None else total + term
                if part == 2:
                    out[rows, :] = total.T.astype(jnp.bfloat16)
                    copy = pltpu.make_async_copy(
                        out.at[rows, :],
                        out_hbm.at[pl.ds(run[0] + chunk * CHUNK_C, CHUNK_C), :],
                        sems.at[len(copies) + len(written)],
                    )
                    copy.start()
                    written.append(copy)
                yield

    def turn_weights():
        copies[-1].wait()
        for k in range(27):
            span = slice(k * T, (k + 1) * T)
            wt[0:channels, span] = w_ref[span, :].T
            wt[channels:, span] = w_ref[(26 - k) * T : (27 - k) * T, :]
            if k % 2:
                yield
        copy = pltpu.make_async_copy(wt, wt_hbm, sems.at[len(copies)])
        copy.start()
        written.append(copy)

    written = []
    turning = turn_weights()
    pending = iter(())
    per = CHUNK_C // T
    for chunk in range(size // CHUNK_C):
        tiles = range(chunk * per, (chunk + 1) * per)
        center, first_tile = run[0] - origin, run[0] // T
        moves = gather_columns(
            tiles, range(27), xe, center, rel, first_tile, *buffers[chunk % 2]
        )
        for turn, _ in enumerate(moves):
            if turn % 3 == 2:
                next(pending, None)
            if chunk == 0 and make_wt and turn >= 4:
                next(turning, None)
        for _ in pending:
            pass
        if chunk == 0:
            if make_wt:
                for _ in turning:
                    pass
            else:
                copies[-1].wait()
        pending = product(chunk)
    for _ in pending:
        pass
    for copy in written:
        copy.wait()


def conv_run(feats, grads, low, high, neigh, weight, run, earlier, name):
    voxels, channels = feats.shape
    out = jax.ShapeDtypeStruct((voxels, channels), jnp.bfloat16)
    first, end = rows_needed(run)
    halos = ((low,) if first < 0 else ()) + ((high,) if end > voxels else ())
    turned = jax.ShapeDtypeStruct((2 * channels, 27 * channels), jnp.bfloat16)
    make_wt = not earlier
    operands = (feats, grads, neigh, weight if make_wt else earlier[2]) + halos + earlier[:2]
    size = run[1] - run[0]
    results = pl.pallas_call(
        functools.partial(conv_kernel, voxels, run, len(halos), make_wt),
        out_shape=(out, out) + ((turned,) if make_wt else ()),
        in_specs=[HBM] * len(operands),
        out_specs=(HBM, HBM) + ((HBM,) if make_wt else ()),
        input_output_aliases={4 + len(halos) + i: i for i in range(len(earlier[:2]))},
        scratch_shapes=[
            pltpu.VMEM(turned.shape, jnp.bfloat16),
        ]
        + ([pltpu.VMEM(weight.shape, jnp.bfloat16)] if make_wt else [])
        + [
            pltpu.VMEM((size, channels), jnp.bfloat16),
            pltpu.VMEM((size, channels), jnp.bfloat16),
            pltpu.VMEM((size + 2 * (LAYER + ROW), 2 * channels), jnp.bfloat16),
            pltpu.VMEM(neigh.shape, jnp.int32),
            pltpu.VMEM(neigh.shape, jnp.int32),
        ]
        + [pltpu.VMEM((27 * T, CHUNK_C), jnp.bfloat16)] * 4
        + [pltpu.SemaphoreType.DMA((8 + 2 * size // CHUNK_C,))],
        compiler_params=pltpu.CompilerParams(vmem_limit_bytes=FULL_VMEM_LIMIT),
        cost_estimate=pl.CostEstimate(
            flops=10**6 if make_wt else 10**10, bytes_accessed=10**4, transcendentals=0
        ),
        name=name,
    )(*operands)
    return tuple(results) + earlier[2:]


def sum_kernel(*refs):
    *parts, out_ref = refs
    terms = [ref[i] for ref in parts for i in range(ref.shape[0])]
    total = terms[0].astype(jnp.float32)
    for term in terms[1:]:
        total += term.astype(jnp.float32)
    total = total.astype(out_ref.dtype)
    for i in range(out_ref.shape[0]):
        out_ref[i] = total


def sum_parts(parts, copies, name):
    shape = parts[0].shape[1:]
    return pl.pallas_call(
        sum_kernel,
        out_shape=jax.ShapeDtypeStruct((copies,) + shape, parts[0].dtype),
        in_specs=[VMEM] * len(parts),
        out_specs=VMEM,
        compiler_params=pltpu.CompilerParams(vmem_limit_bytes=VMEM_LIMIT),
        cost_estimate=pl.CostEstimate(flops=10**6, bytes_accessed=10**4, transcendentals=0),
        name=name,
    )(*parts)


def widen_kernel(in_ref, *rest):
    out_ref = rest[-1]
    out_ref[...] = in_ref[...].astype(out_ref.dtype)


def widen(rows, own, count, earlier, name):
    half, channels = rows.shape
    block = (half // 2, channels)

    def place(i):
        side = own_side() if own else 1 - own_side()
        return side * 2 + i, 0

    return pl.pallas_call(
        widen_kernel,
        grid=(2,),
        in_specs=[pl.BlockSpec(block, lambda i: (i, 0))]
        + [pl.BlockSpec(memory_space=pl.ANY)] * len(earlier),
        out_specs=pl.BlockSpec(block, place),
        out_shape=jax.ShapeDtypeStruct((count, channels), jnp.float32),
        input_output_aliases={1 + i: i for i in range(len(earlier))},
        compiler_params=pltpu.CompilerParams(vmem_limit_bytes=VMEM_LIMIT),
        name=name,
    )(rows, *earlier)


def local(features, neighbours, weight, grad_out):
    feats, grads = features[0], grad_out[0]
    voxels, channels = feats.shape
    neigh = neighbours.reshape(27, voxels // T, T)
    space, dp = lax.axis_size("space"), lax.axis_size("dp")
    up = [(i, i + 1) for i in range(space - 1)]
    down = [(i + 1, i) for i in range(space - 1)]
    low = lax.ppermute(
        stack_layer(feats, grads, voxels // LAYER - 1, FULL_VMEM_LIMIT, "stack_last_layer"), "space", up
    )

    scale = 1.0 / math.sqrt(dp * space * voxels)
    share = -(-27 * channels // (16 * dp)) * 16
    inner = grad_w_inner(feats, grads, neigh)
    inner, later_feats, later_grads = lax.optimization_barrier((inner, feats, grads))
    first = stack_layer(later_feats, later_grads, 0, VMEM_LIMIT, "stack_first_layer")
    high = lax.ppermute(first, "space", down)
    inner, first = lax.optimization_barrier((inner, first))
    mine, other = grad_w_halo(feats, grads, low, neigh, inner, scale, share * dp)
    swap = [(i, i ^ 1) for i in range(dp)]
    alike = [list(range(0, dp, 2)), list(range(1, dp, 2))]
    other = lax.ppermute(other, "dp", swap)
    mine = sum_parts((mine[None], other[None]), 1, "sum_of_pair")
    mine, flat_weight = lax.optimization_barrier(
        (mine, weight.reshape(27 * channels, channels))
    )
    chunks = voxels // CHUNK_C
    ends = [0, chunks // 4 * CHUNK_C, chunks * 3 // 4 * CHUNK_C, voxels]

    def conv(done, part):
        run = (ends[part], ends[part + 1])
        name = "conv_run_%d" % part
        return conv_run(feats, grads, low, high, neigh, flat_weight, run, done, name)

    def exchange(pieces):
        return lax.all_to_all(pieces, "dp", 0, 0, axis_index_groups=alike, tiled=True)

    pieces = exchange(mine.reshape(dp // 2, share, channels))
    flat_weight, high = lax.optimization_barrier((flat_weight, high))
    done = conv((), 0)
    pieces, done = lax.optimization_barrier((pieces, done))
    pieces = lax.all_to_all(sum_parts((pieces,), space, "sum_for_space"), "space", 0, 0, tiled=True)
    done = conv(done, 1)
    pieces, done = lax.optimization_barrier((pieces, done))
    pieces = exchange(sum_parts((pieces,), dp // 2, "sum_for_dp"))
    done = conv(done, 2)
    pieces, done = lax.optimization_barrier((pieces, done))
    mine = pieces.reshape(dp // 2 * share, channels)
    other = lax.ppermute(mine, "dp", swap)
    grad_w = widen(mine, True, 27 * channels, (), "widen_own_half")
    grad_w = widen(other, False, 27 * channels, (grad_w,), "widen_other_half")
    conv_out, grad_in, _ = done
    return conv_out[None], grad_in[None], grad_w.reshape(27, channels, channels)


def solution(mesh):
    in_specs = (P("dp", "space", None), P("dp", None, "space"), P(), P("dp", "space", None))
    out_specs = (P("dp", "space", None), P("dp", "space", None), P())
    return jax.shard_map(local, mesh=mesh, in_specs=in_specs, out_specs=out_specs, check_vma=False)
```

```python
import functools
import math

import jax
import jax.numpy as jnp
from jax import lax
from jax.experimental import pallas as pl
from jax.experimental.pallas import tpu as pltpu
from jax.sharding import PartitionSpec as P

PSIDE = 64
ROW = PSIDE // 4
LAYER = PSIDE * ROW
T = 128
CHUNK_W = 256
CHUNK_C = 256
VMEM_LIMIT = 28 * 1024 * 1024
FULL_VMEM_LIMIT = 58 * 1024 * 1024
VMEM = pl.BlockSpec(memory_space=pltpu.VMEM)
HBM = pl.BlockSpec(memory_space=pltpu.HBM)


def offset_of(k):
    return k // 9 - 1, (k // 3) % 3 - 1, k % 3 - 1


def row_in_scene_window(neighbours, shift):
    return jnp.where(neighbours >= 0, (neighbours - shift) & (T - 1), -1)


def one_hot(hit):
    return jnp.where(hit, jnp.ones((), jnp.bfloat16), jnp.zeros((), jnp.bfloat16))


def own_side():
    return lax.bitwise_and(lax.axis_index("dp"), 1).astype(jnp.int32)


def fill_edges(xe):
    edge = jnp.zeros((ROW, xe.shape[1]), jnp.bfloat16)
    xe[0:ROW, :] = edge
    xe[xe.shape[0] - ROW :, :] = edge


def one_hot_columns(rel, k, tile):
    spot = lax.broadcasted_iota(jnp.int32, (T, T), 0).astype(jnp.bfloat16)
    row = jnp.broadcast_to(rel[k, tile : tile + 1, :], (ROW, T)).astype(jnp.bfloat16)
    return one_hot(jnp.concatenate([row] * (T // ROW), axis=0) == spot)


def gather_columns(tiles, ks, xe, origin, rel, first_tile, to_f, to_g):
    channels = xe.shape[1] // 2
    none = jnp.zeros((T, T), jnp.bfloat16)
    kept = []

    def put(k, cols, part):
        to_f[k * T : (k + 1) * T, cols] = part[:channels]
        to_g[k * T : (k + 1) * T, cols] = part[channels:]

    def put_dot(source, right, places):
        picked = jnp.dot(source, right, preferred_element_type=jnp.float32).astype(jnp.bfloat16)
        for q, (k, cols) in enumerate(places):
            put(k, cols, picked[:, q * T : (q + 1) * T])

    for h, tile in enumerate(tiles):
        cols = slice(h * T, (h + 1) * T)
        for dz, dy in sorted({offset_of(k)[:2] for k in ks}):
            some = [k for k in ks if offset_of(k)[:2] == (dz, dy)]
            start = origin + tile * T + ROW * dy + LAYER * dz
            window = xe[start : start + T, :].T
            if 13 in some:
                put(13, cols, window)
                some.remove(13)
            if len(some) > 1:
                pair = (some.pop(0), some.pop())
                right = [one_hot_columns(rel, k, first_tile + tile) for k in pair]
                put_dot(window, jnp.concatenate(right, axis=1), [(k, cols) for k in pair])
            for k in some:
                kept.append((k, cols, window, one_hot_columns(rel, k, first_tile + tile)))
            if len(kept) == 2:
                (k0, cols0, window0, hot0), (k1, cols1, window1, hot1) = kept
                right = jnp.concatenate(
                    [
                        jnp.concatenate([hot0, none], axis=1),
                        jnp.concatenate([none, hot1], axis=1),
                    ],
                    axis=0,
                )
                both = jnp.concatenate([window0, window1], axis=1)
                put_dot(both, right, [(k0, cols0), (k1, cols1)])
                kept = []
            yield
    for k, cols, window, hot in kept:
        put_dot(window, hot, [(k, cols)])


def weight_terms(chunks, ks_of, origin, f_ref, g_ref, xe, rel, buffers, acc):
    def product(chunk):
        here = slice(chunk * CHUNK_W, (chunk + 1) * CHUNK_W)
        picked_f, picked_g = buffers[chunk % 2]
        ks = ks_of(chunk)
        left_f, left_g = f_ref[here, :].T, g_ref[here, :].T
        if 13 in ks:
            picked_g[13 * T :, :] = left_g
        for left, picked, side, end in ((left_g, picked_f, 0, 13), (left_f, picked_g, 13, 14)):
            for group in (range(0, 4), range(4, 8), range(8, end)):
                group = [k for k in group if k in ks]
                if group:
                    span = slice(group[0] * T, (group[-1] + 1) * T)
                    to = slice((side + group[0]) * T, (side + group[-1] + 1) * T)
                    acc[:, to] += lax.dot_general(
                        left,
                        picked[span, :],
                        (((1,), (1,)), ((), ())),
                        preferred_element_type=jnp.float32,
                    )
                    yield

    pending = iter(())
    per = CHUNK_W // T
    for chunk in chunks:
        tiles = range(chunk * per, (chunk + 1) * per)
        ks = [k for k in ks_of(chunk) if k < 13]
        for _ in gather_columns(tiles, ks, xe, origin, rel, 0, *buffers[chunk % 2]):
            next(pending, None)
        for _ in pending:
            pass
        pending = product(chunk)
    for _ in pending:
        pass


def weight_inner_kernel(voxels, f_ref, g_ref, nb_ref, acc, xe, rel, gf, gg, gf2, gg2):
    channels = f_ref.shape[1]
    xe[ROW : ROW + voxels, 0:channels] = f_ref[...]
    xe[ROW : ROW + voxels, channels:] = g_ref[...]
    fill_edges(xe)
    for k in range(13):
        rel[k, :, :] = row_in_scene_window(nb_ref[k], ROW * offset_of(k)[1])
    acc[...] = jnp.zeros_like(acc)

    def ks_of(chunk):
        return range(9 if chunk < LAYER // CHUNK_W else 0, 14)

    chunks = range(voxels // CHUNK_W)
    weight_terms(chunks, ks_of, ROW, f_ref, g_ref, xe, rel, ((gf, gg), (gf2, gg2)), acc)


def weight_halo_kernel(scale, f_ref, g_ref, low_ref, nb_ref, in_ref, mine_ref, other_ref, xe, rel, gf, gg, gf2, gg2, acc, out_ref):
    channels = f_ref.shape[1]
    xe[ROW : ROW + LAYER, 0:channels] = low_ref[0]
    xe[ROW : ROW + LAYER, channels:] = low_ref[1]
    fill_edges(xe)
    for k in range(9):
        rel[k, :, :] = row_in_scene_window(nb_ref[k, 0 : LAYER // T, :], ROW * offset_of(k)[1])
    acc[...] = jnp.zeros_like(acc)
    chunks = range(LAYER // CHUNK_W)
    buffers = ((gf, gg), (gf2, gg2))
    weight_terms(chunks, lambda _: range(9), ROW + LAYER, f_ref, g_ref, xe, rel, buffers, acc)

    def total(block, touched):
        span = slice(block * T, (block + 1) * T)
        return (in_ref[:, span] + acc[:, span] if touched else in_ref[:, span]) * scale

    for k in range(13):
        out_ref[k * T : (k + 1) * T, :] = total(k, k < 9).T.astype(out_ref.dtype)
    for k in range(14):
        out_ref[(26 - k) * T : (27 - k) * T, :] = total(13 + k, k < 9).astype(out_ref.dtype)
    if out_ref.shape[0] > 27 * T:
        out_ref[27 * T :, :] = jnp.zeros((out_ref.shape[0] - 27 * T, out_ref.shape[1]), out_ref.dtype)
    half = out_ref.shape[0] // 2
    parity = own_side()
    mine_ref[...] = out_ref[pl.ds(pl.multiple_of(parity * half, 16), half), :]
    other_ref[...] = out_ref[pl.ds(pl.multiple_of((1 - parity) * half, 16), half), :]


def weight_scratch(rows, channels):
    return [
        pltpu.VMEM((rows + 2 * ROW, 2 * channels), jnp.bfloat16),
        pltpu.VMEM((13, rows // T, T), jnp.int32),
    ] + [
        pltpu.VMEM((13 * T, CHUNK_W), jnp.bfloat16),
        pltpu.VMEM((14 * T, CHUNK_W), jnp.bfloat16),
    ] * 2


def grad_w_inner(feats, grads, neigh):
    voxels, channels = feats.shape
    return pl.pallas_call(
        functools.partial(weight_inner_kernel, voxels),
        out_shape=jax.ShapeDtypeStruct((channels, 27 * T), jnp.float32),
        in_specs=[VMEM] * 3,
        out_specs=VMEM,
        scratch_shapes=weight_scratch(voxels, channels),
        compiler_params=pltpu.CompilerParams(vmem_limit_bytes=VMEM_LIMIT),
        cost_estimate=pl.CostEstimate(flops=8 * 10**9, bytes_accessed=4 * 10**6, transcendentals=0),
        name="weight_gradient_inner",
    )(feats, grads, neigh)


def grad_w_halo(feats, grads, low, neigh, partial, scale, rows):
    channels = feats.shape[1]
    out = jax.ShapeDtypeStruct((rows // 2, channels), jnp.bfloat16)
    return pl.pallas_call(
        functools.partial(weight_halo_kernel, scale),
        out_shape=(out, out),
        in_specs=[VMEM] * 5,
        out_specs=(VMEM, VMEM),
        scratch_shapes=weight_scratch(LAYER, channels)
        + [
            pltpu.VMEM((channels, 27 * T), jnp.float32),
            pltpu.VMEM((rows, channels), jnp.bfloat16),
        ],
        compiler_params=pltpu.CompilerParams(vmem_limit_bytes=VMEM_LIMIT),
        cost_estimate=pl.CostEstimate(flops=10**6, bytes_accessed=10**4, transcendentals=0),
        name="weight_gradient_halo",
    )(feats, grads, low, neigh, partial)


def stack_kernel(f_ref, g_ref, out_ref):
    out_ref[0] = f_ref[...]
    out_ref[1] = g_ref[...]


def stack_layer(feats, grads, layer, vmem, name):
    channels = feats.shape[1]
    block = pl.BlockSpec((LAYER, channels), lambda i: (layer, 0))
    return pl.pallas_call(
        stack_kernel,
        grid=(1,),
        out_shape=jax.ShapeDtypeStruct((2, LAYER, channels), jnp.bfloat16),
        in_specs=[block, block],
        out_specs=VMEM,
        compiler_params=pltpu.CompilerParams(vmem_limit_bytes=vmem),
        name=name,
    )(feats, grads)


def rows_needed(run):
    first, end = run
    return (
        first - LAYER - (ROW if first % LAYER else 0),
        end + LAYER + (ROW if end % LAYER else 0),
    )


def conv_kernel(voxels, run, halos, make_wt, f_ref, g_ref, nb_ref, w_hbm, *rest):
    halos = list(rest[:halos])
    if make_wt:
        conv_hbm, gin_hbm, wt_hbm, wt, w_ref, *scratch = rest[-15:]
    else:
        conv_hbm, gin_hbm, wt, *scratch = rest[-13:]
    conv_ref, gin_ref, xe, nb, rel, gf, gg, gf2, gg2, sems = scratch
    channels = f_ref.shape[1]
    size = run[1] - run[0]

    origin = run[0] - LAYER - ROW
    low, high = rows_needed(run)
    main = (max(low, 0), min(high, voxels))
    rows = pl.ds(main[0], main[1] - main[0])
    to = pl.ds(main[0] - origin, main[1] - main[0])
    copies = [
        (nb_ref, nb),
        (f_ref.at[rows, :], xe.at[to, pl.ds(0, channels)]),
        (g_ref.at[rows, :], xe.at[to, pl.ds(channels, channels)]),
    ]
    parts = []
    if low < 0:
        parts.append((pl.ds(LAYER + low, -low), pl.ds(low - origin, -low)))
    if high > voxels:
        parts.append((pl.ds(0, high - voxels), pl.ds(voxels - origin, high - voxels)))
    for halo, (rows, to) in zip(halos, parts):
        for side in range(2):
            lanes = pl.ds(side * channels, channels)
            copies.append((halo.at[side, rows, :], xe.at[to, lanes]))
    early = len(copies)
    copies.append((w_hbm, w_ref if make_wt else wt))
    copies = [
        pltpu.make_async_copy(source, target, sems.at[i])
        for i, (source, target) in enumerate(copies)
    ]
    for copy in copies:
        copy.start()
    edge = jnp.zeros((ROW, 2 * channels), jnp.bfloat16)
    if low - origin:
        xe[0:ROW, :] = edge
    if high - origin < xe.shape[0]:
        xe[xe.shape[0] - ROW :, :] = edge
    copies[0].wait()
    for k in range(27):
        rel[k, :, :] = row_in_scene_window(nb[k], ROW * offset_of(k)[1])
    for copy in copies[1:early]:
        copy.wait()

    buffers = ((gf, gg), (gf2, gg2))

    def product(chunk):
        rows = slice(chunk * CHUNK_C, (chunk + 1) * CHUNK_C)
        kernels = (slice(0, channels), slice(channels, 2 * channels))
        outs = ((conv_ref, conv_hbm), (gin_ref, gin_hbm))
        for (out, out_hbm), picked, side in zip(outs, buffers[chunk % 2], kernels):
            total = None
            for part in range(3):
                span = slice(part * 9 * T, (part + 1) * 9 * T)
                term = jnp.dot(wt[side, span], picked[span, :], preferred_element_type=jnp.float32)
                total = term if total is None else total + term
                if part == 2:
                    out[rows, :] = total.T.astype(jnp.bfloat16)
                    copy = pltpu.make_async_copy(
                        out.at[rows, :],
                        out_hbm.at[pl.ds(run[0] + chunk * CHUNK_C, CHUNK_C), :],
                        sems.at[len(copies) + len(written)],
                    )
                    copy.start()
                    written.append(copy)
                yield

    def turn_weights():
        copies[-1].wait()
        for k in range(27):
            span = slice(k * T, (k + 1) * T)
            wt[0:channels, span] = w_ref[span, :].T
            wt[channels:, span] = w_ref[(26 - k) * T : (27 - k) * T, :]
            if k % 2:
                yield
        copy = pltpu.make_async_copy(wt, wt_hbm, sems.at[len(copies)])
        copy.start()
        written.append(copy)

    written = []
    turning = turn_weights()
    pending = iter(())
    per = CHUNK_C // T
    for chunk in range(size // CHUNK_C):
        tiles = range(chunk * per, (chunk + 1) * per)
        center, first_tile = run[0] - origin, run[0] // T
        moves = gather_columns(
            tiles, range(27), xe, center, rel, first_tile, *buffers[chunk % 2]
        )
        for turn, _ in enumerate(moves):
            if turn % 3 == 2:
                next(pending, None)
            if chunk == 0 and make_wt and turn >= 4:
                next(turning, None)
        for _ in pending:
            pass
        if chunk == 0:
            if make_wt:
                for _ in turning:
                    pass
            else:
                copies[-1].wait()
        pending = product(chunk)
    for _ in pending:
        pass
    for copy in written:
        copy.wait()


def conv_run(feats, grads, low, high, neigh, weight, run, earlier, name):
    voxels, channels = feats.shape
    out = jax.ShapeDtypeStruct((voxels, channels), jnp.bfloat16)
    first, end = rows_needed(run)
    halos = ((low,) if first < 0 else ()) + ((high,) if end > voxels else ())
    turned = jax.ShapeDtypeStruct((2 * channels, 27 * channels), jnp.bfloat16)
    make_wt = not earlier
    operands = (feats, grads, neigh, weight if make_wt else earlier[2]) + halos + earlier[:2]
    size = run[1] - run[0]
    results = pl.pallas_call(
        functools.partial(conv_kernel, voxels, run, len(halos), make_wt),
        out_shape=(out, out) + ((turned,) if make_wt else ()),
        in_specs=[HBM] * len(operands),
        out_specs=(HBM, HBM) + ((HBM,) if make_wt else ()),
        input_output_aliases={4 + len(halos) + i: i for i in range(len(earlier[:2]))},
        scratch_shapes=[
            pltpu.VMEM(turned.shape, jnp.bfloat16),
        ]
        + ([pltpu.VMEM(weight.shape, jnp.bfloat16)] if make_wt else [])
        + [
            pltpu.VMEM((size, channels), jnp.bfloat16),
            pltpu.VMEM((size, channels), jnp.bfloat16),
            pltpu.VMEM((size + 2 * (LAYER + ROW), 2 * channels), jnp.bfloat16),
            pltpu.VMEM(neigh.shape, jnp.int32),
            pltpu.VMEM(neigh.shape, jnp.int32),
        ]
        + [pltpu.VMEM((27 * T, CHUNK_C), jnp.bfloat16)] * 4
        + [pltpu.SemaphoreType.DMA((8 + 2 * size // CHUNK_C,))],
        compiler_params=pltpu.CompilerParams(vmem_limit_bytes=FULL_VMEM_LIMIT),
        cost_estimate=pl.CostEstimate(
            flops=10**6 if make_wt else 10**10, bytes_accessed=10**4, transcendentals=0
        ),
        name=name,
    )(*operands)
    return tuple(results) + earlier[2:]


def sum_kernel(*refs):
    *parts, out_ref = refs
    terms = [ref[i] for ref in parts for i in range(ref.shape[0])]
    total = terms[0].astype(jnp.float32)
    for term in terms[1:]:
        total += term.astype(jnp.float32)
    total = total.astype(out_ref.dtype)
    for i in range(out_ref.shape[0]):
        out_ref[i] = total


def sum_parts(parts, copies, name):
    shape = parts[0].shape[1:]
    return pl.pallas_call(
        sum_kernel,
        out_shape=jax.ShapeDtypeStruct((copies,) + shape, parts[0].dtype),
        in_specs=[VMEM] * len(parts),
        out_specs=VMEM,
        compiler_params=pltpu.CompilerParams(vmem_limit_bytes=VMEM_LIMIT),
        cost_estimate=pl.CostEstimate(flops=10**6, bytes_accessed=10**4, transcendentals=0),
        name=name,
    )(*parts)


def widen_kernel(in_ref, *rest):
    out_ref = rest[-1]
    out_ref[...] = in_ref[...].astype(out_ref.dtype)


def widen(rows, own, count, earlier, name):
    half, channels = rows.shape
    block = (half // 2, channels)

    def place(i):
        side = own_side() if own else 1 - own_side()
        return side * 2 + i, 0

    return pl.pallas_call(
        widen_kernel,
        grid=(2,),
        in_specs=[pl.BlockSpec(block, lambda i: (i, 0))]
        + [pl.BlockSpec(memory_space=pl.ANY)] * len(earlier),
        out_specs=pl.BlockSpec(block, place),
        out_shape=jax.ShapeDtypeStruct((count, channels), jnp.float32),
        input_output_aliases={1 + i: i for i in range(len(earlier))},
        compiler_params=pltpu.CompilerParams(vmem_limit_bytes=VMEM_LIMIT),
        name=name,
    )(rows, *earlier)


def local(features, neighbours, weight, grad_out):
    feats, grads = features[0], grad_out[0]
    voxels, channels = feats.shape
    neigh = neighbours.reshape(27, voxels // T, T)
    space, dp = lax.axis_size("space"), lax.axis_size("dp")
    up = [(i, i + 1) for i in range(space - 1)]
    down = [(i + 1, i) for i in range(space - 1)]
    low = lax.ppermute(
        stack_layer(feats, grads, voxels // LAYER - 1, FULL_VMEM_LIMIT, "stack_last_layer"), "space", up
    )
    high = lax.ppermute(
        stack_layer(feats, grads, 0, VMEM_LIMIT, "stack_first_layer"), "space", down
    )

    scale = 1.0 / math.sqrt(dp * space * voxels)
    share = -(-27 * channels // (16 * dp)) * 16
    inner = grad_w_inner(feats, grads, neigh)
    mine, other = grad_w_halo(feats, grads, low, neigh, inner, scale, share * dp)
    mine, other, high = lax.optimization_barrier((mine, other, high))
    swap = [(i, i ^ 1) for i in range(dp)]
    alike = [list(range(0, dp, 2)), list(range(1, dp, 2))]
    other = lax.ppermute(other, "dp", swap)
    mine = sum_parts((mine[None], other[None]), 1, "sum_of_pair")
    mine, flat_weight = lax.optimization_barrier(
        (mine, weight.reshape(27 * channels, channels))
    )
    chunks = voxels // CHUNK_C
    ends = [0, chunks // 4 * CHUNK_C, chunks * 3 // 4 * CHUNK_C, voxels]

    def conv(done, part):
        run = (ends[part], ends[part + 1])
        name = "conv_run_%d" % part
        return conv_run(feats, grads, low, high, neigh, flat_weight, run, done, name)

    def exchange(pieces):
        return lax.all_to_all(pieces, "dp", 0, 0, axis_index_groups=alike, tiled=True)

    pieces = exchange(mine.reshape(dp // 2, share, channels))
    done = conv((), 0)
    pieces, done = lax.optimization_barrier((pieces, done))
    pieces = lax.all_to_all(sum_parts((pieces,), space, "sum_for_space"), "space", 0, 0, tiled=True)
    done = conv(done, 1)
    pieces, done = lax.optimization_barrier((pieces, done))
    pieces = exchange(sum_parts((pieces,), dp // 2, "sum_for_dp"))
    done = conv(done, 2)
    pieces, done = lax.optimization_barrier((pieces, done))
    mine = pieces.reshape(dp // 2 * share, channels)
    other = lax.ppermute(mine, "dp", swap)
    grad_w = widen(mine, True, 27 * channels, (), "widen_own_half")
    grad_w = widen(other, False, 27 * channels, (grad_w,), "widen_other_half")
    conv_out, grad_in, _ = done
    return conv_out[None], grad_in[None], grad_w.reshape(27, channels, channels)


def solution(mesh):
    in_specs = (P("dp", "space", None), P("dp", None, "space"), P(), P("dp", "space", None))
    out_specs = (P("dp", "space", None), P("dp", "space", None), P())
    return jax.shard_map(local, mesh=mesh, in_specs=in_specs, out_specs=out_specs, check_vma=False)
```

```python
import functools
import math

import jax
import jax.numpy as jnp
from jax import lax
from jax.experimental import pallas as pl
from jax.experimental.pallas import tpu as pltpu
from jax.sharding import PartitionSpec as P

PSIDE = 64
ROW = PSIDE // 4
LAYER = PSIDE * ROW
T = 128
CHUNK_W = 256
CHUNK_C = 256
VMEM_LIMIT = 28 * 1024 * 1024
FULL_VMEM_LIMIT = 58 * 1024 * 1024
VMEM = pl.BlockSpec(memory_space=pltpu.VMEM)
HBM = pl.BlockSpec(memory_space=pltpu.HBM)


def offset_of(k):
    return k // 9 - 1, (k // 3) % 3 - 1, k % 3 - 1


def row_in_scene_window(neighbours, shift):
    return jnp.where(neighbours >= 0, (neighbours - shift) & (T - 1), -1)


def one_hot(hit):
    return jnp.where(hit, jnp.ones((), jnp.bfloat16), jnp.zeros((), jnp.bfloat16))


def own_side():
    return lax.bitwise_and(lax.axis_index("dp"), 1).astype(jnp.int32)


def fill_edges(xe):
    edge = jnp.zeros((ROW, xe.shape[1]), jnp.bfloat16)
    xe[0:ROW, :] = edge
    xe[xe.shape[0] - ROW :, :] = edge


def one_hot_columns(rel, k, tile):
    spot = lax.broadcasted_iota(jnp.int32, (T, T), 0).astype(jnp.bfloat16)
    row = jnp.broadcast_to(rel[k, tile : tile + 1, :], (ROW, T)).astype(jnp.bfloat16)
    return one_hot(jnp.concatenate([row] * (T // ROW), axis=0) == spot)


def gather_columns(tiles, ks, xe, origin, rel, first_tile, to_f, to_g):
    channels = xe.shape[1] // 2
    none = jnp.zeros((T, T), jnp.bfloat16)
    kept = []

    def put(k, cols, part):
        to_f[k * T : (k + 1) * T, cols] = part[:channels]
        to_g[k * T : (k + 1) * T, cols] = part[channels:]

    def put_dot(source, right, places):
        picked = jnp.dot(source, right, preferred_element_type=jnp.float32).astype(jnp.bfloat16)
        for q, (k, cols) in enumerate(places):
            put(k, cols, picked[:, q * T : (q + 1) * T])

    for h, tile in enumerate(tiles):
        cols = slice(h * T, (h + 1) * T)
        for dz, dy in sorted({offset_of(k)[:2] for k in ks}):
            some = [k for k in ks if offset_of(k)[:2] == (dz, dy)]
            start = origin + tile * T + ROW * dy + LAYER * dz
            window = xe[start : start + T, :].T
            if 13 in some:
                put(13, cols, window)
                some.remove(13)
            if len(some) > 1:
                pair = (some.pop(0), some.pop())
                right = [one_hot_columns(rel, k, first_tile + tile) for k in pair]
                put_dot(window, jnp.concatenate(right, axis=1), [(k, cols) for k in pair])
            for k in some:
                kept.append((k, cols, window, one_hot_columns(rel, k, first_tile + tile)))
            if len(kept) == 2:
                (k0, cols0, window0, hot0), (k1, cols1, window1, hot1) = kept
                right = jnp.concatenate(
                    [
                        jnp.concatenate([hot0, none], axis=1),
                        jnp.concatenate([none, hot1], axis=1),
                    ],
                    axis=0,
                )
                both = jnp.concatenate([window0, window1], axis=1)
                put_dot(both, right, [(k0, cols0), (k1, cols1)])
                kept = []
            yield
    for k, cols, window, hot in kept:
        put_dot(window, hot, [(k, cols)])


def weight_terms(chunks, ks_of, origin, f_ref, g_ref, xe, rel, buffers, acc):
    def product(chunk):
        here = slice(chunk * CHUNK_W, (chunk + 1) * CHUNK_W)
        picked_f, picked_g = buffers[chunk % 2]
        ks = ks_of(chunk)
        left_f, left_g = f_ref[here, :].T, g_ref[here, :].T
        if 13 in ks:
            picked_g[13 * T :, :] = left_g
        for left, picked, side, end in ((left_g, picked_f, 0, 13), (left_f, picked_g, 13, 14)):
            for group in (range(0, 4), range(4, 8), range(8, end)):
                group = [k for k in group if k in ks]
                if group:
                    span = slice(group[0] * T, (group[-1] + 1) * T)
                    to = slice((side + group[0]) * T, (side + group[-1] + 1) * T)
                    acc[:, to] += lax.dot_general(
                        left,
                        picked[span, :],
                        (((1,), (1,)), ((), ())),
                        preferred_element_type=jnp.float32,
                    )
                    yield

    pending = iter(())
    per = CHUNK_W // T
    for chunk in chunks:
        tiles = range(chunk * per, (chunk + 1) * per)
        ks = [k for k in ks_of(chunk) if k < 13]
        for _ in gather_columns(tiles, ks, xe, origin, rel, 0, *buffers[chunk % 2]):
            next(pending, None)
        for _ in pending:
            pass
        pending = product(chunk)
    for _ in pending:
        pass


def weight_inner_kernel(voxels, f_ref, g_ref, nb_ref, acc, xe, rel, gf, gg, gf2, gg2):
    channels = f_ref.shape[1]
    xe[ROW : ROW + voxels, 0:channels] = f_ref[...]
    xe[ROW : ROW + voxels, channels:] = g_ref[...]
    fill_edges(xe)
    for k in range(13):
        rel[k, :, :] = row_in_scene_window(nb_ref[k], ROW * offset_of(k)[1])
    acc[...] = jnp.zeros_like(acc)

    def ks_of(chunk):
        return range(9 if chunk < LAYER // CHUNK_W else 0, 14)

    chunks = range(voxels // CHUNK_W)
    weight_terms(chunks, ks_of, ROW, f_ref, g_ref, xe, rel, ((gf, gg), (gf2, gg2)), acc)


def weight_halo_kernel(scale, f_ref, g_ref, low_ref, nb_ref, in_ref, mine_ref, other_ref, xe, rel, gf, gg, gf2, gg2, acc, out_ref):
    channels = f_ref.shape[1]
    xe[ROW : ROW + LAYER, 0:channels] = low_ref[0]
    xe[ROW : ROW + LAYER, channels:] = low_ref[1]
    fill_edges(xe)
    for k in range(9):
        rel[k, :, :] = row_in_scene_window(nb_ref[k, 0 : LAYER // T, :], ROW * offset_of(k)[1])
    acc[...] = jnp.zeros_like(acc)
    chunks = range(LAYER // CHUNK_W)
    buffers = ((gf, gg), (gf2, gg2))
    weight_terms(chunks, lambda _: range(9), ROW + LAYER, f_ref, g_ref, xe, rel, buffers, acc)

    def total(block, touched):
        span = slice(block * T, (block + 1) * T)
        return (in_ref[:, span] + acc[:, span] if touched else in_ref[:, span]) * scale

    for k in range(13):
        out_ref[k * T : (k + 1) * T, :] = total(k, k < 9).T.astype(out_ref.dtype)
    for k in range(14):
        out_ref[(26 - k) * T : (27 - k) * T, :] = total(13 + k, k < 9).astype(out_ref.dtype)
    if out_ref.shape[0] > 27 * T:
        out_ref[27 * T :, :] = jnp.zeros((out_ref.shape[0] - 27 * T, out_ref.shape[1]), out_ref.dtype)
    half = out_ref.shape[0] // 2
    parity = own_side()
    mine_ref[...] = out_ref[pl.ds(pl.multiple_of(parity * half, 16), half), :]
    other_ref[...] = out_ref[pl.ds(pl.multiple_of((1 - parity) * half, 16), half), :]


def weight_scratch(rows, channels):
    return [
        pltpu.VMEM((rows + 2 * ROW, 2 * channels), jnp.bfloat16),
        pltpu.VMEM((13, rows // T, T), jnp.int32),
    ] + [
        pltpu.VMEM((13 * T, CHUNK_W), jnp.bfloat16),
        pltpu.VMEM((14 * T, CHUNK_W), jnp.bfloat16),
    ] * 2


def grad_w_inner(feats, grads, neigh):
    voxels, channels = feats.shape
    return pl.pallas_call(
        functools.partial(weight_inner_kernel, voxels),
        out_shape=jax.ShapeDtypeStruct((channels, 27 * T), jnp.float32),
        in_specs=[VMEM] * 3,
        out_specs=VMEM,
        scratch_shapes=weight_scratch(voxels, channels),
        compiler_params=pltpu.CompilerParams(vmem_limit_bytes=VMEM_LIMIT),
        cost_estimate=pl.CostEstimate(flops=8 * 10**9, bytes_accessed=4 * 10**6, transcendentals=0),
        name="weight_gradient_inner",
    )(feats, grads, neigh)


def grad_w_halo(feats, grads, low, neigh, partial, scale, rows):
    channels = feats.shape[1]
    out = jax.ShapeDtypeStruct((rows // 2, channels), jnp.bfloat16)
    return pl.pallas_call(
        functools.partial(weight_halo_kernel, scale),
        out_shape=(out, out),
        in_specs=[VMEM] * 5,
        out_specs=(VMEM, VMEM),
        scratch_shapes=weight_scratch(LAYER, channels)
        + [
            pltpu.VMEM((channels, 27 * T), jnp.float32),
            pltpu.VMEM((rows, channels), jnp.bfloat16),
        ],
        compiler_params=pltpu.CompilerParams(vmem_limit_bytes=VMEM_LIMIT),
        cost_estimate=pl.CostEstimate(flops=10**6, bytes_accessed=10**4, transcendentals=0),
        name="weight_gradient_halo",
    )(feats, grads, low, neigh, partial)


def stack_kernel(f_ref, g_ref, out_ref):
    out_ref[0] = f_ref[...]
    out_ref[1] = g_ref[...]


def stack_by_copies_kernel(layer, f_ref, g_ref, out_ref, held, sems):
    rows = pl.ds(layer * LAYER, LAYER)
    copies = []
    for i, ref in enumerate((f_ref, g_ref)):
        copies.append(
            (
                pltpu.make_async_copy(ref.at[rows, :], held.at[i], sems.at[i]),
                pltpu.make_async_copy(held.at[i], out_ref.at[i], sems.at[2 + i]),
            )
        )
    for fetch, _ in copies:
        fetch.start()
    for fetch, store in copies:
        fetch.wait()
        store.start()
    for _, store in copies:
        store.wait()


def stack_layer(feats, grads, layer, name):
    channels = feats.shape[1]
    block = pl.BlockSpec((LAYER, channels), lambda i: (layer, 0))
    return pl.pallas_call(
        stack_kernel,
        grid=(1,),
        out_shape=jax.ShapeDtypeStruct((2, LAYER, channels), jnp.bfloat16),
        in_specs=[block, block],
        out_specs=VMEM,
        compiler_params=pltpu.CompilerParams(vmem_limit_bytes=VMEM_LIMIT),
        name=name,
    )(feats, grads)


def stack_layer_by_copies(feats, grads, layer, name):
    channels = feats.shape[1]
    shape = (2, LAYER, channels)
    return pl.pallas_call(
        functools.partial(stack_by_copies_kernel, layer),
        out_shape=jax.ShapeDtypeStruct(shape, jnp.bfloat16),
        in_specs=[HBM, HBM],
        out_specs=HBM,
        scratch_shapes=[pltpu.VMEM(shape, jnp.bfloat16), pltpu.SemaphoreType.DMA((4,))],
        compiler_params=pltpu.CompilerParams(vmem_limit_bytes=FULL_VMEM_LIMIT),
        name=name,
    )(feats, grads)


def rows_needed(run):
    first, end = run
    return (
        first - LAYER - (ROW if first % LAYER else 0),
        end + LAYER + (ROW if end % LAYER else 0),
    )


def conv_kernel(voxels, run, halos, make_wt, f_ref, g_ref, nb_ref, w_hbm, *rest):
    halos = list(rest[:halos])
    if make_wt:
        conv_hbm, gin_hbm, wt_hbm, wt, w_ref, *scratch = rest[-15:]
    else:
        conv_hbm, gin_hbm, wt, *scratch = rest[-13:]
    conv_ref, gin_ref, xe, nb, rel, gf, gg, gf2, gg2, sems = scratch
    channels = f_ref.shape[1]
    size = run[1] - run[0]

    origin = run[0] - LAYER - ROW
    low, high = rows_needed(run)
    main = (max(low, 0), min(high, voxels))
    rows = pl.ds(main[0], main[1] - main[0])
    to = pl.ds(main[0] - origin, main[1] - main[0])
    copies = [
        (nb_ref, nb),
        (f_ref.at[rows, :], xe.at[to, pl.ds(0, channels)]),
        (g_ref.at[rows, :], xe.at[to, pl.ds(channels, channels)]),
    ]
    parts = []
    if low < 0:
        parts.append((pl.ds(LAYER + low, -low), pl.ds(low - origin, -low)))
    if high > voxels:
        parts.append((pl.ds(0, high - voxels), pl.ds(voxels - origin, high - voxels)))
    for halo, (rows, to) in zip(halos, parts):
        for side in range(2):
            lanes = pl.ds(side * channels, channels)
            copies.append((halo.at[side, rows, :], xe.at[to, lanes]))
    early = len(copies)
    copies.append((w_hbm, w_ref if make_wt else wt))
    copies = [
        pltpu.make_async_copy(source, target, sems.at[i])
        for i, (source, target) in enumerate(copies)
    ]
    for copy in copies:
        copy.start()
    edge = jnp.zeros((ROW, 2 * channels), jnp.bfloat16)
    if low - origin:
        xe[0:ROW, :] = edge
    if high - origin < xe.shape[0]:
        xe[xe.shape[0] - ROW :, :] = edge
    copies[0].wait()
    for k in range(27):
        rel[k, :, :] = row_in_scene_window(nb[k], ROW * offset_of(k)[1])
    for copy in copies[1:early]:
        copy.wait()

    buffers = ((gf, gg), (gf2, gg2))

    def product(chunk):
        rows = slice(chunk * CHUNK_C, (chunk + 1) * CHUNK_C)
        kernels = (slice(0, channels), slice(channels, 2 * channels))
        outs = ((conv_ref, conv_hbm), (gin_ref, gin_hbm))
        for (out, out_hbm), picked, side in zip(outs, buffers[chunk % 2], kernels):
            total = None
            for part in range(3):
                span = slice(part * 9 * T, (part + 1) * 9 * T)
                term = jnp.dot(wt[side, span], picked[span, :], preferred_element_type=jnp.float32)
                total = term if total is None else total + term
                if part == 2:
                    out[rows, :] = total.T.astype(jnp.bfloat16)
                    copy = pltpu.make_async_copy(
                        out.at[rows, :],
                        out_hbm.at[pl.ds(run[0] + chunk * CHUNK_C, CHUNK_C), :],
                        sems.at[len(copies) + len(written)],
                    )
                    copy.start()
                    written.append(copy)
                yield

    def turn_weights():
        copies[-1].wait()
        for k in range(27):
            span = slice(k * T, (k + 1) * T)
            wt[0:channels, span] = w_ref[span, :].T
            wt[channels:, span] = w_ref[(26 - k) * T : (27 - k) * T, :]
            if k % 2:
                yield
        copy = pltpu.make_async_copy(wt, wt_hbm, sems.at[len(copies)])
        copy.start()
        written.append(copy)

    written = []
    turning = turn_weights()
    pending = iter(())
    per = CHUNK_C // T
    for chunk in range(size // CHUNK_C):
        tiles = range(chunk * per, (chunk + 1) * per)
        center, first_tile = run[0] - origin, run[0] // T
        moves = gather_columns(
            tiles, range(27), xe, center, rel, first_tile, *buffers[chunk % 2]
        )
        for turn, _ in enumerate(moves):
            if turn % 3 == 2:
                next(pending, None)
            if chunk == 0 and make_wt and turn >= 4:
                next(turning, None)
        for _ in pending:
            pass
        if chunk == 0:
            if make_wt:
                for _ in turning:
                    pass
            else:
                copies[-1].wait()
        pending = product(chunk)
    for _ in pending:
        pass
    for copy in written:
        copy.wait()


def conv_run(feats, grads, low, high, neigh, weight, run, earlier, name):
    voxels, channels = feats.shape
    out = jax.ShapeDtypeStruct((voxels, channels), jnp.bfloat16)
    first, end = rows_needed(run)
    halos = ((low,) if first < 0 else ()) + ((high,) if end > voxels else ())
    turned = jax.ShapeDtypeStruct((2 * channels, 27 * channels), jnp.bfloat16)
    make_wt = not earlier
    operands = (feats, grads, neigh, weight if make_wt else earlier[2]) + halos + earlier[:2]
    size = run[1] - run[0]
    results = pl.pallas_call(
        functools.partial(conv_kernel, voxels, run, len(halos), make_wt),
        out_shape=(out, out) + ((turned,) if make_wt else ()),
        in_specs=[HBM] * len(operands),
        out_specs=(HBM, HBM) + ((HBM,) if make_wt else ()),
        input_output_aliases={4 + len(halos) + i: i for i in range(len(earlier[:2]))},
        scratch_shapes=[
            pltpu.VMEM(turned.shape, jnp.bfloat16),
        ]
        + ([pltpu.VMEM(weight.shape, jnp.bfloat16)] if make_wt else [])
        + [
            pltpu.VMEM((size, channels), jnp.bfloat16),
            pltpu.VMEM((size, channels), jnp.bfloat16),
            pltpu.VMEM((size + 2 * (LAYER + ROW), 2 * channels), jnp.bfloat16),
            pltpu.VMEM(neigh.shape, jnp.int32),
            pltpu.VMEM(neigh.shape, jnp.int32),
        ]
        + [pltpu.VMEM((27 * T, CHUNK_C), jnp.bfloat16)] * 4
        + [pltpu.SemaphoreType.DMA((8 + 2 * size // CHUNK_C,))],
        compiler_params=pltpu.CompilerParams(vmem_limit_bytes=FULL_VMEM_LIMIT),
        cost_estimate=pl.CostEstimate(
            flops=10**6 if make_wt else 10**10, bytes_accessed=10**4, transcendentals=0
        ),
        name=name,
    )(*operands)
    return tuple(results) + earlier[2:]


def sum_kernel(*refs):
    *parts, out_ref = refs
    terms = [ref[i] for ref in parts for i in range(ref.shape[0])]
    total = terms[0].astype(jnp.float32)
    for term in terms[1:]:
        total += term.astype(jnp.float32)
    total = total.astype(out_ref.dtype)
    for i in range(out_ref.shape[0]):
        out_ref[i] = total


def sum_parts(parts, copies, name):
    shape = parts[0].shape[1:]
    return pl.pallas_call(
        sum_kernel,
        out_shape=jax.ShapeDtypeStruct((copies,) + shape, parts[0].dtype),
        in_specs=[VMEM] * len(parts),
        out_specs=VMEM,
        compiler_params=pltpu.CompilerParams(vmem_limit_bytes=VMEM_LIMIT),
        cost_estimate=pl.CostEstimate(flops=10**6, bytes_accessed=10**4, transcendentals=0),
        name=name,
    )(*parts)


def widen_kernel(in_ref, *rest):
    out_ref = rest[-1]
    out_ref[...] = in_ref[...].astype(out_ref.dtype)


def widen(rows, own, count, earlier, name):
    half, channels = rows.shape
    block = (half // 2, channels)

    def place(i):
        side = own_side() if own else 1 - own_side()
        return side * 2 + i, 0

    return pl.pallas_call(
        widen_kernel,
        grid=(2,),
        in_specs=[pl.BlockSpec(block, lambda i: (i, 0))]
        + [pl.BlockSpec(memory_space=pl.ANY)] * len(earlier),
        out_specs=pl.BlockSpec(block, place),
        out_shape=jax.ShapeDtypeStruct((count, channels), jnp.float32),
        input_output_aliases={1 + i: i for i in range(len(earlier))},
        compiler_params=pltpu.CompilerParams(vmem_limit_bytes=VMEM_LIMIT),
        name=name,
    )(rows, *earlier)


def local(features, neighbours, weight, grad_out):
    feats, grads = features[0], grad_out[0]
    voxels, channels = feats.shape
    neigh = neighbours.reshape(27, voxels // T, T)
    space, dp = lax.axis_size("space"), lax.axis_size("dp")
    up = [(i, i + 1) for i in range(space - 1)]
    down = [(i + 1, i) for i in range(space - 1)]
    low = lax.ppermute(
        stack_layer_by_copies(feats, grads, voxels // LAYER - 1, "stack_last_layer"), "space", up
    )
    high = lax.ppermute(
        stack_layer(feats, grads, 0, "stack_first_layer"), "space", down
    )

    scale = 1.0 / math.sqrt(dp * space * voxels)
    group = dp // 2 * space
    share = -(-27 * channels // (32 * group)) * 16
    swap = [(i, i ^ 1) for i in range(dp)]
    alike = [
        [d * space + z for d in range(side, dp, 2) for z in range(space)] for side in range(2)
    ]
    inner = grad_w_inner(feats, grads, neigh)
    mine, other = grad_w_halo(feats, grads, low, neigh, inner, scale, 2 * group * share)
    mine, other, high = lax.optimization_barrier((mine, other, high))
    other = lax.ppermute(other, "dp", swap)
    mine = sum_parts((mine[None], other[None]), 1, "sum_of_pair")
    mine, flat_weight = lax.optimization_barrier(
        (mine, weight.reshape(27 * channels, channels))
    )
    half = voxels // CHUNK_C // 2 * CHUNK_C
    ends = [0, half, voxels]

    def conv(done, part):
        run = (ends[part], ends[part + 1])
        name = "conv_run_%d" % part
        return conv_run(feats, grads, low, high, neigh, flat_weight, run, done, name)

    def exchange(pieces):
        return lax.all_to_all(
            pieces, ("dp", "space"), 0, 0, axis_index_groups=alike, tiled=True
        )

    pieces = exchange(mine.reshape(group, share, channels))
    done = conv((), 0)
    pieces, done = lax.optimization_barrier((pieces, done))
    pieces = exchange(sum_parts((pieces,), group, "sum_and_spread"))
    done = conv(done, 1)
    pieces, done = lax.optimization_barrier((pieces, done))
    mine = pieces.reshape(group * share, channels)
    other = lax.ppermute(mine, "dp", swap)
    grad_w = widen(mine, True, 27 * channels, (), "widen_own_half")
    grad_w = widen(other, False, 27 * channels, (grad_w,), "widen_other_half")
    conv_out, grad_in, _ = done
    return conv_out[None], grad_in[None], grad_w.reshape(27, channels, channels)


def solution(mesh):
    in_specs = (P("dp", "space", None), P("dp", None, "space"), P(), P("dp", "space", None))
    out_specs = (P("dp", "space", None), P("dp", "space", None), P())
    return jax.shard_map(local, mesh=mesh, in_specs=in_specs, out_specs=out_specs, check_vma=False)
```

```python
import functools
import math

import jax
import jax.numpy as jnp
from jax import lax
from jax.experimental import pallas as pl
from jax.experimental.pallas import tpu as pltpu
from jax.sharding import PartitionSpec as P

PSIDE = 64
ROW = PSIDE // 4
LAYER = PSIDE * ROW
T = 128
CHUNK_W = 256
CHUNK_C = 256
VMEM_LIMIT = 28 * 1024 * 1024
FULL_VMEM_LIMIT = 58 * 1024 * 1024
VMEM = pl.BlockSpec(memory_space=pltpu.VMEM)
HBM = pl.BlockSpec(memory_space=pltpu.HBM)


def offset_of(k):
    return k // 9 - 1, (k // 3) % 3 - 1, k % 3 - 1


def row_in_scene_window(neighbours, shift):
    return jnp.where(neighbours >= 0, (neighbours - shift) & (T - 1), -1)


def one_hot(hit):
    return jnp.where(hit, jnp.ones((), jnp.bfloat16), jnp.zeros((), jnp.bfloat16))


def own_side():
    return lax.bitwise_and(lax.axis_index("dp"), 1).astype(jnp.int32)


def fill_edges(xe):
    edge = jnp.zeros((ROW, xe.shape[1]), jnp.bfloat16)
    xe[0:ROW, :] = edge
    xe[xe.shape[0] - ROW :, :] = edge


def one_hot_columns(rel, k, tile):
    spot = lax.broadcasted_iota(jnp.int32, (T, T), 0).astype(jnp.bfloat16)
    row = jnp.broadcast_to(rel[k, tile : tile + 1, :], (ROW, T)).astype(jnp.bfloat16)
    return one_hot(jnp.concatenate([row] * (T // ROW), axis=0) == spot)


def gather_columns(tiles, ks, xe, origin, rel, first_tile, to_f, to_g):
    channels = xe.shape[1] // 2
    none = jnp.zeros((T, T), jnp.bfloat16)
    kept = []

    def put(k, cols, part):
        to_f[k * T : (k + 1) * T, cols] = part[:channels]
        to_g[k * T : (k + 1) * T, cols] = part[channels:]

    def put_dot(source, right, places):
        picked = jnp.dot(source, right, preferred_element_type=jnp.float32).astype(jnp.bfloat16)
        for q, (k, cols) in enumerate(places):
            put(k, cols, picked[:, q * T : (q + 1) * T])

    for h, tile in enumerate(tiles):
        cols = slice(h * T, (h + 1) * T)
        for dz, dy in sorted({offset_of(k)[:2] for k in ks}):
            some = [k for k in ks if offset_of(k)[:2] == (dz, dy)]
            start = origin + tile * T + ROW * dy + LAYER * dz
            window = xe[start : start + T, :].T
            if 13 in some:
                put(13, cols, window)
                some.remove(13)
            if len(some) > 1:
                pair = (some.pop(0), some.pop())
                right = [one_hot_columns(rel, k, first_tile + tile) for k in pair]
                put_dot(window, jnp.concatenate(right, axis=1), [(k, cols) for k in pair])
            for k in some:
                kept.append((k, cols, window, one_hot_columns(rel, k, first_tile + tile)))
            if len(kept) == 2:
                (k0, cols0, window0, hot0), (k1, cols1, window1, hot1) = kept
                right = jnp.concatenate(
                    [
                        jnp.concatenate([hot0, none], axis=1),
                        jnp.concatenate([none, hot1], axis=1),
                    ],
                    axis=0,
                )
                both = jnp.concatenate([window0, window1], axis=1)
                put_dot(both, right, [(k0, cols0), (k1, cols1)])
                kept = []
            yield
    for k, cols, window, hot in kept:
        put_dot(window, hot, [(k, cols)])


def weight_terms(chunks, ks_of, origin, f_ref, g_ref, xe, rel, buffers, acc):
    def product(chunk):
        here = slice(chunk * CHUNK_W, (chunk + 1) * CHUNK_W)
        picked_f, picked_g = buffers[chunk % 2]
        ks = ks_of(chunk)
        left_f, left_g = f_ref[here, :].T, g_ref[here, :].T
        if 13 in ks:
            picked_g[13 * T :, :] = left_g
        for left, picked, side, end in ((left_g, picked_f, 0, 13), (left_f, picked_g, 13, 14)):
            for group in (range(0, 4), range(4, 8), range(8, end)):
                group = [k for k in group if k in ks]
                if group:
                    span = slice(group[0] * T, (group[-1] + 1) * T)
                    to = slice((side + group[0]) * T, (side + group[-1] + 1) * T)
                    acc[:, to] += lax.dot_general(
                        left,
                        picked[span, :],
                        (((1,), (1,)), ((), ())),
                        preferred_element_type=jnp.float32,
                    )
                    yield

    pending = iter(())
    per = CHUNK_W // T
    for chunk in chunks:
        tiles = range(chunk * per, (chunk + 1) * per)
        ks = [k for k in ks_of(chunk) if k < 13]
        for _ in gather_columns(tiles, ks, xe, origin, rel, 0, *buffers[chunk % 2]):
            next(pending, None)
        for _ in pending:
            pass
        pending = product(chunk)
    for _ in pending:
        pass


def weight_inner_kernel(voxels, f_ref, g_ref, nb_ref, acc, xe, rel, gf, gg, gf2, gg2):
    channels = f_ref.shape[1]
    xe[ROW : ROW + voxels, 0:channels] = f_ref[...]
    xe[ROW : ROW + voxels, channels:] = g_ref[...]
    fill_edges(xe)
    for k in range(13):
        rel[k, :, :] = row_in_scene_window(nb_ref[k], ROW * offset_of(k)[1])
    acc[...] = jnp.zeros_like(acc)

    def ks_of(chunk):
        return range(9 if chunk < LAYER // CHUNK_W else 0, 14)

    chunks = range(voxels // CHUNK_W)
    weight_terms(chunks, ks_of, ROW, f_ref, g_ref, xe, rel, ((gf, gg), (gf2, gg2)), acc)


def weight_halo_kernel(scale, f_ref, g_ref, low_ref, nb_ref, in_ref, mine_ref, other_ref, xe, rel, gf, gg, gf2, gg2, acc, out_ref):
    channels = f_ref.shape[1]
    xe[ROW : ROW + LAYER, 0:channels] = low_ref[0]
    xe[ROW : ROW + LAYER, channels:] = low_ref[1]
    fill_edges(xe)
    for k in range(9):
        rel[k, :, :] = row_in_scene_window(nb_ref[k, 0 : LAYER // T, :], ROW * offset_of(k)[1])
    acc[...] = jnp.zeros_like(acc)
    chunks = range(LAYER // CHUNK_W)
    buffers = ((gf, gg), (gf2, gg2))
    weight_terms(chunks, lambda _: range(9), ROW + LAYER, f_ref, g_ref, xe, rel, buffers, acc)

    def total(block, touched):
        span = slice(block * T, (block + 1) * T)
        return (in_ref[:, span] + acc[:, span] if touched else in_ref[:, span]) * scale

    for k in range(13):
        out_ref[k * T : (k + 1) * T, :] = total(k, k < 9).T.astype(out_ref.dtype)
    for k in range(14):
        out_ref[(26 - k) * T : (27 - k) * T, :] = total(13 + k, k < 9).astype(out_ref.dtype)
    if out_ref.shape[0] > 27 * T:
        out_ref[27 * T :, :] = jnp.zeros((out_ref.shape[0] - 27 * T, out_ref.shape[1]), out_ref.dtype)
    half = out_ref.shape[0] // 2
    parity = own_side()
    mine_ref[...] = out_ref[pl.ds(pl.multiple_of(parity * half, 16), half), :]
    other_ref[...] = out_ref[pl.ds(pl.multiple_of((1 - parity) * half, 16), half), :]


def weight_scratch(rows, channels):
    return [
        pltpu.VMEM((rows + 2 * ROW, 2 * channels), jnp.bfloat16),
        pltpu.VMEM((13, rows // T, T), jnp.int32),
    ] + [
        pltpu.VMEM((13 * T, CHUNK_W), jnp.bfloat16),
        pltpu.VMEM((14 * T, CHUNK_W), jnp.bfloat16),
    ] * 2


def grad_w_inner(feats, grads, neigh):
    voxels, channels = feats.shape
    return pl.pallas_call(
        functools.partial(weight_inner_kernel, voxels),
        out_shape=jax.ShapeDtypeStruct((channels, 27 * T), jnp.float32),
        in_specs=[VMEM] * 3,
        out_specs=VMEM,
        scratch_shapes=weight_scratch(voxels, channels),
        compiler_params=pltpu.CompilerParams(vmem_limit_bytes=VMEM_LIMIT),
        cost_estimate=pl.CostEstimate(flops=8 * 10**9, bytes_accessed=4 * 10**6, transcendentals=0),
        name="weight_gradient_inner",
    )(feats, grads, neigh)


def grad_w_halo(feats, grads, low, neigh, partial, scale, rows):
    channels = feats.shape[1]
    out = jax.ShapeDtypeStruct((rows // 2, channels), jnp.bfloat16)
    return pl.pallas_call(
        functools.partial(weight_halo_kernel, scale),
        out_shape=(out, out),
        in_specs=[VMEM] * 5,
        out_specs=(VMEM, VMEM),
        scratch_shapes=weight_scratch(LAYER, channels)
        + [
            pltpu.VMEM((channels, 27 * T), jnp.float32),
            pltpu.VMEM((rows, channels), jnp.bfloat16),
        ],
        compiler_params=pltpu.CompilerParams(vmem_limit_bytes=VMEM_LIMIT),
        cost_estimate=pl.CostEstimate(flops=10**6, bytes_accessed=10**4, transcendentals=0),
        name="weight_gradient_halo",
    )(feats, grads, low, neigh, partial)


def stack_kernel(f_ref, g_ref, out_ref):
    out_ref[0] = f_ref[...]
    out_ref[1] = g_ref[...]


def stack_by_copies_kernel(layer, f_ref, g_ref, out_ref, held, sems):
    rows = pl.ds(layer * LAYER, LAYER)
    copies = []
    for i, ref in enumerate((f_ref, g_ref)):
        copies.append(
            (
                pltpu.make_async_copy(ref.at[rows, :], held.at[i], sems.at[i]),
                pltpu.make_async_copy(held.at[i], out_ref.at[i], sems.at[2 + i]),
            )
        )
    for fetch, _ in copies:
        fetch.start()
    for fetch, store in copies:
        fetch.wait()
        store.start()
    for _, store in copies:
        store.wait()


def stack_layer(feats, grads, layer, name):
    channels = feats.shape[1]
    block = pl.BlockSpec((LAYER, channels), lambda i: (layer, 0))
    return pl.pallas_call(
        stack_kernel,
        grid=(1,),
        out_shape=jax.ShapeDtypeStruct((2, LAYER, channels), jnp.bfloat16),
        in_specs=[block, block],
        out_specs=VMEM,
        compiler_params=pltpu.CompilerParams(vmem_limit_bytes=VMEM_LIMIT),
        name=name,
    )(feats, grads)


def stack_layer_by_copies(feats, grads, layer, name):
    channels = feats.shape[1]
    shape = (2, LAYER, channels)
    return pl.pallas_call(
        functools.partial(stack_by_copies_kernel, layer),
        out_shape=jax.ShapeDtypeStruct(shape, jnp.bfloat16),
        in_specs=[HBM, HBM],
        out_specs=HBM,
        scratch_shapes=[pltpu.VMEM(shape, jnp.bfloat16), pltpu.SemaphoreType.DMA((4,))],
        compiler_params=pltpu.CompilerParams(vmem_limit_bytes=FULL_VMEM_LIMIT),
        name=name,
    )(feats, grads)


def rows_needed(run):
    first, end = run
    return (
        first - LAYER - (ROW if first % LAYER else 0),
        end + LAYER + (ROW if end % LAYER else 0),
    )


def conv_kernel(voxels, run, halos, make_wt, f_ref, g_ref, nb_ref, w_hbm, *rest):
    halos = list(rest[:halos])
    if make_wt:
        conv_hbm, gin_hbm, wt_hbm, wt, w_ref, *scratch = rest[-15:]
    else:
        conv_hbm, gin_hbm, wt, *scratch = rest[-13:]
    conv_ref, gin_ref, xe, nb, rel, gf, gg, gf2, gg2, sems = scratch
    channels = f_ref.shape[1]
    size = run[1] - run[0]

    origin = run[0] - LAYER - ROW
    low, high = rows_needed(run)
    main = (max(low, 0), min(high, voxels))
    rows = pl.ds(main[0], main[1] - main[0])
    to = pl.ds(main[0] - origin, main[1] - main[0])
    copies = [
        (nb_ref, nb),
        (f_ref.at[rows, :], xe.at[to, pl.ds(0, channels)]),
        (g_ref.at[rows, :], xe.at[to, pl.ds(channels, channels)]),
    ]
    parts = []
    if low < 0:
        parts.append((pl.ds(LAYER + low, -low), pl.ds(low - origin, -low)))
    if high > voxels:
        parts.append((pl.ds(0, high - voxels), pl.ds(voxels - origin, high - voxels)))
    for halo, (rows, to) in zip(halos, parts):
        for side in range(2):
            lanes = pl.ds(side * channels, channels)
            copies.append((halo.at[side, rows, :], xe.at[to, lanes]))
    early = len(copies)
    copies.append((w_hbm, w_ref if make_wt else wt))
    copies = [
        pltpu.make_async_copy(source, target, sems.at[i])
        for i, (source, target) in enumerate(copies)
    ]
    for copy in copies:
        copy.start()
    edge = jnp.zeros((ROW, 2 * channels), jnp.bfloat16)
    if low - origin:
        xe[0:ROW, :] = edge
    if high - origin < xe.shape[0]:
        xe[xe.shape[0] - ROW :, :] = edge
    copies[0].wait()
    for k in range(27):
        rel[k, :, :] = row_in_scene_window(nb[k], ROW * offset_of(k)[1])
    for copy in copies[1:early]:
        copy.wait()

    buffers = ((gf, gg), (gf2, gg2))

    def product(chunk):
        rows = slice(chunk * CHUNK_C, (chunk + 1) * CHUNK_C)
        kernels = (slice(0, channels), slice(channels, 2 * channels))
        outs = ((conv_ref, conv_hbm), (gin_ref, gin_hbm))
        for (out, out_hbm), picked, side in zip(outs, buffers[chunk % 2], kernels):
            total = None
            for part in range(3):
                span = slice(part * 9 * T, (part + 1) * 9 * T)
                term = jnp.dot(wt[side, span], picked[span, :], preferred_element_type=jnp.float32)
                total = term if total is None else total + term
                if part == 2:
                    out[rows, :] = total.T.astype(jnp.bfloat16)
                    copy = pltpu.make_async_copy(
                        out.at[rows, :],
                        out_hbm.at[pl.ds(run[0] + chunk * CHUNK_C, CHUNK_C), :],
                        sems.at[len(copies) + len(written)],
                    )
                    copy.start()
                    written.append(copy)
                yield

    def turn_weights():
        copies[-1].wait()
        for k in range(27):
            span = slice(k * T, (k + 1) * T)
            wt[0:channels, span] = w_ref[span, :].T
            wt[channels:, span] = w_ref[(26 - k) * T : (27 - k) * T, :]
            if k % 2:
                yield
        copy = pltpu.make_async_copy(wt, wt_hbm, sems.at[len(copies)])
        copy.start()
        written.append(copy)

    written = []
    turning = turn_weights()
    pending = iter(())
    per = CHUNK_C // T
    for chunk in range(size // CHUNK_C):
        tiles = range(chunk * per, (chunk + 1) * per)
        center, first_tile = run[0] - origin, run[0] // T
        moves = gather_columns(
            tiles, range(27), xe, center, rel, first_tile, *buffers[chunk % 2]
        )
        for turn, _ in enumerate(moves):
            if turn % 3 == 2:
                next(pending, None)
            if chunk == 0 and make_wt and turn >= 4:
                next(turning, None)
        for _ in pending:
            pass
        if chunk == 0:
            if make_wt:
                for _ in turning:
                    pass
            else:
                copies[-1].wait()
        pending = product(chunk)
    for _ in pending:
        pass
    for copy in written:
        copy.wait()


def conv_run(feats, grads, low, high, neigh, weight, run, earlier, name):
    voxels, channels = feats.shape
    out = jax.ShapeDtypeStruct((voxels, channels), jnp.bfloat16)
    first, end = rows_needed(run)
    halos = ((low,) if first < 0 else ()) + ((high,) if end > voxels else ())
    turned = jax.ShapeDtypeStruct((2 * channels, 27 * channels), jnp.bfloat16)
    make_wt = not earlier
    operands = (feats, grads, neigh, weight if make_wt else earlier[2]) + halos + earlier[:2]
    size = run[1] - run[0]
    results = pl.pallas_call(
        functools.partial(conv_kernel, voxels, run, len(halos), make_wt),
        out_shape=(out, out) + ((turned,) if make_wt else ()),
        in_specs=[HBM] * len(operands),
        out_specs=(HBM, HBM) + ((HBM,) if make_wt else ()),
        input_output_aliases={4 + len(halos) + i: i for i in range(len(earlier[:2]))},
        scratch_shapes=[
            pltpu.VMEM(turned.shape, jnp.bfloat16),
        ]
        + ([pltpu.VMEM(weight.shape, jnp.bfloat16)] if make_wt else [])
        + [
            pltpu.VMEM((size, channels), jnp.bfloat16),
            pltpu.VMEM((size, channels), jnp.bfloat16),
            pltpu.VMEM((size + 2 * (LAYER + ROW), 2 * channels), jnp.bfloat16),
            pltpu.VMEM(neigh.shape, jnp.int32),
            pltpu.VMEM(neigh.shape, jnp.int32),
        ]
        + [pltpu.VMEM((27 * T, CHUNK_C), jnp.bfloat16)] * 4
        + [pltpu.SemaphoreType.DMA((8 + 2 * size // CHUNK_C,))],
        compiler_params=pltpu.CompilerParams(vmem_limit_bytes=FULL_VMEM_LIMIT),
        cost_estimate=pl.CostEstimate(
            flops=10**6 if make_wt else 10**10, bytes_accessed=10**4, transcendentals=0
        ),
        name=name,
    )(*operands)
    return tuple(results) + earlier[2:]


def sum_kernel(*refs):
    *parts, out_ref = refs
    terms = [ref[i] for ref in parts for i in range(ref.shape[0])]
    total = terms[0].astype(jnp.float32)
    for term in terms[1:]:
        total += term.astype(jnp.float32)
    total = total.astype(out_ref.dtype)
    for i in range(out_ref.shape[0]):
        out_ref[i] = total


def sum_parts(parts, copies, name):
    shape = parts[0].shape[1:]
    return pl.pallas_call(
        sum_kernel,
        out_shape=jax.ShapeDtypeStruct((copies,) + shape, parts[0].dtype),
        in_specs=[VMEM] * len(parts),
        out_specs=VMEM,
        compiler_params=pltpu.CompilerParams(vmem_limit_bytes=VMEM_LIMIT),
        cost_estimate=pl.CostEstimate(flops=10**6, bytes_accessed=10**4, transcendentals=0),
        name=name,
    )(*parts)


def widen_kernel(own, count, in_ref, *rest):
    out_hbm, wide, sems = rest[-3:]
    half = in_ref.shape[0]
    piece = half // 2
    side = own_side() if own else 1 - own_side()

    def copy(where, i):
        first = where * half + i * piece
        size = min(piece, count - first)
        return pltpu.make_async_copy(
            wide.at[pl.ds(i * piece, size), :], out_hbm.at[pl.ds(first, size), :], sems.at[i]
        )

    for i in range(2):
        rows = slice(i * piece, (i + 1) * piece)
        wide[rows, :] = in_ref[rows, :].astype(jnp.float32)
        for where in range(2):
            pl.when(side == where)(copy(where, i).start)
    for i in range(2):
        for where in range(2):
            pl.when(side == where)(copy(where, i).wait)


def widen(rows, own, count, earlier, name):
    return pl.pallas_call(
        functools.partial(widen_kernel, own, count),
        in_specs=[VMEM] + [HBM] * len(earlier),
        out_specs=HBM,
        out_shape=jax.ShapeDtypeStruct((count, rows.shape[1]), jnp.float32),
        input_output_aliases={1 + i: i for i in range(len(earlier))},
        scratch_shapes=[pltpu.VMEM(rows.shape, jnp.float32), pltpu.SemaphoreType.DMA((2,))],
        compiler_params=pltpu.CompilerParams(vmem_limit_bytes=VMEM_LIMIT),
        name=name,
    )(rows, *earlier)


def local(features, neighbours, weight, grad_out):
    feats, grads = features[0], grad_out[0]
    voxels, channels = feats.shape
    neigh = neighbours.reshape(27, voxels // T, T)
    space, dp = lax.axis_size("space"), lax.axis_size("dp")
    up = [(i, i + 1) for i in range(space - 1)]
    down = [(i + 1, i) for i in range(space - 1)]
    low = lax.ppermute(
        stack_layer_by_copies(feats, grads, voxels // LAYER - 1, "stack_last_layer"), "space", up
    )
    high = lax.ppermute(
        stack_layer(feats, grads, 0, "stack_first_layer"), "space", down
    )

    scale = 1.0 / math.sqrt(dp * space * voxels)
    group = dp // 2 * space
    share = -(-27 * channels // (32 * group)) * 16
    swap = [(i, i ^ 1) for i in range(dp)]
    alike = [
        [d * space + z for d in range(side, dp, 2) for z in range(space)] for side in range(2)
    ]
    inner = grad_w_inner(feats, grads, neigh)
    mine, other = grad_w_halo(feats, grads, low, neigh, inner, scale, 2 * group * share)
    mine, other, high = lax.optimization_barrier((mine, other, high))
    other = lax.ppermute(other, "dp", swap)
    mine = sum_parts((mine[None], other[None]), 1, "sum_of_pair")
    mine, flat_weight = lax.optimization_barrier(
        (mine, weight.reshape(27 * channels, channels))
    )
    half = voxels // CHUNK_C // 2 * CHUNK_C
    ends = [0, half, voxels]

    def conv(done, part):
        run = (ends[part], ends[part + 1])
        name = "conv_run_%d" % part
        return conv_run(feats, grads, low, high, neigh, flat_weight, run, done, name)

    def exchange(pieces):
        return lax.all_to_all(
            pieces, ("dp", "space"), 0, 0, axis_index_groups=alike, tiled=True
        )

    pieces = exchange(mine.reshape(group, share, channels))
    done = conv((), 0)
    pieces, done = lax.optimization_barrier((pieces, done))
    pieces = exchange(sum_parts((pieces,), group, "sum_and_spread"))
    done = conv(done, 1)
    pieces, done = lax.optimization_barrier((pieces, done))
    mine = pieces.reshape(group * share, channels)
    other = lax.ppermute(mine, "dp", swap)
    grad_w = widen(mine, True, 27 * channels, (), "widen_own_half")
    grad_w = widen(other, False, 27 * channels, (grad_w,), "widen_other_half")
    conv_out, grad_in, _ = done
    return conv_out[None], grad_in[None], grad_w.reshape(27, channels, channels)


def solution(mesh):
    in_specs = (P("dp", "space", None), P("dp", None, "space"), P(), P("dp", "space", None))
    out_specs = (P("dp", "space", None), P("dp", "space", None), P())
    return jax.shard_map(local, mesh=mesh, in_specs=in_specs, out_specs=out_specs, check_vma=False)
```

```python
import functools
import itertools
import math

import jax
import jax.numpy as jnp
from jax import lax
from jax.experimental import pallas as pl
from jax.experimental.pallas import tpu as pltpu
from jax.sharding import PartitionSpec as P

PSIDE = 64
ROW = PSIDE // 4
LAYER = PSIDE * ROW
T = 128
CHUNK_W = 256
CHUNK_C = 256
VMEM_LIMIT = 28 * 1024 * 1024
FULL_VMEM_LIMIT = 58 * 1024 * 1024
VMEM = pl.BlockSpec(memory_space=pltpu.VMEM)
HBM = pl.BlockSpec(memory_space=pltpu.HBM)


def offset_of(k):
    return k // 9 - 1, (k // 3) % 3 - 1, k % 3 - 1


def row_in_scene_window(neighbours, shift):
    return jnp.where(neighbours >= 0, (neighbours - shift) & (T - 1), -1)


def one_hot(hit):
    return jnp.where(hit, jnp.ones((), jnp.bfloat16), jnp.zeros((), jnp.bfloat16))


def own_side():
    return lax.bitwise_and(lax.axis_index("dp"), 1).astype(jnp.int32)


def fill_edges(xe):
    edge = jnp.zeros((ROW, xe.shape[1]), jnp.bfloat16)
    xe[0:ROW, :] = edge
    xe[xe.shape[0] - ROW :, :] = edge


def one_hot_columns(rel, k, tile):
    spot = lax.broadcasted_iota(jnp.int32, (T, T), 0).astype(jnp.bfloat16)
    row = jnp.broadcast_to(rel[k, tile : tile + 1, :], (ROW, T)).astype(jnp.bfloat16)
    return one_hot(jnp.concatenate([row] * (T // ROW), axis=0) == spot)


def gather_columns(tiles, ks, xe, origin, rel, first_tile, to_f, to_g):
    channels = xe.shape[1] // 2
    none = jnp.zeros((T, T), jnp.bfloat16)
    kept = []

    def put(k, cols, part):
        to_f[k * T : (k + 1) * T, cols] = part[:channels]
        to_g[k * T : (k + 1) * T, cols] = part[channels:]

    def put_dot(source, right, places):
        picked = jnp.dot(source, right, preferred_element_type=jnp.float32).astype(jnp.bfloat16)
        for q, (k, cols) in enumerate(places):
            put(k, cols, picked[:, q * T : (q + 1) * T])

    for h, tile in enumerate(tiles):
        cols = slice(h * T, (h + 1) * T)
        for dz, dy in sorted({offset_of(k)[:2] for k in ks}):
            some = [k for k in ks if offset_of(k)[:2] == (dz, dy)]
            start = origin + tile * T + ROW * dy + LAYER * dz
            window = xe[start : start + T, :].T
            if 13 in some:
                put(13, cols, window)
                some.remove(13)
            if len(some) > 1:
                pair = (some.pop(0), some.pop())
                right = [one_hot_columns(rel, k, first_tile + tile) for k in pair]
                put_dot(window, jnp.concatenate(right, axis=1), [(k, cols) for k in pair])
            for k in some:
                kept.append((k, cols, window, one_hot_columns(rel, k, first_tile + tile)))
            if len(kept) == 2:
                (k0, cols0, window0, hot0), (k1, cols1, window1, hot1) = kept
                right = jnp.concatenate(
                    [
                        jnp.concatenate([hot0, none], axis=1),
                        jnp.concatenate([none, hot1], axis=1),
                    ],
                    axis=0,
                )
                both = jnp.concatenate([window0, window1], axis=1)
                put_dot(both, right, [(k0, cols0), (k1, cols1)])
                kept = []
            yield
    for k, cols, window, hot in kept:
        put_dot(window, hot, [(k, cols)])


def weight_terms(chunks, ks_of, origin, f_ref, g_ref, xe, rel, buffers, acc):
    def product(chunk):
        here = slice(chunk * CHUNK_W, (chunk + 1) * CHUNK_W)
        picked_f, picked_g = buffers[chunk % 2]
        ks = ks_of(chunk)
        left_f, left_g = f_ref[here, :].T, g_ref[here, :].T
        if 13 in ks:
            picked_g[13 * T :, :] = left_g
        for left, picked, side, end in ((left_g, picked_f, 0, 13), (left_f, picked_g, 13, 14)):
            for group in (range(0, 4), range(4, 8), range(8, end)):
                group = [k for k in group if k in ks]
                if group:
                    span = slice(group[0] * T, (group[-1] + 1) * T)
                    to = slice((side + group[0]) * T, (side + group[-1] + 1) * T)
                    acc[:, to] += lax.dot_general(
                        left,
                        picked[span, :],
                        (((1,), (1,)), ((), ())),
                        preferred_element_type=jnp.float32,
                    )
                    yield

    pending = iter(())
    per = CHUNK_W // T
    for chunk in chunks:
        tiles = range(chunk * per, (chunk + 1) * per)
        ks = [k for k in ks_of(chunk) if k < 13]
        for _ in gather_columns(tiles, ks, xe, origin, rel, 0, *buffers[chunk % 2]):
            next(pending, None)
        for _ in pending:
            pass
        pending = product(chunk)
    for _ in pending:
        pass


def weight_inner_kernel(voxels, f_ref, g_ref, nb_ref, acc, xe, rel, gf, gg, gf2, gg2):
    channels = f_ref.shape[1]
    xe[ROW : ROW + voxels, 0:channels] = f_ref[...]
    xe[ROW : ROW + voxels, channels:] = g_ref[...]
    fill_edges(xe)
    for k in range(13):
        rel[k, :, :] = row_in_scene_window(nb_ref[k], ROW * offset_of(k)[1])
    acc[...] = jnp.zeros_like(acc)

    def ks_of(chunk):
        return range(9 if chunk < LAYER // CHUNK_W else 0, 14)

    chunks = range(voxels // CHUNK_W)
    weight_terms(chunks, ks_of, ROW, f_ref, g_ref, xe, rel, ((gf, gg), (gf2, gg2)), acc)


def weight_halo_kernel(scale, f_ref, g_ref, low_ref, nb_ref, in_ref, mine_ref, other_ref, xe, rel, gf, gg, gf2, gg2, acc, out_ref):
    channels = f_ref.shape[1]
    xe[ROW : ROW + LAYER, 0:channels] = low_ref[0]
    xe[ROW : ROW + LAYER, channels:] = low_ref[1]
    fill_edges(xe)
    for k in range(9):
        rel[k, :, :] = row_in_scene_window(nb_ref[k, 0 : LAYER // T, :], ROW * offset_of(k)[1])
    acc[...] = jnp.zeros_like(acc)
    chunks = range(LAYER // CHUNK_W)
    buffers = ((gf, gg), (gf2, gg2))
    weight_terms(chunks, lambda _: range(9), ROW + LAYER, f_ref, g_ref, xe, rel, buffers, acc)

    def total(block, touched):
        span = slice(block * T, (block + 1) * T)
        return (in_ref[:, span] + acc[:, span] if touched else in_ref[:, span]) * scale

    for k in range(13):
        out_ref[k * T : (k + 1) * T, :] = total(k, k < 9).T.astype(out_ref.dtype)
    for k in range(14):
        out_ref[(26 - k) * T : (27 - k) * T, :] = total(13 + k, k < 9).astype(out_ref.dtype)
    if out_ref.shape[0] > 27 * T:
        out_ref[27 * T :, :] = jnp.zeros((out_ref.shape[0] - 27 * T, out_ref.shape[1]), out_ref.dtype)
    half = out_ref.shape[0] // 2
    parity = own_side()
    mine_ref[...] = out_ref[pl.ds(pl.multiple_of(parity * half, 16), half), :]
    other_ref[...] = out_ref[pl.ds(pl.multiple_of((1 - parity) * half, 16), half), :]


def weight_scratch(rows, channels):
    return [
        pltpu.VMEM((rows + 2 * ROW, 2 * channels), jnp.bfloat16),
        pltpu.VMEM((13, rows // T, T), jnp.int32),
    ] + [
        pltpu.VMEM((13 * T, CHUNK_W), jnp.bfloat16),
        pltpu.VMEM((14 * T, CHUNK_W), jnp.bfloat16),
    ] * 2


def grad_w_inner(feats, grads, neigh):
    voxels, channels = feats.shape
    return pl.pallas_call(
        functools.partial(weight_inner_kernel, voxels),
        out_shape=jax.ShapeDtypeStruct((channels, 27 * T), jnp.float32),
        in_specs=[VMEM] * 3,
        out_specs=VMEM,
        scratch_shapes=weight_scratch(voxels, channels),
        compiler_params=pltpu.CompilerParams(vmem_limit_bytes=VMEM_LIMIT),
        cost_estimate=pl.CostEstimate(flops=8 * 10**9, bytes_accessed=4 * 10**6, transcendentals=0),
        name="weight_gradient_inner",
    )(feats, grads, neigh)


def grad_w_halo(feats, grads, low, neigh, partial, scale, rows):
    channels = feats.shape[1]
    out = jax.ShapeDtypeStruct((rows // 2, channels), jnp.bfloat16)
    return pl.pallas_call(
        functools.partial(weight_halo_kernel, scale),
        out_shape=(out, out),
        in_specs=[VMEM] * 5,
        out_specs=(VMEM, VMEM),
        scratch_shapes=weight_scratch(LAYER, channels)
        + [
            pltpu.VMEM((channels, 27 * T), jnp.float32),
            pltpu.VMEM((rows, channels), jnp.bfloat16),
        ],
        compiler_params=pltpu.CompilerParams(vmem_limit_bytes=VMEM_LIMIT),
        cost_estimate=pl.CostEstimate(flops=10**6, bytes_accessed=10**4, transcendentals=0),
        name="weight_gradient_halo",
    )(feats, grads, low, neigh, partial)


def stack_kernel(f_ref, g_ref, out_ref):
    out_ref[0] = f_ref[...]
    out_ref[1] = g_ref[...]


def stack_by_copies_kernel(layer, f_ref, g_ref, out_ref, held, sems):
    rows = pl.ds(layer * LAYER, LAYER)
    copies = []
    for i, ref in enumerate((f_ref, g_ref)):
        copies.append(
            (
                pltpu.make_async_copy(ref.at[rows, :], held.at[i], sems.at[i]),
                pltpu.make_async_copy(held.at[i], out_ref.at[i], sems.at[2 + i]),
            )
        )
    for fetch, _ in copies:
        fetch.start()
    for fetch, store in copies:
        fetch.wait()
        store.start()
    for _, store in copies:
        store.wait()


def stack_layer(feats, grads, layer, name):
    channels = feats.shape[1]
    block = pl.BlockSpec((LAYER, channels), lambda i: (layer, 0))
    return pl.pallas_call(
        stack_kernel,
        grid=(1,),
        out_shape=jax.ShapeDtypeStruct((2, LAYER, channels), jnp.bfloat16),
        in_specs=[block, block],
        out_specs=VMEM,
        compiler_params=pltpu.CompilerParams(vmem_limit_bytes=VMEM_LIMIT),
        name=name,
    )(feats, grads)


def stack_layer_by_copies(feats, grads, layer, name):
    channels = feats.shape[1]
    shape = (2, LAYER, channels)
    return pl.pallas_call(
        functools.partial(stack_by_copies_kernel, layer),
        out_shape=jax.ShapeDtypeStruct(shape, jnp.bfloat16),
        in_specs=[HBM, HBM],
        out_specs=HBM,
        scratch_shapes=[pltpu.VMEM(shape, jnp.bfloat16), pltpu.SemaphoreType.DMA((4,))],
        compiler_params=pltpu.CompilerParams(vmem_limit_bytes=FULL_VMEM_LIMIT),
        name=name,
    )(feats, grads)


def rows_needed(run):
    first, end = run
    return (
        first - LAYER - (ROW if first % LAYER else 0),
        end + LAYER + (ROW if end % LAYER else 0),
    )


def conv_kernel(voxels, run, halos, make_wt, f_ref, g_ref, nb_ref, w_hbm, *rest):
    halos = list(rest[:halos])
    if make_wt:
        conv_hbm, gin_hbm, wt_hbm, wt, w_ref, *scratch = rest[-15:]
    else:
        conv_hbm, gin_hbm, wt, *scratch = rest[-13:]
    conv_ref, gin_ref, xe, nb, rel, gf, gg, gf2, gg2, sems = scratch
    channels = f_ref.shape[1]
    size = run[1] - run[0]

    origin = run[0] - LAYER - ROW
    low, high = rows_needed(run)
    main = (max(low, 0), min(high, voxels))
    rows = pl.ds(main[0], main[1] - main[0])
    to = pl.ds(main[0] - origin, main[1] - main[0])
    copies = [
        (nb_ref, nb),
        (f_ref.at[rows, :], xe.at[to, pl.ds(0, channels)]),
        (g_ref.at[rows, :], xe.at[to, pl.ds(channels, channels)]),
    ]
    parts = []
    if low < 0:
        parts.append((pl.ds(LAYER + low, -low), pl.ds(low - origin, -low)))
    if high > voxels:
        parts.append((pl.ds(0, high - voxels), pl.ds(voxels - origin, high - voxels)))
    for halo, (rows, to) in zip(halos, parts):
        for side in range(2):
            lanes = pl.ds(side * channels, channels)
            copies.append((halo.at[side, rows, :], xe.at[to, lanes]))
    early = len(copies)
    copies.append((w_hbm, w_ref if make_wt else wt))
    copies = [
        pltpu.make_async_copy(source, target, sems.at[i])
        for i, (source, target) in enumerate(copies)
    ]
    for copy in copies:
        copy.start()
    edge = jnp.zeros((ROW, 2 * channels), jnp.bfloat16)
    if low - origin:
        xe[0:ROW, :] = edge
    if high - origin < xe.shape[0]:
        xe[xe.shape[0] - ROW :, :] = edge
    copies[0].wait()
    for k in range(27):
        rel[k, :, :] = row_in_scene_window(nb[k], ROW * offset_of(k)[1])
    for copy in copies[1:early]:
        copy.wait()

    buffers = ((gf, gg), (gf2, gg2))

    def product(chunk, sides=(0, 1)):
        rows = slice(chunk * CHUNK_C, (chunk + 1) * CHUNK_C)
        kernels = (slice(0, channels), slice(channels, 2 * channels))
        outs = ((conv_ref, conv_hbm), (gin_ref, gin_hbm))
        for i in sides:
            (out, out_hbm), picked, side = outs[i], buffers[chunk % 2][i], kernels[i]
            total = None
            for part in range(3):
                span = slice(part * 9 * T, (part + 1) * 9 * T)
                term = jnp.dot(wt[side, span], picked[span, :], preferred_element_type=jnp.float32)
                total = term if total is None else total + term
                if part == 2:
                    out[rows, :] = total.T.astype(jnp.bfloat16)
                    copy = pltpu.make_async_copy(
                        out.at[rows, :],
                        out_hbm.at[pl.ds(run[0] + chunk * CHUNK_C, CHUNK_C), :],
                        sems.at[len(copies) + len(written)],
                    )
                    copy.start()
                    written.append(copy)
                yield

    def turn_weights():
        copies[-1].wait()
        for k in range(27):
            span = slice(k * T, (k + 1) * T)
            wt[0:channels, span] = w_ref[span, :].T
            wt[channels:, span] = w_ref[(26 - k) * T : (27 - k) * T, :]
            if k % 2:
                yield
        copy = pltpu.make_async_copy(wt, wt_hbm, sems.at[len(copies)])
        copy.start()
        written.append(copy)

    written = []
    turning = turn_weights()
    pending = iter(())
    per = CHUNK_C // T
    for chunk in range(size // CHUNK_C):
        tiles = range(chunk * per, (chunk + 1) * per)
        center, first_tile = run[0] - origin, run[0] // T
        moves = gather_columns(
            tiles, range(27), xe, center, rel, first_tile, *buffers[chunk % 2]
        )
        last = 0 < chunk == size // CHUNK_C - 1
        own = [product(chunk, (0,)), product(chunk, (1,))] if last else [product(chunk)]
        for turn, _ in enumerate(moves):
            if turn % (2 if last else 3) == 1 + (not last):
                next(pending, None)
            if last and turn in (13, 14, 16, 17):
                next(own[(turn - 1) % 3])
            if chunk == 0 and make_wt and turn >= 4:
                next(turning, None)
        for _ in pending:
            pass
        if chunk == 0:
            if make_wt:
                for _ in turning:
                    pass
            else:
                copies[-1].wait()
        pending = itertools.chain(*own)
    for _ in pending:
        pass
    for copy in written:
        copy.wait()


def conv_run(feats, grads, low, high, neigh, weight, run, earlier, name):
    voxels, channels = feats.shape
    out = jax.ShapeDtypeStruct((voxels, channels), jnp.bfloat16)
    first, end = rows_needed(run)
    halos = ((low,) if first < 0 else ()) + ((high,) if end > voxels else ())
    turned = jax.ShapeDtypeStruct((2 * channels, 27 * channels), jnp.bfloat16)
    make_wt = not earlier
    operands = (feats, grads, neigh, weight if make_wt else earlier[2]) + halos + earlier[:2]
    size = run[1] - run[0]
    results = pl.pallas_call(
        functools.partial(conv_kernel, voxels, run, len(halos), make_wt),
        out_shape=(out, out) + ((turned,) if make_wt else ()),
        in_specs=[HBM] * len(operands),
        out_specs=(HBM, HBM) + ((HBM,) if make_wt else ()),
        input_output_aliases={4 + len(halos) + i: i for i in range(len(earlier[:2]))},
        scratch_shapes=[
            pltpu.VMEM(turned.shape, jnp.bfloat16),
        ]
        + ([pltpu.VMEM(weight.shape, jnp.bfloat16)] if make_wt else [])
        + [
            pltpu.VMEM((size, channels), jnp.bfloat16),
            pltpu.VMEM((size, channels), jnp.bfloat16),
            pltpu.VMEM((size + 2 * (LAYER + ROW), 2 * channels), jnp.bfloat16),
            pltpu.VMEM(neigh.shape, jnp.int32),
            pltpu.VMEM(neigh.shape, jnp.int32),
        ]
        + [pltpu.VMEM((27 * T, CHUNK_C), jnp.bfloat16)] * 4
        + [pltpu.SemaphoreType.DMA((8 + 2 * size // CHUNK_C,))],
        compiler_params=pltpu.CompilerParams(vmem_limit_bytes=FULL_VMEM_LIMIT),
        cost_estimate=pl.CostEstimate(
            flops=10**6 if make_wt else 10**10, bytes_accessed=10**4, transcendentals=0
        ),
        name=name,
    )(*operands)
    return tuple(results) + earlier[2:]


def sum_kernel(*refs):
    *parts, out_ref = refs
    terms = [ref[i] for ref in parts for i in range(ref.shape[0])]
    total = terms[0].astype(jnp.float32)
    for term in terms[1:]:
        total += term.astype(jnp.float32)
    total = total.astype(out_ref.dtype)
    for i in range(out_ref.shape[0]):
        out_ref[i] = total


def sum_parts(parts, copies, name):
    shape = parts[0].shape[1:]
    return pl.pallas_call(
        sum_kernel,
        out_shape=jax.ShapeDtypeStruct((copies,) + shape, parts[0].dtype),
        in_specs=[VMEM] * len(parts),
        out_specs=VMEM,
        compiler_params=pltpu.CompilerParams(vmem_limit_bytes=VMEM_LIMIT),
        cost_estimate=pl.CostEstimate(flops=10**6, bytes_accessed=10**4, transcendentals=0),
        name=name,
    )(*parts)


def widen_kernel(own, count, in_ref, *rest):
    out_hbm, wide, sems = rest[-3:]
    half = in_ref.shape[0]
    piece = half // 2
    side = own_side() if own else 1 - own_side()

    def copy(where, i):
        first = where * half + i * piece
        size = min(piece, count - first)
        return pltpu.make_async_copy(
            wide.at[pl.ds(i * piece, size), :], out_hbm.at[pl.ds(first, size), :], sems.at[i]
        )

    for i in range(2):
        rows = slice(i * piece, (i + 1) * piece)
        wide[rows, :] = in_ref[rows, :].astype(jnp.float32)
        for where in range(2):
            pl.when(side == where)(copy(where, i).start)
    for i in range(2):
        for where in range(2):
            pl.when(side == where)(copy(where, i).wait)


def widen(rows, own, count, earlier, name):
    return pl.pallas_call(
        functools.partial(widen_kernel, own, count),
        in_specs=[VMEM] + [HBM] * len(earlier),
        out_specs=HBM,
        out_shape=jax.ShapeDtypeStruct((count, rows.shape[1]), jnp.float32),
        input_output_aliases={1 + i: i for i in range(len(earlier))},
        scratch_shapes=[pltpu.VMEM(rows.shape, jnp.float32), pltpu.SemaphoreType.DMA((2,))],
        compiler_params=pltpu.CompilerParams(vmem_limit_bytes=VMEM_LIMIT),
        name=name,
    )(rows, *earlier)


def local(features, neighbours, weight, grad_out):
    feats, grads = features[0], grad_out[0]
    voxels, channels = feats.shape
    neigh = neighbours.reshape(27, voxels // T, T)
    space, dp = lax.axis_size("space"), lax.axis_size("dp")
    up = [(i, i + 1) for i in range(space - 1)]
    down = [(i + 1, i) for i in range(space - 1)]
    low = lax.ppermute(
        stack_layer_by_copies(feats, grads, voxels // LAYER - 1, "stack_last_layer"), "space", up
    )
    high = lax.ppermute(
        stack_layer(feats, grads, 0, "stack_first_layer"), "space", down
    )

    scale = 1.0 / math.sqrt(dp * space * voxels)
    group = dp // 2 * space
    share = -(-27 * channels // (32 * group)) * 16
    swap = [(i, i ^ 1) for i in range(dp)]
    alike = [
        [d * space + z for d in range(side, dp, 2) for z in range(space)] for side in range(2)
    ]
    inner = grad_w_inner(feats, grads, neigh)
    mine, other = grad_w_halo(feats, grads, low, neigh, inner, scale, 2 * group * share)
    mine, other, high = lax.optimization_barrier((mine, other, high))
    other = lax.ppermute(other, "dp", swap)
    mine = sum_parts((mine[None], other[None]), 1, "sum_of_pair")
    mine, flat_weight = lax.optimization_barrier(
        (mine, weight.reshape(27 * channels, channels))
    )
    half = voxels // CHUNK_C // 2 * CHUNK_C
    ends = [0, half, voxels]

    def conv(done, part):
        run = (ends[part], ends[part + 1])
        name = "conv_run_%d" % part
        return conv_run(feats, grads, low, high, neigh, flat_weight, run, done, name)

    def exchange(pieces):
        return lax.all_to_all(
            pieces, ("dp", "space"), 0, 0, axis_index_groups=alike, tiled=True
        )

    pieces = exchange(mine.reshape(group, share, channels))
    done = conv((), 0)
    pieces, done = lax.optimization_barrier((pieces, done))
    pieces = exchange(sum_parts((pieces,), group, "sum_and_spread"))
    done = conv(done, 1)
    pieces, done = lax.optimization_barrier((pieces, done))
    mine = pieces.reshape(group * share, channels)
    other = lax.ppermute(mine, "dp", swap)
    grad_w = widen(mine, True, 27 * channels, (), "widen_own_half")
    grad_w = widen(other, False, 27 * channels, (grad_w,), "widen_other_half")
    conv_out, grad_in, _ = done
    return conv_out[None], grad_in[None], grad_w.reshape(27, channels, channels)


def solution(mesh):
    in_specs = (P("dp", "space", None), P("dp", None, "space"), P(), P("dp", "space", None))
    out_specs = (P("dp", "space", None), P("dp", "space", None), P())
    return jax.shard_map(local, mesh=mesh, in_specs=in_specs, out_specs=out_specs, check_vma=False)
```

```python
import functools
import math

import jax
import jax.numpy as jnp
from jax import lax
from jax.experimental import pallas as pl
from jax.experimental.pallas import tpu as pltpu
from jax.sharding import PartitionSpec as P

PSIDE = 64
ROW = PSIDE // 4
LAYER = PSIDE * ROW
T = 128
CHUNK_W = 256
CHUNK_C = 256
VMEM_LIMIT = 28 * 1024 * 1024
FULL_VMEM_LIMIT = 58 * 1024 * 1024
VMEM = pl.BlockSpec(memory_space=pltpu.VMEM)
HBM = pl.BlockSpec(memory_space=pltpu.HBM)


def offset_of(k):
    return k // 9 - 1, (k // 3) % 3 - 1, k % 3 - 1


def row_in_scene_window(neighbours, shift):
    return jnp.where(neighbours >= 0, (neighbours - shift) & (T - 1), -1)


def one_hot(hit):
    return jnp.where(hit, jnp.ones((), jnp.bfloat16), jnp.zeros((), jnp.bfloat16))


def own_side():
    return lax.bitwise_and(lax.axis_index("dp"), 1).astype(jnp.int32)


def fill_edges(xe):
    edge = jnp.zeros((ROW, xe.shape[1]), jnp.bfloat16)
    xe[0:ROW, :] = edge
    xe[xe.shape[0] - ROW :, :] = edge


def one_hot_columns(rel, k, tile):
    spot = lax.broadcasted_iota(jnp.int32, (T, T), 0).astype(jnp.bfloat16)
    row = jnp.broadcast_to(rel[k, tile : tile + 1, :], (ROW, T)).astype(jnp.bfloat16)
    return one_hot(jnp.concatenate([row] * (T // ROW), axis=0) == spot)


def gather_columns(tiles, ks, xe, origin, rel, first_tile, to_f, to_g):
    channels = xe.shape[1] // 2
    none = jnp.zeros((T, T), jnp.bfloat16)
    kept = []

    def put(k, cols, part):
        to_f[k * T : (k + 1) * T, cols] = part[:channels]
        to_g[k * T : (k + 1) * T, cols] = part[channels:]

    def put_dot(source, right, places):
        picked = jnp.dot(source, right, preferred_element_type=jnp.float32).astype(jnp.bfloat16)
        for q, (k, cols) in enumerate(places):
            put(k, cols, picked[:, q * T : (q + 1) * T])

    for h, tile in enumerate(tiles):
        cols = slice(h * T, (h + 1) * T)
        for dz, dy in sorted({offset_of(k)[:2] for k in ks}):
            some = [k for k in ks if offset_of(k)[:2] == (dz, dy)]
            start = origin + tile * T + ROW * dy + LAYER * dz
            window = xe[start : start + T, :].T
            if 13 in some:
                put(13, cols, window)
                some.remove(13)
            if len(some) > 1:
                pair = (some.pop(0), some.pop())
                right = [one_hot_columns(rel, k, first_tile + tile) for k in pair]
                put_dot(window, jnp.concatenate(right, axis=1), [(k, cols) for k in pair])
            for k in some:
                kept.append((k, cols, window, one_hot_columns(rel, k, first_tile + tile)))
            if len(kept) == 2:
                (k0, cols0, window0, hot0), (k1, cols1, window1, hot1) = kept
                right = jnp.concatenate(
                    [
                        jnp.concatenate([hot0, none], axis=1),
                        jnp.concatenate([none, hot1], axis=1),
                    ],
                    axis=0,
                )
                both = jnp.concatenate([window0, window1], axis=1)
                put_dot(both, right, [(k0, cols0), (k1, cols1)])
                kept = []
            yield
    for k, cols, window, hot in kept:
        put_dot(window, hot, [(k, cols)])


def weight_terms(chunks, ks_of, origin, f_ref, g_ref, xe, rel, buffers, acc, fresh=False):
    def product(chunk):
        here = slice(chunk * CHUNK_W, (chunk + 1) * CHUNK_W)
        picked_f, picked_g = buffers[chunk % 2]
        ks = ks_of(chunk)
        left_f, left_g = f_ref[here, :].T, g_ref[here, :].T
        if 13 in ks:
            picked_g[13 * T :, :] = left_g
        for left, picked, side, end in ((left_g, picked_f, 0, 13), (left_f, picked_g, 13, 14)):
            for group in (range(0, 4), range(4, 8), range(8, end)):
                group = [k for k in group if k in ks]
                if group:
                    span = slice(group[0] * T, (group[-1] + 1) * T)
                    to = slice((side + group[0]) * T, (side + group[-1] + 1) * T)
                    term = lax.dot_general(
                        left,
                        picked[span, :],
                        (((1,), (1,)), ((), ())),
                        preferred_element_type=jnp.float32,
                    )
                    acc[:, to] = term if fresh and chunk == chunks[0] else acc[:, to] + term
                    yield

    pending = iter(())
    per = CHUNK_W // T
    for chunk in chunks:
        tiles = range(chunk * per, (chunk + 1) * per)
        ks = [k for k in ks_of(chunk) if k < 13]
        for _ in gather_columns(tiles, ks, xe, origin, rel, 0, *buffers[chunk % 2]):
            next(pending, None)
        for _ in pending:
            pass
        pending = product(chunk)
    for _ in pending:
        pass


def weight_inner_kernel(voxels, f_ref, g_ref, nb_ref, acc, xe, rel, gf, gg, gf2, gg2):
    channels = f_ref.shape[1]
    xe[ROW : ROW + voxels, 0:channels] = f_ref[...]
    xe[ROW : ROW + voxels, channels:] = g_ref[...]
    fill_edges(xe)
    for k in range(13):
        rel[k, :, :] = row_in_scene_window(nb_ref[k], ROW * offset_of(k)[1])
    acc[...] = jnp.zeros_like(acc)

    def ks_of(chunk):
        return range(9 if chunk < LAYER // CHUNK_W else 0, 14)

    chunks = range(voxels // CHUNK_W)
    weight_terms(chunks, ks_of, ROW, f_ref, g_ref, xe, rel, ((gf, gg), (gf2, gg2)), acc)


def weight_halo_kernel(scale, f_ref, g_ref, low_ref, nb_ref, in_ref, mine_ref, other_ref, xe, rel, gf, gg, gf2, gg2, acc, out_ref):
    channels = f_ref.shape[1]
    xe[ROW : ROW + LAYER, 0:channels] = low_ref[0]
    xe[ROW : ROW + LAYER, channels:] = low_ref[1]
    fill_edges(xe)
    for k in range(9):
        rel[k, :, :] = row_in_scene_window(nb_ref[k, 0 : LAYER // T, :], ROW * offset_of(k)[1])
    chunks = range(LAYER // CHUNK_W)
    buffers = ((gf, gg), (gf2, gg2))
    weight_terms(chunks, lambda _: range(9), ROW + LAYER, f_ref, g_ref, xe, rel, buffers, acc, True)

    def total(block, touched):
        span = slice(block * T, (block + 1) * T)
        return (in_ref[:, span] + acc[:, span] if touched else in_ref[:, span]) * scale

    for k in range(13):
        out_ref[k * T : (k + 1) * T, :] = total(k, k < 9).T.astype(out_ref.dtype)
    for k in range(14):
        out_ref[(26 - k) * T : (27 - k) * T, :] = total(13 + k, k < 9).astype(out_ref.dtype)
    if out_ref.shape[0] > 27 * T:
        out_ref[27 * T :, :] = jnp.zeros((out_ref.shape[0] - 27 * T, out_ref.shape[1]), out_ref.dtype)
    half = out_ref.shape[0] // 2
    parity = own_side()
    mine_ref[...] = out_ref[pl.ds(pl.multiple_of(parity * half, 16), half), :]
    other_ref[...] = out_ref[pl.ds(pl.multiple_of((1 - parity) * half, 16), half), :]


def weight_scratch(rows, channels):
    return [
        pltpu.VMEM((rows + 2 * ROW, 2 * channels), jnp.bfloat16),
        pltpu.VMEM((13, rows // T, T), jnp.int32),
    ] + [
        pltpu.VMEM((13 * T, CHUNK_W), jnp.bfloat16),
        pltpu.VMEM((14 * T, CHUNK_W), jnp.bfloat16),
    ] * 2


def grad_w_inner(feats, grads, neigh):
    voxels, channels = feats.shape
    return pl.pallas_call(
        functools.partial(weight_inner_kernel, voxels),
        out_shape=jax.ShapeDtypeStruct((channels, 27 * T), jnp.float32),
        in_specs=[VMEM] * 3,
        out_specs=VMEM,
        scratch_shapes=weight_scratch(voxels, channels),
        compiler_params=pltpu.CompilerParams(vmem_limit_bytes=VMEM_LIMIT),
        cost_estimate=pl.CostEstimate(flops=8 * 10**9, bytes_accessed=4 * 10**6, transcendentals=0),
        name="weight_gradient_inner",
    )(feats, grads, neigh)


def grad_w_halo(feats, grads, low, neigh, partial, scale, rows):
    channels = feats.shape[1]
    out = jax.ShapeDtypeStruct((rows // 2, channels), jnp.bfloat16)
    return pl.pallas_call(
        functools.partial(weight_halo_kernel, scale),
        out_shape=(out, out),
        in_specs=[VMEM] * 5,
        out_specs=(VMEM, VMEM),
        scratch_shapes=weight_scratch(LAYER, channels)
        + [
            pltpu.VMEM((channels, 27 * T), jnp.float32),
            pltpu.VMEM((rows, channels), jnp.bfloat16),
        ],
        compiler_params=pltpu.CompilerParams(vmem_limit_bytes=VMEM_LIMIT),
        cost_estimate=pl.CostEstimate(flops=10**6, bytes_accessed=10**4, transcendentals=0),
        name="weight_gradient_halo",
    )(feats, grads, low, neigh, partial)


def stack_kernel(f_ref, g_ref, out_ref):
    out_ref[0] = f_ref[...]
    out_ref[1] = g_ref[...]


def stack_by_copies_kernel(layer, f_ref, g_ref, out_ref, held, sems):
    rows = pl.ds(layer * LAYER, LAYER)
    copies = []
    for i, ref in enumerate((f_ref, g_ref)):
        copies.append(
            (
                pltpu.make_async_copy(ref.at[rows, :], held.at[i], sems.at[i]),
                pltpu.make_async_copy(held.at[i], out_ref.at[i], sems.at[2 + i]),
            )
        )
    for fetch, _ in copies:
        fetch.start()
    for fetch, store in copies:
        fetch.wait()
        store.start()
    for _, store in copies:
        store.wait()


def stack_layer(feats, grads, layer, name):
    channels = feats.shape[1]
    block = pl.BlockSpec((LAYER, channels), lambda i: (layer, 0))
    return pl.pallas_call(
        stack_kernel,
        grid=(1,),
        out_shape=jax.ShapeDtypeStruct((2, LAYER, channels), jnp.bfloat16),
        in_specs=[block, block],
        out_specs=VMEM,
        compiler_params=pltpu.CompilerParams(vmem_limit_bytes=VMEM_LIMIT),
        name=name,
    )(feats, grads)


def stack_layer_by_copies(feats, grads, layer, name):
    channels = feats.shape[1]
    shape = (2, LAYER, channels)
    return pl.pallas_call(
        functools.partial(stack_by_copies_kernel, layer),
        out_shape=jax.ShapeDtypeStruct(shape, jnp.bfloat16),
        in_specs=[HBM, HBM],
        out_specs=HBM,
        scratch_shapes=[pltpu.VMEM(shape, jnp.bfloat16), pltpu.SemaphoreType.DMA((4,))],
        compiler_params=pltpu.CompilerParams(vmem_limit_bytes=FULL_VMEM_LIMIT),
        name=name,
    )(feats, grads)


def rows_needed(run):
    first, end = run
    return (
        first - LAYER - (ROW if first % LAYER else 0),
        end + LAYER + (ROW if end % LAYER else 0),
    )


def conv_kernel(voxels, run, halos, make_wt, f_ref, g_ref, nb_ref, w_hbm, *rest):
    halos = list(rest[:halos])
    if make_wt:
        conv_hbm, gin_hbm, wt_hbm, wt, w_ref, *scratch = rest[-15:]
    else:
        conv_hbm, gin_hbm, wt, *scratch = rest[-13:]
    conv_ref, gin_ref, xe, nb, rel, gf, gg, gf2, gg2, sems = scratch
    channels = f_ref.shape[1]
    size = run[1] - run[0]

    origin = run[0] - LAYER - ROW
    low, high = rows_needed(run)
    main = (max(low, 0), min(high, voxels))
    rows = pl.ds(main[0], main[1] - main[0])
    to = pl.ds(main[0] - origin, main[1] - main[0])
    copies = [
        (nb_ref, nb),
        (f_ref.at[rows, :], xe.at[to, pl.ds(0, channels)]),
        (g_ref.at[rows, :], xe.at[to, pl.ds(channels, channels)]),
    ]
    parts = []
    if low < 0:
        parts.append((pl.ds(LAYER + low, -low), pl.ds(low - origin, -low)))
    if high > voxels:
        parts.append((pl.ds(0, high - voxels), pl.ds(voxels - origin, high - voxels)))
    for halo, (rows, to) in zip(halos, parts):
        for side in range(2):
            lanes = pl.ds(side * channels, channels)
            copies.append((halo.at[side, rows, :], xe.at[to, lanes]))
    early = len(copies)
    copies.append((w_hbm, w_ref if make_wt else wt))
    copies = [
        pltpu.make_async_copy(source, target, sems.at[i])
        for i, (source, target) in enumerate(copies)
    ]
    for copy in copies:
        copy.start()
    edge = jnp.zeros((ROW, 2 * channels), jnp.bfloat16)
    if low - origin:
        xe[0:ROW, :] = edge
    if high - origin < xe.shape[0]:
        xe[xe.shape[0] - ROW :, :] = edge
    copies[0].wait()
    for k in range(27):
        rel[k, :, :] = row_in_scene_window(nb[k], ROW * offset_of(k)[1])
    for copy in copies[1:early]:
        copy.wait()

    buffers = ((gf, gg), (gf2, gg2))

    def product(chunk):
        rows = slice(chunk * CHUNK_C, (chunk + 1) * CHUNK_C)
        kernels = (slice(0, channels), slice(channels, 2 * channels))
        outs = ((conv_ref, conv_hbm), (gin_ref, gin_hbm))
        for (out, out_hbm), picked, side in zip(outs, buffers[chunk % 2], kernels):
            total = None
            for part in range(3):
                span = slice(part * 9 * T, (part + 1) * 9 * T)
                term = jnp.dot(wt[side, span], picked[span, :], preferred_element_type=jnp.float32)
                total = term if total is None else total + term
                if part == 2:
                    out[rows, :] = total.T.astype(jnp.bfloat16)
                    copy = pltpu.make_async_copy(
                        out.at[rows, :],
                        out_hbm.at[pl.ds(run[0] + chunk * CHUNK_C, CHUNK_C), :],
                        sems.at[len(copies) + len(written)],
                    )
                    copy.start()
                    written.append(copy)
                yield

    def turn_weights():
        copies[-1].wait()
        for k in range(27):
            span = slice(k * T, (k + 1) * T)
            wt[0:channels, span] = w_ref[span, :].T
            wt[channels:, span] = w_ref[(26 - k) * T : (27 - k) * T, :]
            if k % 2:
                yield
        copy = pltpu.make_async_copy(wt, wt_hbm, sems.at[len(copies)])
        copy.start()
        written.append(copy)

    written = []
    turning = turn_weights()
    pending = iter(())
    per = CHUNK_C // T
    for chunk in range(size // CHUNK_C):
        tiles = range(chunk * per, (chunk + 1) * per)
        center, first_tile = run[0] - origin, run[0] // T
        moves = gather_columns(
            tiles, range(27), xe, center, rel, first_tile, *buffers[chunk % 2]
        )
        for turn, _ in enumerate(moves):
            if turn % 3 == 2:
                next(pending, None)
            if chunk == 0 and make_wt and turn >= 4:
                next(turning, None)
        for _ in pending:
            pass
        if chunk == 0:
            if make_wt:
                for _ in turning:
                    pass
            else:
                copies[-1].wait()
        pending = product(chunk)
    for _ in pending:
        pass
    for copy in written:
        copy.wait()


def conv_run(feats, grads, low, high, neigh, weight, run, earlier, name):
    voxels, channels = feats.shape
    out = jax.ShapeDtypeStruct((voxels, channels), jnp.bfloat16)
    first, end = rows_needed(run)
    halos = ((low,) if first < 0 else ()) + ((high,) if end > voxels else ())
    turned = jax.ShapeDtypeStruct((2 * channels, 27 * channels), jnp.bfloat16)
    make_wt = not earlier
    operands = (feats, grads, neigh, weight if make_wt else earlier[2]) + halos + earlier[:2]
    size = run[1] - run[0]
    results = pl.pallas_call(
        functools.partial(conv_kernel, voxels, run, len(halos), make_wt),
        out_shape=(out, out) + ((turned,) if make_wt else ()),
        in_specs=[HBM] * len(operands),
        out_specs=(HBM, HBM) + ((HBM,) if make_wt else ()),
        input_output_aliases={4 + len(halos) + i: i for i in range(len(earlier[:2]))},
        scratch_shapes=[
            pltpu.VMEM(turned.shape, jnp.bfloat16),
        ]
        + ([pltpu.VMEM(weight.shape, jnp.bfloat16)] if make_wt else [])
        + [
            pltpu.VMEM((size, channels), jnp.bfloat16),
            pltpu.VMEM((size, channels), jnp.bfloat16),
            pltpu.VMEM((size + 2 * (LAYER + ROW), 2 * channels), jnp.bfloat16),
            pltpu.VMEM(neigh.shape, jnp.int32),
            pltpu.VMEM(neigh.shape, jnp.int32),
        ]
        + [pltpu.VMEM((27 * T, CHUNK_C), jnp.bfloat16)] * 4
        + [pltpu.SemaphoreType.DMA((8 + 2 * size // CHUNK_C,))],
        compiler_params=pltpu.CompilerParams(vmem_limit_bytes=FULL_VMEM_LIMIT),
        cost_estimate=pl.CostEstimate(
            flops=10**6 if make_wt else 10**10, bytes_accessed=10**4, transcendentals=0
        ),
        name=name,
    )(*operands)
    return tuple(results) + earlier[2:]


def sum_kernel(*refs):
    *parts, out_ref = refs
    terms = [ref[i] for ref in parts for i in range(ref.shape[0])]
    total = terms[0].astype(jnp.float32)
    for term in terms[1:]:
        total += term.astype(jnp.float32)
    total = total.astype(out_ref.dtype)
    for i in range(out_ref.shape[0]):
        out_ref[i] = total


def sum_parts(parts, copies, name):
    shape = parts[0].shape[1:]
    return pl.pallas_call(
        sum_kernel,
        out_shape=jax.ShapeDtypeStruct((copies,) + shape, parts[0].dtype),
        in_specs=[VMEM] * len(parts),
        out_specs=VMEM,
        compiler_params=pltpu.CompilerParams(vmem_limit_bytes=VMEM_LIMIT),
        cost_estimate=pl.CostEstimate(flops=10**6, bytes_accessed=10**4, transcendentals=0),
        name=name,
    )(*parts)


def widen_kernel(own, count, in_ref, *rest):
    out_hbm, wide, sems = rest[-3:]
    half = in_ref.shape[0]
    piece = half // 2
    side = own_side() if own else 1 - own_side()

    def copy(where, i):
        first = where * half + i * piece
        size = min(piece, count - first)
        return pltpu.make_async_copy(
            wide.at[pl.ds(i * piece, size), :], out_hbm.at[pl.ds(first, size), :], sems.at[i]
        )

    for i in range(2):
        rows = slice(i * piece, (i + 1) * piece)
        wide[rows, :] = in_ref[rows, :].astype(jnp.float32)
        for where in range(2):
            pl.when(side == where)(copy(where, i).start)
    for i in range(2):
        for where in range(2):
            pl.when(side == where)(copy(where, i).wait)


def widen(rows, own, count, earlier, name):
    return pl.pallas_call(
        functools.partial(widen_kernel, own, count),
        in_specs=[VMEM] + [HBM] * len(earlier),
        out_specs=HBM,
        out_shape=jax.ShapeDtypeStruct((count, rows.shape[1]), jnp.float32),
        input_output_aliases={1 + i: i for i in range(len(earlier))},
        scratch_shapes=[pltpu.VMEM(rows.shape, jnp.float32), pltpu.SemaphoreType.DMA((2,))],
        compiler_params=pltpu.CompilerParams(vmem_limit_bytes=VMEM_LIMIT),
        name=name,
    )(rows, *earlier)


def local(features, neighbours, weight, grad_out):
    feats, grads = features[0], grad_out[0]
    voxels, channels = feats.shape
    neigh = neighbours.reshape(27, voxels // T, T)
    space, dp = lax.axis_size("space"), lax.axis_size("dp")
    up = [(i, i + 1) for i in range(space - 1)]
    down = [(i + 1, i) for i in range(space - 1)]
    low = lax.ppermute(
        stack_layer_by_copies(feats, grads, voxels // LAYER - 1, "stack_last_layer"), "space", up
    )
    high = lax.ppermute(
        stack_layer(feats, grads, 0, "stack_first_layer"), "space", down
    )

    scale = 1.0 / math.sqrt(dp * space * voxels)
    group = dp // 2 * space
    share = -(-27 * channels // (32 * group)) * 16
    swap = [(i, i ^ 1) for i in range(dp)]
    alike = [
        [d * space + z for d in range(side, dp, 2) for z in range(space)] for side in range(2)
    ]
    inner = grad_w_inner(feats, grads, neigh)
    mine, other = grad_w_halo(feats, grads, low, neigh, inner, scale, 2 * group * share)
    mine, other, high = lax.optimization_barrier((mine, other, high))
    other = lax.ppermute(other, "dp", swap)
    mine = sum_parts((mine[None], other[None]), 1, "sum_of_pair")
    mine, flat_weight = lax.optimization_barrier(
        (mine, weight.reshape(27 * channels, channels))
    )
    half = voxels // CHUNK_C // 2 * CHUNK_C
    ends = [0, half, voxels]

    def conv(done, part):
        run = (ends[part], ends[part + 1])
        name = "conv_run_%d" % part
        return conv_run(feats, grads, low, high, neigh, flat_weight, run, done, name)

    def exchange(pieces):
        return lax.all_to_all(
            pieces, ("dp", "space"), 0, 0, axis_index_groups=alike, tiled=True
        )

    pieces = exchange(mine.reshape(group, share, channels))
    done = conv((), 0)
    pieces, done = lax.optimization_barrier((pieces, done))
    pieces = exchange(sum_parts((pieces,), group, "sum_and_spread"))
    done = conv(done, 1)
    pieces, done = lax.optimization_barrier((pieces, done))
    mine = pieces.reshape(group * share, channels)
    other = lax.ppermute(mine, "dp", swap)
    grad_w = widen(mine, True, 27 * channels, (), "widen_own_half")
    grad_w = widen(other, False, 27 * channels, (grad_w,), "widen_other_half")
    conv_out, grad_in, _ = done
    return conv_out[None], grad_in[None], grad_w.reshape(27, channels, channels)


def solution(mesh):
    in_specs = (P("dp", "space", None), P("dp", None, "space"), P(), P("dp", "space", None))
    out_specs = (P("dp", "space", None), P("dp", "space", None), P())
    return jax.shard_map(local, mesh=mesh, in_specs=in_specs, out_specs=out_specs, check_vma=False)
```
